32 devices in a mesh: dp: 8 (over z, y), chan: 4 (over x, core).
Axes of the slice: x: 2, y: 2, z: 4, core: 2. Of those that a mesh axis runs over, the one named last changes fastest.
Arguments:
- latents: bfloat16 [16, 576, 1536], P('dp', None, 'chan'), may hold values from -6 to 6
- valid_mask: int32 [16, 576], P('dp'), may hold values from 0 to 1, as said below
- bucket_ids: int32 [16], P('dp'), may hold values from 0 to 2
- text_count: int32 [16], P('dp'), may hold values from 19 to 77, as said below
- text_tokens: bfloat16 [16, 77, 1536], P('dp', None, 'chan'), may hold values from -6 to 6
- noise_embed: float32 [16, 64], P('dp'), may hold values from -5 to 5
- conv_kernel: float32 [9, 1536], P(None, 'chan'), may hold values from -2 to 2
- conv_bias: float32 [1536], P('chan'), may hold values from -2 to 2
- mixer_expand_weight: bfloat16 [1536, 6144], P(None, 'chan'), may hold values from -0.15625 to 0.15625
- ffn_in_bias: float32 [6144], P('chan'), may hold values from -2 to 2
- grn_gamma: float32 [6144], P('chan'), may hold values from -4 to 4
- grn_beta: float32 [6144], P('chan'), may hold values from -2 to 2
- mixer_contract_weight: bfloat16 [6144, 1536], P('chan'), may hold values from -0.078125 to 0.078125
- ffn_out_bias: float32 [1536], P('chan'), may hold values from -2 to 2
- scale_weight: float32 [64, 1536], P(None, 'chan'), may hold values from -0.1875 to 0.1875
- scale_bias: float32 [1536], P('chan'), may hold values from -1 to 1
- shift_weight: float32 [64, 1536], P(None, 'chan'), may hold values from -0.375 to 0.375
- shift_bias: float32 [1536], P('chan'), may hold values from -2 to 2
- text_weight: bfloat16 [1536, 1536], P(None, 'chan'), may hold values from -0.15625 to 0.15625
- text_bias: float32 [1536], P('chan'), may hold values from -2 to 2
- query_weight: bfloat16 [1536, 1536], P(None, 'chan'), may hold values from -0.15625 to 0.15625
- query_bias: float32 [1536], P('chan'), may hold values from -2 to 2
- key_weight: bfloat16 [1536, 1536], P(None, 'chan'), may hold values from -0.15625 to 0.15625
- value_weight: bfloat16 [1536, 1536], P(None, 'chan'), may hold values from -0.15625 to 0.15625
- value_bias: float32 [1536], P('chan'), may hold values from -2 to 2
- attn_out: bfloat16 [1536, 1536], P('chan'), may hold values from -0.625 to 0.625
- attn_out_bias: float32 [1536], P('chan'), may hold values from -2 to 2
- upstream: bfloat16 [16, 576, 1536], P('dp', None, 'chan'), may hold values from -6 to 6
Outputs:
- result: bfloat16 [16, 576, 1536], P('dp', None, 'chan')
- grad_latents: bfloat16 [16, 576, 1536], P('dp', None, 'chan')
- grad_conv_kernel: float32 [9, 1536], P(None, 'chan')
- grad_conv_bias: float32 [1536], P('chan')
- grad_ffn_in: float32 [1536, 6144], P('dp', 'chan')
- grad_ffn_in_bias: float32 [6144], P('chan')
- grad_grn_gamma: float32 [6144], P('chan')
- grad_grn_beta: float32 [6144], P('chan')
- mixer_contract_gradient: float32 [6144, 1536], P('chan', 'dp')
- grad_ffn_out_bias: float32 [1536], P('chan')
- grad_scale_weight: float32 [64, 1536], P(None, 'chan')
- grad_scale_bias: float32 [1536], P('chan')
- grad_shift_weight: float32 [64, 1536], P(None, 'chan')
- grad_shift_bias: float32 [1536], P('chan')
- grad_text_weight: float32 [1536, 1536], P('dp', 'chan')
- grad_text_bias: float32 [1536], P('chan')
- grad_query_weight: float32 [1536, 1536], P('dp', 'chan')
- grad_query_bias: float32 [1536], P('chan')
- grad_key_weight: float32 [1536, 1536], P('dp', 'chan')
- grad_value_weight: float32 [1536, 1536], P('dp', 'chan')
- grad_value_bias: float32 [1536], P('chan')
- grad_attn_out: float32 [1536, 1536], P('chan', 'dp')
- grad_attn_out_bias: float32 [1536], P('chan')
The draws below stay inside these ranges and needn't reach their ends.
Inputs may be any that keep to these rules, and one draw needn't show every extreme that they name: `valid_mask`: A latent's valid slots are its first ones in slot order, at least 558 of them; some latent has all valid and some has exactly that least number. `text_count`: some latent has all 77 text tokens valid and some has 19.
All inputs are finite; a program needn't handle non-finite values.
Results may differ from the reference program's by a relative error of at most 0.02.
Values may be sent and summed in bfloat16 or wider, within the bound.
No kernel may reach another device: no remote copies, remote signals or barrier semaphores. Data moves between devices by JAX's collectives and lax.ppermute only.
A program may use at most 256 MiB of HBM per device.

```python
import jax
import jax.numpy as jnp
from jax import lax

C = 1536
HEADS = 24
FF = 6144
R = 64
SLOTS = 576
TT = 77
LATENTS = 16


def draw_valid_mask(key, part):
    key = jax.random.fold_in(key, 7)
    missing = jax.random.randint(key, (LATENTS,), 0, SLOTS // 32 + 1)
    missing = missing.at[0].set(0).at[1].set(SLOTS // 32)
    counts = SLOTS - missing
    return (jnp.arange(SLOTS, dtype=jnp.int32)[None, :] < counts[:, None]).astype(jnp.int32)


def draw_text_count(key, part):
    key = jax.random.fold_in(key, 9)
    counts = jax.random.randint(key, (LATENTS,), TT // 4, TT + 1)
    return counts.at[0].set(TT).at[1].set(TT // 4).astype(jnp.int32)


def place_ends(entries, rng, low, high):
    shape = entries.shape
    spot = [jax.random.randint(jax.random.fold_in(rng, axis), (), 0, shape[axis]) for axis in range(len(shape))]
    entries = entries.at[tuple(spot)].set(low)
    longest = shape.index(max(shape))
    spot[longest] = (spot[longest] + 1) % shape[longest]
    return entries.at[tuple(spot)].set(high)


def with_spikes(values, own_key, source, target, blocks, factor):
    owner, partner = [(jnp.arange(values.shape[dim]) // (values.shape[dim] // blocks)).reshape([-1 if axis == dim else 1 for axis in range(values.ndim)]) for dim in (source, target)]
    chosen = jax.random.permutation(own_key, blocks)[partner]
    strong = (owner == chosen) | (owner == (partner + blocks // 2) % blocks)
    return jnp.where(strong, factor * values, values)


def steps_of(stream_key, shape, pieces, low, top_value):
    loudness, own = 1.0, jax.random.fold_in(stream_key, 6)
    for position, blocks in pieces:
        steps = jnp.exp(jax.random.uniform(jax.random.fold_in(own, position), (blocks,), jnp.float32, low / len(pieces), top_value / len(pieces)))
        loudness = loudness * jnp.repeat(steps, shape[position] // blocks).reshape([-1 if axis == position else 1 for axis in range(len(shape))])
    return loudness


def bell_draw(rng, shape, width, limit, cuts=(), kind=jnp.bfloat16):
    factor_of = steps_of(rng, shape, cuts, -0.22, 0.18) if cuts else 1.0
    drawn = jax.random.normal(rng, shape, jnp.float32) * width * factor_of
    return jnp.minimum(jnp.maximum(drawn, -limit), limit).astype(kind)


def heavy_noise(own_key, shape, scale, limit, cuts, heavy, kind=jnp.bfloat16):
    array = scale * jax.random.normal(own_key, shape, jnp.float32)
    if cuts:
        array = array * steps_of(own_key, shape, cuts, -0.22, 0.18)
    return jnp.clip(with_spikes(array, jax.random.fold_in(own_key, 3), *heavy), -limit, limit).astype(kind)


def setup_inputs(seed: int = 0) -> dict:
    key_list = jax.random.split(jax.random.key(seed), 29)
    return {
        "latents": bell_draw(key_list[0], (LATENTS, SLOTS, C), 1.0, 6.0, ((0, 8), (2, 4))),
        "valid_mask": draw_valid_mask(jax.random.fold_in(key_list[28], 71), 0),
        "bucket_ids": place_ends(jax.random.randint(key_list[2], (LATENTS,), 0, 3), jax.random.fold_in(key_list[2], 1), 0, 2).astype(jnp.int32),
        "text_count": draw_text_count(jax.random.fold_in(key_list[28], 71), 0),
        "text_tokens": bell_draw(key_list[4], (LATENTS, TT, C), 1.0, 6.0, ((0, 8), (2, 4))),
        "noise_embed": bell_draw(key_list[5], (LATENTS, R), 1.0, 5.0, ((0, 8),), jnp.float32),
        "conv_kernel": bell_draw(key_list[6], (9, C), 0.33, 2.0, ((1, 4),), jnp.float32),
        "conv_bias": bell_draw(key_list[7], (C,), 0.3, 2.0, ((0, 4),), jnp.float32),
        "mixer_expand_weight": bell_draw(key_list[8], (C, FF), C ** -0.5, 0.15625, ((1, 4),)),
        "ffn_in_bias": bell_draw(key_list[9], (FF,), 0.3, 2.0, ((0, 4),), jnp.float32),
        "grn_gamma": bell_draw(key_list[10], (FF,), 1.0, 4.0, ((0, 4),), jnp.float32),
        "grn_beta": bell_draw(key_list[11], (FF,), 0.3, 2.0, ((0, 4),), jnp.float32),
        "mixer_contract_weight": bell_draw(key_list[12], (FF, C), FF ** -0.5, 0.078125, ((0, 4),)),
        "ffn_out_bias": bell_draw(key_list[13], (C,), 0.3, 2.0, ((0, 4),), jnp.float32),
        "scale_weight": bell_draw(key_list[14], (R, C), (R * 16) ** -0.5, 0.1875, ((1, 4),), jnp.float32),
        "scale_bias": bell_draw(key_list[15], (C,), 0.2, 1.0, ((0, 4),), jnp.float32),
        "shift_weight": bell_draw(key_list[16], (R, C), (R * 4) ** -0.5, 0.375, ((1, 4),), jnp.float32),
        "shift_bias": bell_draw(key_list[17], (C,), 0.3, 2.0, ((0, 4),), jnp.float32),
        "text_weight": bell_draw(key_list[18], (C, C), C ** -0.5, 0.15625, ((1, 4),)),
        "text_bias": bell_draw(key_list[19], (C,), 0.3, 2.0, ((0, 4),), jnp.float32),
        "query_weight": bell_draw(key_list[20], (C, C), C ** -0.5, 0.15625, ((1, 4),)),
        "query_bias": bell_draw(key_list[21], (C,), 0.3, 2.0, ((0, 4),), jnp.float32),
        "key_weight": bell_draw(key_list[22], (C, C), C ** -0.5, 0.15625, ((1, 4),)),
        "value_weight": bell_draw(key_list[23], (C, C), C ** -0.5, 0.15625, ((1, 4),)),
        "value_bias": bell_draw(key_list[24], (C,), 0.3, 2.0, ((0, 4),), jnp.float32),
        "attn_out": bell_draw(key_list[25], (C, C), (C // 16) ** -0.5, 0.625, ((0, 4),)),
        "attn_out_bias": bell_draw(key_list[26], (C,), 0.3, 2.0, ((0, 4),), jnp.float32),
        "upstream": heavy_noise(key_list[27], (LATENTS, SLOTS, C), 1.0, 6.0, ((0, 8), (2, 4)), (0, 2, 8, 2.0)),
    }


@jax.custom_vjp
def low(v):
    return lax.optimization_barrier(v.astype(jnp.bfloat16)).astype(jnp.float32)

@jax.custom_vjp
def low_back(v):
    return v

def low_keep(v):
    return (low(v), None)

def low_pass(kept, grad):
    return (grad,)

def back_keep(v):
    return (v, None)

def back_low(kept, grad):
    return (low(grad),)
low.defvjp(low_keep, low_pass)
low_back.defvjp(back_keep, back_low)

def matmul(left, right):
    return jnp.dot(left, right, precision=lax.Precision.HIGHEST)

def depthwise(masked, bucket, kernel, kernel_bias):
    widths = jnp.where(bucket == 0, 36, jnp.where(bucket == 1, 24, 18)).astype(jnp.int32)
    heights = jnp.where(bucket == 0, 16, jnp.where(bucket == 1, 24, 32)).astype(jnp.int32)
    slot_count = masked.shape[0]
    places = jnp.arange(slot_count, dtype=jnp.int32)
    row_pos = places // widths
    col_pos = places % widths
    margin = 40
    padded = jnp.pad(masked, ((margin, margin), (0, 0)))
    summed = jnp.zeros_like(masked) + kernel_bias
    for row_step in (-1, 0, 1):
        for col_step in (-1, 0, 1):
            offset = (margin + row_step * widths + col_step).astype(jnp.int32)
            shifted = lax.dynamic_slice_in_dim(padded, offset, slot_count, 0)
            inside = (row_pos + row_step >= 0) & (row_pos + row_step < heights) & (col_pos + col_step >= 0) & (col_pos + col_step < widths)
            summed = summed + jnp.where(inside[:, None], shifted, 0.0) * kernel[(row_step + 1) * 3 + col_step + 1]
    return summed

def layer_norm(values):
    mean_value = lax.optimization_barrier(jnp.mean(values, axis=-1, keepdims=True))
    centred = values - mean_value
    variance = lax.optimization_barrier(jnp.mean(centred * centred, axis=-1, keepdims=True))
    return centred * lax.rsqrt(variance + 1e-06)

def forward(params, latent, mask_row, bucket, count, caption_row, embed_row):
    conv_kernel, conv_bias, mixer_expand_weight, ffn_in_bias, grn_gamma, grn_beta, mixer_contract_weight, ffn_out_bias, scale_weight, scale_bias, shift_weight, shift_bias, text_weight, text_bias, query_weight, query_bias, key_weight, value_weight, value_bias, attn_out, attn_out_bias = params
    mask_float = mask_row.astype(jnp.float32)[:, None]
    conv_out = depthwise(latent * mask_float, bucket, conv_kernel, conv_bias)
    normed = low(layer_norm(conv_out))
    hidden_pre = low_back(matmul(normed, mixer_expand_weight) + ffn_in_bias)
    active = jax.nn.gelu(hidden_pre, approximate=False)
    spatial = jnp.sqrt(lax.optimization_barrier(jnp.sum(mask_float * active * active, axis=0)))
    response = spatial / (jnp.mean(spatial) + 1e-06)
    gated = low(grn_gamma * (active * response) + grn_beta + active)
    first = latent + low_back(matmul(gated, mixer_contract_weight)) + ffn_out_bias
    scale_row = matmul(embed_row[None, :], scale_weight)[0] + scale_bias
    shift_row = matmul(embed_row[None, :], shift_weight)[0] + shift_bias
    second = first * (1.0 + scale_row) + shift_row
    normed_two = low(layer_norm(second))
    text_pre = low(low_back(matmul(low(jax.nn.silu(caption_row)), text_weight) + text_bias))
    context = jnp.concatenate([normed_two, text_pre], axis=0)
    queries = low(low_back(matmul(normed_two, query_weight) + query_bias))
    keys = low(low_back(matmul(context, key_weight)))
    values = low(low_back(matmul(context, value_weight) + value_bias))
    head_dim = C // HEADS
    key_rows = context.shape[0]
    head_q = queries.reshape(SLOTS, HEADS, head_dim)
    head_k = keys.reshape(key_rows, HEADS, head_dim)
    head_v = values.reshape(key_rows, HEADS, head_dim)
    scores = low_back(jnp.einsum('qhd,khd->hqk', head_q, head_k, precision=lax.Precision.HIGHEST) * head_dim ** (-0.5))
    key_valid = jnp.concatenate([mask_row > 0, jnp.arange(TT, dtype=jnp.int32) < count])
    scores = jnp.where(key_valid[None, None, :], scores, -1e+30)
    probs = jax.nn.softmax(scores, axis=-1)
    attended = jnp.einsum('hqk,khd->qhd', low(probs), head_v, precision=lax.Precision.HIGHEST)
    attended = low(low_back(attended)).reshape(SLOTS, C)
    return second + low_back(matmul(attended, attn_out)) + attn_out_bias

def reference(latents, valid_mask, bucket_ids, text_count, text_tokens, noise_embed, conv_kernel, conv_bias, mixer_expand_weight, ffn_in_bias, grn_gamma, grn_beta, mixer_contract_weight, ffn_out_bias, scale_weight, scale_bias, shift_weight, shift_bias, text_weight, text_bias, query_weight, query_bias, key_weight, value_weight, value_bias, attn_out, attn_out_bias, upstream):
    params = tuple((weight.astype(jnp.float32) for weight in (conv_kernel, conv_bias, mixer_expand_weight, ffn_in_bias, grn_gamma, grn_beta, mixer_contract_weight, ffn_out_bias, scale_weight, scale_bias, shift_weight, shift_bias, text_weight, text_bias, query_weight, query_bias, key_weight, value_weight, value_bias, attn_out, attn_out_bias)))

    def one_latent(totals, scanned):
        latent, mask_row, bucket, count, caption_row, embed_row, cot_row = scanned

        def apply_layer(weights, latent_in):
            return forward(weights, latent_in, mask_row, bucket, count, caption_row, embed_row)
        layer_out, pullback = jax.vjp(apply_layer, params, latent)
        grad_params, grad_latent = pullback(cot_row)
        totals = jax.tree.map(jnp.add, totals, grad_params)
        return (totals, (layer_out, grad_latent))
    zeros = jax.tree.map(jnp.zeros_like, params)
    sums, (outputs, grads) = lax.scan(one_latent, zeros, (latents.astype(jnp.float32), valid_mask, bucket_ids, text_count, text_tokens.astype(jnp.float32), noise_embed.astype(jnp.float32), upstream.astype(jnp.float32)))
    return (outputs.astype(jnp.bfloat16), grads.astype(jnp.bfloat16), sums[0], sums[1], sums[2], sums[3], sums[4], sums[5], sums[6], sums[7], sums[8], sums[9], sums[10], sums[11], sums[12], sums[13], sums[14], sums[15], sums[16], sums[17], sums[18], sums[19], sums[20])
```

```python
import functools

import jax
import jax.numpy as jnp
import numpy as np
from jax import lax
from jax.experimental import pallas as pl
from jax.experimental.pallas import tpu as pltpu
from jax.sharding import PartitionSpec as P

BF = jnp.bfloat16
F32 = jnp.float32
HEAD = 64
LANE = 128
EXTRA = 16
MARGIN = 40
WIDTHS = (36, 24, 18)
EPS = 1e-6

VM = pl.BlockSpec(memory_space=pltpu.VMEM)
SM = pl.BlockSpec(memory_space=pltpu.SMEM)
ANY = pl.BlockSpec(memory_space=pl.ANY)


def kernel_call(body, name, outs, args, in_specs, out_specs, grid=(1,), scratch=(), flops=0, limit=56):
    moved = sum(int(np.prod(a.shape)) * a.dtype.itemsize for a in tuple(args) + tuple(outs))
    return pl.pallas_call(
        body,
        name=name,
        out_shape=outs,
        grid=grid,
        in_specs=in_specs,
        out_specs=out_specs,
        scratch_shapes=scratch,
        compiler_params=pltpu.CompilerParams(vmem_limit_bytes=limit << 20),
        cost_estimate=pl.CostEstimate(
            flops=int(flops), bytes_accessed=int(moved), transcendentals=0
        ),
    )(*args)


def sds(shape, dtype):
    return jax.ShapeDtypeStruct(shape, dtype)


def nn(a, b):
    return jnp.dot(a, b, preferred_element_type=F32)


def nt(a, b):
    return lax.dot_general(a, b, (((1,), (1,)), ((), ())), preferred_element_type=F32)


def tn(a, b):
    return lax.dot_general(a, b, (((0,), (0,)), ((), ())), preferred_element_type=F32)


def eye():
    return (
        lax.broadcasted_iota(jnp.int32, (LANE, LANE), 0)
        == lax.broadcasted_iota(jnp.int32, (LANE, LANE), 1)
    ).astype(F32)


def col_to_tile(col):
    size = col.shape[0]
    diag = eye()
    row = lax.broadcasted_iota(jnp.int32, (8, LANE), 0)
    tile = jnp.zeros((8, LANE), F32)
    for t in range(pl.cdiv(size, LANE)):
        n = min(LANE, size - t * LANE)
        line = jnp.sum(col[t * LANE : t * LANE + n] * diag[:n], axis=0, keepdims=True)
        tile = jnp.where(row == t, line, tile)
    return tile


def tile_to_col(tile, size):
    diag = eye()
    cols = []
    for t in range(pl.cdiv(size, LANE)):
        n = min(LANE, size - t * LANE)
        cols.append(jnp.sum(tile[t : t + 1] * diag[:n], axis=1, keepdims=True))
    return jnp.concatenate(cols, axis=0)


def split_stats(both):
    high = both.astype(BF)
    rest = both - high.astype(F32)
    mid = rest.astype(BF)
    low = (rest - mid.astype(F32)).astype(BF)
    return jnp.concatenate([high, mid, low], axis=1)


def join_stats(tile):
    wide = tile.astype(F32)
    return wide[:, :LANE] + wide[:, LANE : 2 * LANE] + wide[:, 2 * LANE : 3 * LANE]


def stats_tile(first, second):
    return split_stats(jnp.concatenate([col_to_tile(first), col_to_tile(second)], axis=0))


def block_copies(me, refs, dst, sems, width, rows=None):
    copies = []
    for k, ref in enumerate(refs):
        place = pl.multiple_of((me ^ k) * width, LANE)
        target = dst.at[:, pl.ds(place, width)] if rows is None else dst.at[rows, pl.ds(place, width)]
        copies.append(pltpu.make_async_copy(ref, target, sems.at[k]))
    return copies


def scatter_copies(me, part, send, keep, sems, width):
    copies = []
    for k, dst in enumerate((keep.at[0], send.at[0], keep.at[1], send.at[1])):
        place = pl.multiple_of((me ^ k) * width, LANE)
        copies.append(pltpu.make_async_copy(part.at[:, pl.ds(place, width)], dst, sems.at[k]))
    return copies


def run_copies(copies):
    for c in copies:
        c.start()
    for c in copies:
        c.wait()


def norm_rows(raw, out, stat, size, width, blocks):
    total = width * blocks
    means = []
    for b in range(blocks):
        means.append(tile_to_col(raw[size : size + 8, b * width : b * width + LANE].astype(F32), size))
    mean_sum = jnp.zeros((size, 1), F32)
    for b in range(blocks):
        part = raw[:size, b * width : (b + 1) * width].astype(F32)
        mean_sum = mean_sum + jnp.sum(part, axis=1, keepdims=True) + width * means[b]
    mean = mean_sum * (1.0 / total)
    square = jnp.zeros((size, 1), F32)
    for b in range(blocks):
        part = raw[:size, b * width : (b + 1) * width].astype(F32) + (means[b] - mean)
        square = square + jnp.sum(part * part, axis=1, keepdims=True)
    inverse = lax.rsqrt(square * (1.0 / total) + EPS)
    for b in range(blocks):
        part = raw[:size, b * width : (b + 1) * width].astype(F32) + (means[b] - mean)
        out[:size, b * width : (b + 1) * width] = (part * inverse).astype(BF)
    stat[0] = jnp.broadcast_to(mean, (size, LANE))
    stat[1] = jnp.broadcast_to(inverse, (size, LANE))


def send_rows(values, pay, size, width):
    mean = jnp.mean(values, axis=1, keepdims=True).astype(BF).astype(F32)
    pay[:size] = (values - mean).astype(BF)
    tile = col_to_tile(mean).astype(BF)
    pay[size:] = jnp.zeros((EXTRA, width), BF)
    pay[size : size + EXTRA, :LANE] = jnp.concatenate([tile, jnp.zeros((8, LANE), BF)], axis=0)


def column_masks(size, width):
    slot = lax.broadcasted_iota(jnp.int32, (size, 1), 0).astype(F32)
    col = slot - width * jnp.floor((slot + 0.5) * (1.0 / width))
    return col > 0.5, col < width - 1.5


def conv_forward_body(l, info, x_ref, taps, bias, pay, conv, pad):
    size, width = conv.shape
    slot = lax.broadcasted_iota(jnp.int32, (size, 1), 0)
    x = jnp.where(slot < info[l, 0], x_ref[...].astype(F32), 0.0)
    pad[:MARGIN] = jnp.zeros((MARGIN, width), F32)
    pad[MARGIN + size :] = jnp.zeros((MARGIN, width), F32)
    here = slice(MARGIN, MARGIN + size)
    for bucket, w in enumerate(WIDTHS):

        @pl.when(info[l, 1] == bucket)
        def _():
            not_first, not_last = column_masks(size, w)
            pad[here] = x
            left = jnp.where(not_first, pad[MARGIN - 1 : MARGIN - 1 + size], 0.0)
            right = jnp.where(not_last, pad[MARGIN + 1 : MARGIN + 1 + size], 0.0)
            total = bias[...] + left * taps[3:4] + x * taps[4:5] + right * taps[5:6]
            pad[here] = left * taps[0:1] + x * taps[1:2] + right * taps[2:3]
            total = total + pad[MARGIN - w : MARGIN - w + size]
            pad[here] = left * taps[6:7] + x * taps[7:8] + right * taps[8:9]
            conv[...] = total + pad[MARGIN + w : MARGIN + w + size]

    send_rows(conv[...], pay, size, width)


def conv_backward_body(l, info, keep, got, far, conv, stat, x_ref, first_grad, taps, out, sums, pad, total_width):
    size, width = conv.shape
    slot = lax.broadcasted_iota(jnp.int32, (size, 1), 0)
    mask = slot < info[l, 0]
    grad = keep[:size].astype(F32) + got[:size].astype(F32) + far[:size].astype(F32)
    both = join_stats(keep[size:]) + join_stats(got[size:]) + join_stats(far[size:])
    both = both * (1.0 / total_width)
    mean_grad = tile_to_col(both[:8], size)
    mean_cross = tile_to_col(both[8:], size)
    mean = stat[0][:, :1]
    inverse = stat[1][:, :1]
    normed = (conv[...] - mean) * inverse
    grad = inverse * (grad - mean_grad - normed * mean_cross)
    x = jnp.where(mask, x_ref[...].astype(F32), 0.0)
    pad[:MARGIN] = jnp.zeros((MARGIN, width), F32)
    pad[MARGIN + size :] = jnp.zeros((MARGIN, width), F32)
    here = slice(MARGIN, MARGIN + size)
    sums[...] = jnp.zeros_like(sums)
    sums[9:10] = jnp.sum(grad, axis=0, keepdims=True)
    for bucket, w in enumerate(WIDTHS):

        @pl.when(info[l, 1] == bucket)
        def _():
            not_first, not_last = column_masks(size, w)
            pad[here] = x
            left = jnp.where(not_first, pad[MARGIN - 1 : MARGIN - 1 + size], 0.0)
            right = jnp.where(not_last, pad[MARGIN + 1 : MARGIN + 1 + size], 0.0)
            pad[here] = grad
            rows = (pad[MARGIN + w : MARGIN + w + size], grad, pad[MARGIN - w : MARGIN - w + size])
            for r in range(3):
                for c, side in enumerate((left, x, right)):
                    tap = 3 * r + c
                    sums[tap : tap + 1] = jnp.sum(rows[r] * side, axis=0, keepdims=True)
            back = [sum(rows[r] * taps[3 * r + c : 3 * r + c + 1] for r in range(3)) for c in range(3)]
            pad[here] = jnp.where(not_first, back[0], 0.0)
            total = back[1] + pad[MARGIN + 1 : MARGIN + 1 + size]
            pad[here] = jnp.where(not_last, back[2], 0.0)
            total = total + pad[MARGIN - 1 : MARGIN - 1 + size]
            out[...] = (first_grad[...] + jnp.where(mask, total, 0.0)).astype(BF)


def gelu_both(h):
    t_den = 1.0 + (0.3275911 * 0.7071067811865476) * jnp.abs(h)
    t = pl.reciprocal(t_den, approx=True)
    t = t * (2.0 - t_den * t)
    bell = jnp.exp(-0.5 * h * h)
    poly = t * (
        0.127414796 + t * (-0.142248368 + t * (0.7107068705 + t * (-0.7265760135 + t * 0.5307027145)))
    )
    tail = poly * bell
    phi = jnp.where(h >= 0, 1.0 - tail, tail)
    return h * phi, phi + h * bell * 0.3989422804014327


def ffn_in_body(l, lats, info, b0, b1, b2, b3, w, bias, nrm, stat, act, slope, spat, total, raw, sems, width, chunk):
    j = pl.program_id(0)
    size = nrm.shape[0]

    @pl.when(j == 0)
    def _():
        run_copies(block_copies(info[lats, 0], (b0, b1, b2, b3), raw, sems, width))
        norm_rows(raw, nrm, stat, size, width, 4)
        total[...] = jnp.zeros_like(total)

    valid_from = size - size // 32
    cols = act.shape[1]
    square = jnp.zeros((1, cols), F32)
    for r in range(0, size, chunk):
        h = nn(nrm[r : r + chunk], w[...]) + bias[...]
        a, d = gelu_both(h)
        act[r : r + chunk] = a.astype(BF)
        slope[r : r + chunk] = d.astype(BF)
        sq = a * a
        if r + chunk > valid_from:
            slot = r + lax.broadcasted_iota(jnp.int32, (chunk, 1), 0)
            sq = jnp.where(slot < info[l, 0], sq, 0.0)
        square = square + jnp.sum(sq, axis=0, keepdims=True)
    here = jnp.sqrt(square)
    spat[...] = here
    total[...] = total[...] + jnp.sum(here)


def denominator(t0, t1, t2, t3, hidden_total):
    whole = t0[...] + t1[...] + t2[...] + t3[...]
    return whole[:1, :1] * (1.0 / hidden_total) + EPS


def ffn_out_body(lats, hidden_total, info, act, spat, t0, t1, t2, t3, gamma, beta, w, gated, send, keep, part, sems, width, chunk):
    j = pl.program_id(0)
    size = act.shape[0]

    @pl.when(j == 0)
    def _():
        gain = 1.0 + gamma[...] * (spat[...] / denominator(t0, t1, t2, t3, hidden_total))
        for r in range(0, size, chunk):
            rows = slice(r, r + chunk)
            gated[rows] = (act[rows].astype(F32) * gain + beta[...]).astype(BF)

    cols = w.shape[1]
    part[:, pl.ds(pl.multiple_of(j * cols, LANE), cols)] = nn(gated[...], w[...]).astype(BF)

    @pl.when(j == pl.num_programs(0) - 1)
    def _():
        run_copies(scatter_copies(info[lats, 0], part, send, keep, sems, width))


def add_body(stats, keep, got, out):
    size = out.shape[0] - (EXTRA if stats else 0)
    out[:size] = (keep[:size].astype(F32) + got[:size].astype(F32)).astype(BF)
    if stats:
        out[size:] = split_stats(join_stats(keep[size:]) + join_stats(got[size:]))


def middle_body(x, keep, got, far, out_bias, scale, shift, first, pay):
    size, width = first.shape
    value = x[...].astype(F32) + (
        keep[...].astype(F32) + got[...].astype(F32) + far[...].astype(F32) + out_bias[...]
    )
    first[...] = value
    send_rows(value * (1.0 + scale[...]) + shift[...], pay, size, width)


def text_body(lats, info, b0, b1, b2, b3, w, bias, full, low, sems, width, text_len):
    lat_count, rows, _ = low.shape
    copies = []
    for l in range(lat_count):
        for k, ref in enumerate((b0, b1, b2, b3)):
            place = pl.multiple_of((info[lats, 0] ^ k) * width, LANE)
            copies.append(
                pltpu.make_async_copy(ref.at[l], full.at[l, :, pl.ds(place, width)], sems.at[4 * l + k])
            )
    run_copies(copies)
    row = lax.broadcasted_iota(jnp.int32, (rows, 1), 0)
    for l in range(lat_count):
        low[l] = jnp.where(row < text_len, nn(full[l], w[...]) + bias[...], 0.0).astype(BF)


def attention_body(
    l, lats, info, p0, p1, p2, p3, x0, x1, x2, x3, g0, g1, g2, g3, wq, wk, wv, wo, q_bias, v_bias,
    ctx, stat, g_full, att, dqkv, send, keep, sums,
    raw, w_all, w_out, q_s, k_s, v_s, do_s, kt_s, vt_s, att_t, dq_t, scores, part, sems, width,
):
    me = info[lats, 0]
    size = att.shape[0]
    rows = ctx.shape[0]
    total = ctx.shape[1]
    text = rows - size
    factor = HEAD ** (-0.5)
    copy_in = block_copies(me, (p0, p1, p2, p3), raw, sems, width)
    for k, ref in enumerate((x0, x1, x2, x3)):
        place = pl.multiple_of((me ^ k) * width, LANE)
        copy_in.append(
            pltpu.make_async_copy(ref.at[l], ctx.at[size:, pl.ds(place, width)], sems.at[4 + k])
        )
    copy_w = [
        pltpu.make_async_copy(ref, w_all.at[:, k * width : (k + 1) * width], sems.at[8 + k])
        for k, ref in enumerate((wq, wk, wv))
    ]
    copy_g = [pltpu.make_async_copy(wo, w_out, sems.at[11])]
    for k, ref in enumerate((g0, g1, g2, g3)):
        place = pl.multiple_of((me ^ k) * width, LANE)
        copy_g.append(
            pltpu.make_async_copy(ref.at[l], g_full.at[:, pl.ds(place, width)], sems.at[12 + k])
        )
    for c in copy_in + copy_w + copy_g:
        c.start()
    for c in copy_in:
        c.wait()
    norm_rows(raw, ctx, stat, size, width, 4)
    for c in copy_w:
        c.wait()
    q_s[...] = ((nn(ctx[:size], w_all[:, :width]) + q_bias[...]).astype(BF).astype(F32) * factor).astype(BF)
    keys = nn(ctx[...], w_all[:, width : 2 * width]).astype(BF)
    k_s[...] = keys
    kt_s[...] = keys.T
    values = (nn(ctx[...], w_all[:, 2 * width :]) + v_bias[...]).astype(BF)
    v_s[...] = values
    vt_s[...] = values.T
    for c in copy_g:
        c.wait()
    do_s[...] = nt(g_full[...], w_out[...]).astype(BF)
    tail = (size - size // 32) // 8 * 8
    key_row = tail + lax.broadcasted_iota(jnp.int32, (rows - tail, 1), 0)
    key_ok = (key_row < info[l, 0]) | ((key_row >= size) & (key_row < size + info[l, 2]))

    def pair(p, carry):
        lo = pl.multiple_of(p * LANE, LANE)
        q2 = q_s[:, pl.ds(lo, LANE)]
        k2 = k_s[:, pl.ds(lo, LANE)]
        v2 = v_s[:, pl.ds(lo, LANE)]
        do2 = do_s[:, pl.ds(lo, LANE)]
        dks, dvs = [], []
        for half in range(2):
            lanes = slice(half * HEAD, (half + 1) * HEAD)
            line = pl.ds(pl.multiple_of(p * LANE + half * HEAD, HEAD), HEAD)
            qh, kh, vh, doh = q2[:, lanes], k2[:, lanes], v2[:, lanes], do2[:, lanes]
            scores[...] = nt(kh, qh)
            scores[tail:] = jnp.where(key_ok, scores[tail:], -1e30)
            top = jnp.max(scores[...], axis=0, keepdims=True)
            expo = jnp.exp(scores[...] - top)
            probs = expo * (1.0 / jnp.sum(expo, axis=0, keepdims=True))
            low = probs.astype(BF)
            att_t[line] = nn(vt_s[line], low)
            scores[...] = probs
            grad_p = nt(vh, doh)
            dvs.append(nn(low, doh))
            dot = jnp.sum(scores[...] * grad_p, axis=0, keepdims=True)
            grad_s = (scores[...] * (grad_p - dot)).astype(BF)
            dks.append(nn(grad_s, qh))
            dq_t[line] = nn(kt_s[line], grad_s) * factor
        dqkv[:, pl.ds(pl.multiple_of(width + lo, LANE), LANE)] = jnp.concatenate(dks, axis=1).astype(BF)
        dqkv[:, pl.ds(pl.multiple_of(2 * width + lo, LANE), LANE)] = jnp.concatenate(dvs, axis=1).astype(BF)
        return carry

    lax.fori_loop(0, width // LANE, pair, 0)
    att[...] = att_t[...].astype(BF).T
    dq = dq_t[...].astype(BF).T
    dqkv[:size, :width] = dq
    dqkv[size:, :width] = jnp.zeros((text, width), BF)
    sums[...] = jnp.zeros_like(sums)
    sums[0:1] = jnp.sum(dq.astype(F32), axis=0, keepdims=True)
    sums[1:2] = jnp.sum(dqkv[:, 2 * width :].astype(F32), axis=0, keepdims=True)
    first = jnp.zeros((size, 1), F32)
    second = jnp.zeros((size, 1), F32)
    cols = 256
    for n in range(0, total, cols):
        block = nt(dqkv[...], w_all[n : n + cols]).astype(BF)
        part[:rows, n : n + cols] = block
        wide = block[:size].astype(F32)
        first = first + jnp.sum(wide, axis=1, keepdims=True)
        second = second + jnp.sum(wide * ctx[:size, n : n + cols].astype(F32), axis=1, keepdims=True)
    tile = stats_tile(first, second)
    for b in range(4):
        part[rows:, b * width : (b + 1) * width] = tile
    run_copies(scatter_copies(me, part, send, keep, sems, width))


def project_body(lats, info, att, w, send, keep, part, sems, width):
    cols = 512
    for n in range(0, part.shape[1], cols):
        part[:, n : n + cols] = nn(att[...], w[:, n : n + cols]).astype(BF)
    run_copies(scatter_copies(info[lats, 0], part, send, keep, sems, width))


def result_body(first, scale, shift, keep, got, far, bias, out):
    second = first[...] * (1.0 + scale[...]) + shift[...]
    branch = keep[...].astype(F32) + got[...].astype(F32) + far[...].astype(F32) + bias[...]
    out[...] = (second + branch).astype(BF)


def second_grad_body(keep, got, far, g_ref, first_ref, stat, scale, shift, pay, first_grad, text, sums, total_width, text_len):
    size, width = first_grad.shape
    rows = keep.shape[0] - EXTRA
    both = join_stats(keep[rows:]) + join_stats(got[rows:]) + join_stats(far[rows:])
    both = both * (1.0 / total_width)
    mean_grad = tile_to_col(both[:8], size)
    mean_cross = tile_to_col(both[8:], size)
    grad = keep[:size].astype(F32) + got[:size].astype(F32) + far[:size].astype(F32)
    first = first_ref[...]
    gain = 1.0 + scale[...]
    inverse = stat[1][:, :1]
    normed = (first * gain + shift[...] - stat[0][:, :1]) * inverse
    upstream = g_ref[...].astype(F32)
    second_grad = upstream + inverse * (grad - mean_grad - normed * mean_cross)
    scaled = second_grad * gain
    pay[...] = scaled.astype(BF)
    first_grad[...] = scaled
    row = lax.broadcasted_iota(jnp.int32, (rows - size, 1), 0)
    tail = keep[size:rows].astype(F32) + got[size:rows].astype(F32) + far[size:rows].astype(F32)
    low = jnp.where(row < text_len, tail, 0.0).astype(BF)
    text[...] = low
    sums[...] = jnp.zeros_like(sums)
    sums[0:1] = jnp.sum(second_grad * first, axis=0, keepdims=True)
    sums[1:2] = jnp.sum(second_grad, axis=0, keepdims=True)
    sums[2:3] = jnp.sum(scaled, axis=0, keepdims=True)
    sums[3:4] = jnp.sum(low.astype(F32), axis=0, keepdims=True)
    sums[4:5] = jnp.sum(upstream, axis=0, keepdims=True)


def gated_grad_body(lats, info, b0, b1, b2, b3, w, act, gamma, spat, full, out, s1, s2, total, sems, width, chunk):
    j = pl.program_id(0)
    size = full.shape[0]

    @pl.when(j == 0)
    def _():
        run_copies(block_copies(info[lats, 0], (b0, b1, b2, b3), full, sems, width))
        total[...] = jnp.zeros_like(total)

    cols = out.shape[1]
    cross = jnp.zeros((1, cols), F32)
    plain = jnp.zeros((1, cols), F32)
    for r in range(0, size, chunk):
        grad = nt(full[r : r + chunk], w[...])
        out[r : r + chunk] = grad.astype(BF)
        cross = cross + jnp.sum(grad * act[r : r + chunk].astype(F32), axis=0, keepdims=True)
        plain = plain + jnp.sum(grad, axis=0, keepdims=True)
    s1[...] = cross
    s2[...] = plain
    total[...] = total[...] + jnp.sum(cross * gamma[...] * spat[...])


def hidden_grad_body(
    l, lats, hidden_total, info, gg, act, slope, spat, s1, gamma, t0, t1, t2, t3, c0, c1, c2, c3, w, nrm,
    hidden, send, keep, bias_sum, gamma_sum, part, acc, sems, width, chunk,
):
    j = pl.program_id(0)
    size = hidden.shape[0]

    @pl.when(j == 0)
    def _():
        den = denominator(t0, t1, t2, t3, hidden_total)
        cross = (c0[...] + c1[...] + c2[...] + c3[...])[:1, :1]
        response = spat[...] / den
        gamma_sum[...] = response * s1[...]
        grad_spat = gamma[...] * s1[...] / den - cross / (den * den) * (1.0 / hidden_total)
        gain = gamma[...] * response + 1.0
        pull = grad_spat / spat[...]
        total = jnp.zeros_like(bias_sum[...])
        for r in range(0, size, chunk):
            rows = slice(r, r + chunk)
            slot = r + lax.broadcasted_iota(jnp.int32, (chunk, 1), 0)
            active = jnp.where(slot < info[l, 0], act[rows].astype(F32), 0.0)
            grad = gg[rows].astype(F32) * gain + pull * active
            low = (grad * slope[rows].astype(F32)).astype(BF)
            hidden[rows] = low
            total = total + jnp.sum(low.astype(F32), axis=0, keepdims=True)
        bias_sum[...] = total
        acc[...] = jnp.zeros_like(acc)

    cols = w.shape[0]
    block = nt(hidden[...], w[...]).astype(BF)
    part[:size, pl.ds(pl.multiple_of(j * cols, LANE), cols)] = block
    wide = block.astype(F32)
    acc[0] = acc[0] + jnp.sum(wide, axis=1, keepdims=True)
    acc[1] = acc[1] + jnp.sum(wide * nrm[...].astype(F32), axis=1, keepdims=True)

    @pl.when(j == pl.num_programs(0) - 1)
    def _():
        tile = stats_tile(acc[0][:, :1], acc[1][:, :1])
        for b in range(4):
            part[size:, b * width : (b + 1) * width] = tile
        run_copies(scatter_copies(info[lats, 0], part, send, keep, sems, width))


def place_blocks(places, result, send, keep):
    half = keep.shape[0]
    rows = keep.shape[1]
    for s in range(half):
        keep[s] = result[pl.ds(pl.multiple_of(places[s] * rows, 16), rows), :]
        send[s] = result[pl.ds(pl.multiple_of(places[half + s] * rows, 16), rows), :]


def weight_grad_body(pairs, split, plan, places, *refs):
    lefts_rights = refs[:pairs]
    outs = refs[pairs:-1]
    result = refs[-1]
    j = pl.program_id(0)
    for step, terms in enumerate(plan):

        @pl.when(j == step)
        def _():
            total = None
            for left, right in terms:
                term = tn(lefts_rights[left][...], lefts_rights[right][...])
                total = term if total is None else total + term
            result[...] = total.astype(BF)

    if split:
        place_blocks(places, result, *outs)
    else:
        outs[0][...] = result[...]


def weight_grads(name, places, lefts, tiles, cols, dp):
    operands = list(lefts)
    specs = [VM] * len(lefts)
    plan = []
    flops = 0
    for terms in tiles:
        entry = []
        for left, right, start in terms:
            entry.append((left, right, start))
        plan.append(entry)
    rights = []
    for terms in plan:
        for _, right, _ in terms:
            if not any(right is r for r in rights):
                rights.append(right)
    body_plan = []
    for step, terms in enumerate(plan):
        entry = []
        for left, right, _ in terms:
            entry.append((left, len(lefts) + [right is r for r in rights].index(True)))
            flops += 2 * right.shape[0] * lefts[left].shape[1] * cols
        body_plan.append(entry)
    for right in rights:
        table = []
        last = 0
        for terms in plan:
            for _, r, start in terms:
                if r is right:
                    last = start // cols
            table.append(last)
        first = next(start // cols for terms in plan for _, r, start in terms if r is right)
        for i in range(len(table)):
            if not any(r is right for terms in plan[: i + 1] for _, r, _ in terms):
                table[i] = first

        def index(j, table=tuple(table)):
            place = jnp.int32(table[0])
            for i in range(1, len(table)):
                if table[i] != table[i - 1]:
                    place = jnp.where(j >= i, jnp.int32(table[i]), place)
            return (0, place)

        operands.append(right)
        specs.append(pl.BlockSpec((right.shape[0], cols), index))
    width = lefts[0].shape[1]
    wide = cols * len(tiles)
    split = places is not None
    if split:
        half = dp // 2
        shape = sds((half, width // dp, wide), BF)
        outs = (shape, shape)
        out_specs = (pl.BlockSpec((half, width // dp, cols), lambda j: (0, 0, j)),) * 2
        args = (places, *operands)
        body = functools.partial(weight_grad_body, len(operands), True, body_plan)
        in_specs = [SM] + specs
    else:
        outs = (sds((width, wide), BF),)
        out_specs = (pl.BlockSpec((width, cols), lambda j: (0, j)),)
        args = tuple(operands)
        body = functools.partial(weight_grad_body, len(operands), False, body_plan, None)
        in_specs = specs
    return kernel_call(
        body, name, outs, args, in_specs, out_specs, grid=(len(tiles),),
        scratch=[pltpu.VMEM((width, cols), BF)], flops=flops,
    )


def pack_early_body(lat_count, noise, *refs):
    second = refs[:lat_count]
    attn = refs[lat_count : 2 * lat_count]
    gam = refs[2 * lat_count : 3 * lat_count]
    bet = refs[3 * lat_count : 4 * lat_count]
    out = refs[-1]
    width = out.shape[1]
    r = noise.shape[0]
    out[...] = jnp.zeros_like(out)
    out[:r] = sum(noise[:, l : l + 1] * second[l][0:1] for l in range(lat_count))
    out[r : 2 * r] = sum(noise[:, l : l + 1] * second[l][1:2] for l in range(lat_count))
    base = 2 * r
    for i in range(5):
        out[base + i : base + i + 1] = sum(second[l][i : i + 1] for l in range(lat_count))
    for i in range(2):
        out[base + 5 + i : base + 6 + i] = sum(attn[l][i : i + 1] for l in range(lat_count))
    for k, group in enumerate((gam, bet)):
        whole = sum(g[...] for g in group)
        for b in range(whole.shape[1] // width):
            at = base + 8 + 4 * k + b
            out[at : at + 1] = whole[:, b * width : (b + 1) * width]


def pack_late_body(lat_count, *refs):
    conv = refs[:lat_count]
    bias = refs[lat_count : 2 * lat_count]
    out = refs[-1]
    width = out.shape[1]
    out[...] = sum(c[...] for c in conv)
    whole = sum(b[...] for b in bias)
    for b in range(whole.shape[1] // width):
        out[10 + b : 11 + b] = whole[:, b * width : (b + 1) * width]


def local(
    latents, valid_mask, bucket_ids, text_count, text_tokens, noise_embed, conv_kernel, conv_bias,
    mixer_expand_weight, ffn_in_bias, grn_gamma, grn_beta, mixer_contract_weight, ffn_out_bias,
    scale_weight, scale_bias, shift_weight, shift_bias, text_weight, text_bias, query_weight, query_bias,
    key_weight, value_weight, value_bias, attn_out, attn_out_bias, upstream,
):
    lats, size, width = latents.shape
    groups = lax.axis_size("chan")
    dp = lax.axis_size("dp")
    total = width * groups
    hidden = mixer_expand_weight.shape[1]
    hidden_total = hidden * groups
    text_len = text_tokens.shape[1]
    text_rows = pl.cdiv(text_len, 16) * 16
    rows = size + text_rows
    highest = lax.Precision.HIGHEST
    me = lax.axis_index("chan")

    def xswap(v):
        return lax.ppermute(v, "chan", [(i, i ^ 2) for i in range(groups)])

    def cswap(v):
        return lax.ppermute(v, "chan", [(i, i ^ 1) for i in range(groups)])

    def gather(v):
        near = cswap(v)
        far = xswap(v)
        return v, near, far, cswap(far)

    def line(v):
        return v.reshape(1, -1)

    info = jnp.stack(
        [jnp.sum(valid_mask, axis=1), bucket_ids, text_count, jnp.zeros_like(bucket_ids)], axis=1
    )
    info = jnp.concatenate([info, jnp.full((1, 4), me, jnp.int32)], axis=0).astype(jnp.int32)

    def lat_spec(l, *shape):
        return pl.BlockSpec((None,) + shape, lambda *_: (l,) + (0,) * len(shape))

    def part_spec(k, shape):
        return pl.BlockSpec((None,) + tuple(shape[1:]), lambda *_: (k, 0, 0))

    text_act = jax.nn.silu(text_tokens.astype(F32)).astype(BF)
    text_act = jnp.pad(text_act, ((0, 0), (0, text_rows - text_len), (0, 0)))
    text_blocks = gather(text_act)

    def conv_forward(l):
        return kernel_call(
            functools.partial(conv_forward_body, l), "conv_forward_%d" % l,
            (sds((size + EXTRA, width), BF), sds((size, width), F32)),
            (info, latents, conv_kernel, line(conv_bias)),
            [SM, lat_spec(l, size, width), VM, VM], (VM, VM),
            scratch=[pltpu.VMEM((size + 2 * MARGIN, width), F32)], flops=size * width * 40,
        )

    tile_cols = 256

    def ffn_in(l, blocks):
        n = hidden // tile_cols
        col = pl.BlockSpec((1, tile_cols), lambda j: (0, j))
        wide = pl.BlockSpec((size, tile_cols), lambda j: (0, j))
        return kernel_call(
            functools.partial(ffn_in_body, l, lats, width=width, chunk=size // 3), "ffn_in_%d" % l,
            (sds((size, total), BF), sds((2, size, LANE), F32), sds((size, hidden), BF),
             sds((size, hidden), BF), sds((1, hidden), F32), sds((8, LANE), F32)),
            (info, *blocks, mixer_expand_weight, line(ffn_in_bias)),
            [SM] + [ANY] * 4 + [pl.BlockSpec((total, tile_cols), lambda j: (0, j)), col],
            (VM, VM, wide, wide, col, VM), grid=(n,),
            scratch=[pltpu.VMEM((size + EXTRA, total), BF), pltpu.SemaphoreType.DMA((4,))],
            flops=2 * size * total * hidden * 2,
        )

    def ffn_out(l, act, spat, tots):
        n = total // tile_cols
        shape = sds((2, size, width), BF)
        return kernel_call(
            functools.partial(ffn_out_body, lats, hidden_total, width=width, chunk=32), "ffn_out_%d" % l,
            (sds((size, hidden), BF), shape, shape),
            (info, act, spat, *tots, line(grn_gamma), line(grn_beta), mixer_contract_weight),
            [SM] + [VM] * 8 + [pl.BlockSpec((hidden, tile_cols), lambda j: (0, j))],
            (VM, ANY, ANY), grid=(n,),
            scratch=[pltpu.VMEM((size, total), BF), pltpu.SemaphoreType.DMA((4,))],
            flops=2 * size * total * hidden * 1.3,
        )

    def add_blocks(name, keep, got, stats):
        spec = part_spec(1, keep.shape)
        return kernel_call(
            functools.partial(add_body, stats), name, (sds(keep.shape[1:], BF),), (keep, got),
            [spec, spec], (VM,), grid=(1,), flops=keep.size,
        )[0]

    def scatter(name, send, keep, stats):
        got = cswap(send)
        far = xswap(add_blocks(name, keep, got, stats))
        return keep, got, far

    scale_rows = (jnp.dot(noise_embed, scale_weight, precision=highest) + scale_bias)[:, None]
    shift_rows = (jnp.dot(noise_embed, shift_weight, precision=highest) + shift_bias)[:, None]

    def middle(l, pieces):
        keep, got, far = pieces
        spec = part_spec(0, keep.shape)
        row = lat_spec(l, 1, width)
        return kernel_call(
            middle_body, "middle_%d" % l,
            (sds((size, width), F32), sds((size + EXTRA, width), BF)),
            (latents, keep, got, far, line(ffn_out_bias), scale_rows, shift_rows),
            [lat_spec(l, size, width), spec, spec, VM, VM, row, row], (VM, VM), grid=(1,),
            flops=size * width * 20,
        )

    def text_low_rows(blocks):
        return kernel_call(
            functools.partial(text_body, lats, width=width, text_len=text_len), "text_rows",
            (sds((lats, text_rows, total), BF), sds((lats, text_rows, width), BF)),
            (info, *blocks, text_weight, line(text_bias)),
            [SM] + [ANY] * 4 + [VM, VM], (VM, VM),
            scratch=[pltpu.SemaphoreType.DMA((4 * lats,))], flops=2 * lats * text_rows * total * width,
        )

    def attention(l, blocks, texts, grads):
        shape = sds((2, rows + EXTRA, width), BF)
        return kernel_call(
            functools.partial(attention_body, l, lats, width=width), "attention_%d" % l,
            (sds((rows, total), BF), sds((2, size, LANE), F32), sds((size, total), BF),
             sds((size, width), BF), sds((rows, 3 * width), BF), shape, shape, sds((8, width), F32)),
            (info, *blocks, *texts, *grads, query_weight, key_weight, value_weight, attn_out,
             line(query_bias), line(value_bias)),
            [SM] + [ANY] * 16 + [VM, VM],
            (VM, VM, VM, VM, VM, ANY, ANY, VM),
            scratch=[
                pltpu.VMEM((size + EXTRA, total), BF),
                pltpu.VMEM((total, 3 * width), BF),
                pltpu.VMEM((width, total), BF),
                pltpu.VMEM((size, width), BF),
                pltpu.VMEM((rows, width), BF),
                pltpu.VMEM((rows, width), BF),
                pltpu.VMEM((size, width), BF),
                pltpu.VMEM((width, rows), BF),
                pltpu.VMEM((width, rows), BF),
                pltpu.VMEM((width, size), F32),
                pltpu.VMEM((width, size), F32),
                pltpu.VMEM((rows, size), F32),
                pltpu.VMEM((rows + EXTRA, total), BF),
                pltpu.SemaphoreType.DMA((16,)),
            ],
            flops=2 * rows * total * width * 8 + 2 * rows * size * width * 24,
        )

    def project(l, att):
        shape = sds((2, size, width), BF)
        return kernel_call(
            functools.partial(project_body, lats, width=width), "project_%d" % l, (shape, shape),
            (info, att, attn_out), [SM, VM, VM], (ANY, ANY),
            scratch=[pltpu.VMEM((size, total), BF), pltpu.SemaphoreType.DMA((4,))],
            flops=2 * size * total * width,
        )

    def result_rows(l, first, pieces):
        keep, got, far = pieces
        spec = part_spec(0, keep.shape)
        row = lat_spec(l, 1, width)
        return kernel_call(
            result_body, "result_%d" % l, (sds((size, width), BF),),
            (first, scale_rows, shift_rows, keep, got, far, line(attn_out_bias)),
            [VM, row, row, spec, spec, VM, VM], (VM,), grid=(1,), flops=size * width * 6,
        )[0]

    def second_grad(l, pieces, first, stat):
        keep, got, far = pieces
        spec = part_spec(0, keep.shape)
        row = lat_spec(l, 1, width)
        return kernel_call(
            functools.partial(second_grad_body, total_width=total, text_len=text_len), "second_grad_%d" % l,
            (sds((size, width), BF), sds((size, width), F32), sds((text_rows, width), BF), sds((8, width), F32)),
            (keep, got, far, upstream, first, stat, scale_rows, shift_rows),
            [spec, spec, VM, lat_spec(l, size, width), VM, VM, row, row], (VM, VM, VM, VM), grid=(1,),
            flops=size * width * 30,
        )

    def gated_grad(l, blocks, act, spat):
        n = hidden // tile_cols
        col = pl.BlockSpec((1, tile_cols), lambda j: (0, j))
        wide = pl.BlockSpec((size, tile_cols), lambda j: (0, j))
        return kernel_call(
            functools.partial(gated_grad_body, lats, width=width, chunk=size // 3), "gated_grad_%d" % l,
            (sds((size, total), BF), sds((size, hidden), BF), sds((1, hidden), F32), sds((1, hidden), F32),
             sds((8, LANE), F32)),
            (info, *blocks, mixer_contract_weight, act, line(grn_gamma), spat),
            [SM] + [ANY] * 4 + [pl.BlockSpec((tile_cols, total), lambda j: (j, 0)), wide, col, col],
            (VM, wide, col, col, VM), grid=(n,),
            scratch=[pltpu.SemaphoreType.DMA((4,))], flops=2 * size * total * hidden * 1.3,
        )

    def hidden_grad(l, gg, act, slope, spat, s1, tots, crosses, nrm):
        n = total // tile_cols
        shape = sds((2, size + EXTRA, width), BF)
        return kernel_call(
            functools.partial(hidden_grad_body, l, lats, hidden_total, width=width, chunk=32),
            "hidden_grad_%d" % l,
            (sds((size, hidden), BF), shape, shape, sds((1, hidden), F32), sds((1, hidden), F32)),
            (info, gg, act, slope, spat, s1, line(grn_gamma), *tots, *crosses, mixer_expand_weight, nrm),
            [SM] + [VM] * 14
            + [pl.BlockSpec((tile_cols, hidden), lambda j: (j, 0)), pl.BlockSpec((size, tile_cols), lambda j: (0, j))],
            (VM, ANY, ANY, VM, VM), grid=(n,),
            scratch=[
                pltpu.VMEM((size + EXTRA, total), BF),
                pltpu.VMEM((2, size, LANE), F32),
                pltpu.SemaphoreType.DMA((4,)),
            ],
            flops=2 * size * total * hidden * 1.5,
        )

    def conv_backward(l, pieces, conv, stat, first_grad):
        keep, got, far = pieces
        spec = part_spec(0, keep.shape)
        return kernel_call(
            functools.partial(conv_backward_body, l, total_width=total), "conv_backward_%d" % l,
            (sds((size, width), BF), sds((16, width), F32)),
            (info, keep, got, far, conv, stat, latents, first_grad, conv_kernel),
            [SM, spec, spec, VM, VM, VM, lat_spec(l, size, width), VM, VM], (VM, VM), grid=(1,),
            scratch=[pltpu.VMEM((size + 2 * MARGIN, width), F32)], flops=size * width * 80,
        )

    half = dp // 2
    split = dp % 2 == 0 and 4 <= dp <= 16 and (total // dp) % 16 == 0
    if split:
        order = list(range(0, half, 2)) + list(range(half - 1 - half % 2, 0, -2))
        place_of = {z: p for p, z in enumerate(order)}
        table = np.zeros((dp, dp), np.int32)
        for d in range(dp):
            z, y = d // 2, d % 2
            for s in range(half):
                chunk = order[(place_of[z] - 1 - s) % half]
                table[d, s] = 2 * chunk + y
                table[d, half + s] = 2 * chunk + 1 - y
        places = lax.dynamic_index_in_dim(jnp.asarray(table), lax.axis_index("dp"), 0, keepdims=False)
        ring = [(2 * order[p] + y, 2 * order[(p + 1) % half] + y) for p in range(half) for y in range(2)]
    else:
        places = None

    def reduce_dp(parts):
        if not split:
            return lax.psum_scatter(parts[0], "dp", scatter_dimension=0, tiled=True).astype(F32)
        send, keep = parts
        got = lax.ppermute(send, "dp", [(i, i ^ 1) for i in range(dp)])
        moving = None
        for s in range(half):
            here = keep[s].astype(F32) + got[s].astype(F32)
            if moving is not None:
                here = here + moving.astype(F32)
            if s < half - 1:
                moving = lax.ppermute(here.astype(BF), "dp", ring)
        return here

    def sum_dp(v):
        if dp & (dp - 1):
            return lax.psum(v, "dp")
        step = 1
        while step < dp:
            v = v + lax.ppermute(v, "dp", [(i, i ^ step) for i in range(dp)])
            step *= 2
        return v

    every = range(lats)
    convs = [conv_forward(l) for l in every]
    pay1 = [gather(c[0]) for c in convs]
    text_full, text_low = text_low_rows(text_blocks)
    text_low_blocks = gather(text_low)
    up_blocks = gather(upstream)
    ffn = [ffn_in(l, pay1[l]) for l in every]
    tots = [gather(f[5]) for f in ffn]
    outs = [ffn_out(l, ffn[l][2], ffn[l][4], tots[l]) for l in every]
    gated = [o[0] for o in outs]
    mids = [middle(l, scatter("add_ffn_%d" % l, outs[l][1], outs[l][2], False)) for l in every]
    pay2 = [gather(m[1]) for m in mids]
    attn = [attention(l, pay2[l], text_low_blocks, up_blocks) for l in every]
    ctx_parts = [scatter("add_ctx_%d" % l, attn[l][5], attn[l][6], True) for l in every]
    seconds = [second_grad(l, ctx_parts[l], mids[l][0], attn[l][1]) for l in every]
    pay3 = [gather(s[0]) for s in seconds]
    projected = [project(l, attn[l][3]) for l in every]
    out_parts = [scatter("add_out_%d" % l, *projected[l], False) for l in every]
    result = jnp.stack([result_rows(l, mids[l][0], out_parts[l]) for l in every])

    cols = width
    tiles = []
    for k in range(3):
        tiles.append([(l, attn[l][4], k * width) for l in every])
    tiles.append([(lats + l, attn[l][3], 0) for l in every])
    lefts = [attn[l][0] for l in every] + [attn[l][2] for l in every]
    attn_grads = reduce_dp(weight_grads("attn_weight_grads", places, lefts, tiles, cols, dp))

    gg = [gated_grad(l, pay3[l], ffn[l][2], ffn[l][4]) for l in every]
    crosses = [gather(g[4]) for g in gg]
    lefts = [gg[l][0] for l in every] + [text_full[l] for l in every]
    tiles = [[(l, gated[l], k) for l in every] for k in range(0, hidden, cols)]
    tiles.append([(lats + l, seconds[l][2], 0) for l in every])
    mlp_grads = reduce_dp(weight_grads("contract_weight_grads", places, lefts, tiles, cols, dp))

    hid = [
        hidden_grad(l, gg[l][1], ffn[l][2], ffn[l][3], ffn[l][4], gg[l][2], tots[l], crosses[l], ffn[l][0])
        for l in every
    ]
    last_parts = [scatter("add_in_%d" % l, hid[l][1], hid[l][2], True) for l in every]
    lefts = [ffn[l][0] for l in every]
    tiles = [[(l, hid[l][0], k) for l in every] for k in range(0, hidden, cols)]
    in_grads = reduce_dp(weight_grads("expand_weight_grads", places, lefts, tiles, cols, dp))
    backs = [conv_backward(l, last_parts[l], convs[l][1], ffn[l][1], seconds[l][1]) for l in every]
    grad_latents = jnp.stack([b[0] for b in backs])

    noise_cols = noise_embed.T
    r = noise_embed.shape[1]
    early = kernel_call(
        functools.partial(pack_early_body, lats), "pack_early", (sds((2 * r + 16, width), F32),),
        (noise_cols, *[s[3] for s in seconds], *[a[7] for a in attn], *[h[4] for h in hid], *[g[3] for g in gg]),
        [VM] * (1 + 4 * lats), (VM,),
    )[0]
    early = sum_dp(early)
    late = kernel_call(
        functools.partial(pack_late_body, lats), "pack_late", (sds((16, width), F32),),
        (*[b[1] for b in backs], *[h[3] for h in hid]), [VM] * (2 * lats), (VM,),
    )[0]
    late = sum_dp(late)
    base = 2 * r
    return (
        result,
        grad_latents,
        late[:9],
        late[9],
        in_grads,
        late[10 : 10 + hidden // width].reshape(-1),
        early[base + 8 : base + 8 + hidden // width].reshape(-1),
        early[base + 12 : base + 12 + hidden // width].reshape(-1),
        mlp_grads[:, :hidden].T,
        early[base + 2],
        early[:r],
        early[base],
        early[r : 2 * r],
        early[base + 1],
        mlp_grads[:, hidden:],
        early[base + 3],
        attn_grads[:, :width],
        early[base + 5],
        attn_grads[:, width : 2 * width],
        attn_grads[:, 2 * width : 3 * width],
        early[base + 6],
        attn_grads[:, 3 * width :].T,
        early[base + 4],
    )


def solution(mesh):
    rows = P("dp", None, "chan")
    weight_in = P(None, "chan")
    vec = P("chan")
    in_specs = (
        rows, P("dp", None), P("dp"), P("dp"), rows, P("dp", None), weight_in, vec, weight_in, vec, vec, vec,
        P("chan", None), vec, weight_in, vec, weight_in, vec, weight_in, vec, weight_in, vec, weight_in,
        weight_in, vec, P("chan", None), vec, rows,
    )
    out_specs = (
        rows, rows, weight_in, vec, P("dp", "chan"), vec, vec, vec, P("chan", "dp"), vec, weight_in, vec,
        weight_in, vec, P("dp", "chan"), vec, P("dp", "chan"), vec, P("dp", "chan"), P("dp", "chan"), vec,
        P("chan", "dp"), vec,
    )
    return jax.shard_map(local, mesh=mesh, in_specs=in_specs, out_specs=out_specs, check_vma=False)
```

```python
import functools

import jax
import jax.numpy as jnp
import numpy as np
from jax import lax
from jax.experimental import pallas as pl
from jax.experimental.pallas import tpu as pltpu
from jax.sharding import PartitionSpec as P

BF = jnp.bfloat16
F32 = jnp.float32
HEAD = 64
LANE = 128
EXTRA = 16
MARGIN = 40
WIDTHS = (36, 24, 18)
EPS = 1e-6

COSTS = {"gated_grad_1": 10**12}

VM = pl.BlockSpec(memory_space=pltpu.VMEM)
SM = pl.BlockSpec(memory_space=pltpu.SMEM)
ANY = pl.BlockSpec(memory_space=pl.ANY)


class Order:
    def __init__(self, ordered=True):
        self.ordered = ordered
        self.last = None
        self.pinned = []


def kernel_call(
    order, body, name, outs, args, in_specs, out_specs, grid=(1,), scratch=(), hbm=(), limit=20, after=()
):
    count = len(args)
    args = tuple(
        pltpu.with_memory_space_constraint(a, pltpu.HBM) if any(a is p for p in order.pinned) else a for a in args
    )
    outs = tuple(pltpu.HBM(o.shape, o.dtype) if i in hbm else o for i, o in enumerate(outs))
    if order.ordered and order.last is not None:
        args = tuple(args) + (order.last, *after)
        in_specs = list(in_specs) + [ANY] * (1 + len(after))
    extra = len(args) - count

    def ordered(*refs):
        body(*refs[:count], *refs[count + extra :])

    results = pl.pallas_call(
        ordered,
        name=name,
        out_shape=outs,
        grid=grid,
        in_specs=in_specs,
        out_specs=out_specs,
        scratch_shapes=scratch,
        compiler_params=pltpu.CompilerParams(vmem_limit_bytes=limit << 20),
        cost_estimate=pl.CostEstimate(flops=COSTS.get(name, 1000), bytes_accessed=1000, transcendentals=0),
    )(*args)
    order.pinned += [results[i] for i in hbm]
    order.last = min(results, key=lambda r: r.size * r.dtype.itemsize)
    return results


def half_rows(rows):
    return (rows // 16 + 1) // 2 * 16


def hop_body(count, picks, *refs):
    ins, outs, sems = refs[:count], refs[count:-1], refs[-1]
    copies, at = [], 0
    for ref, pick in zip(ins, picks):
        if pick is None:
            rows = ref.shape[-2]
            h = half_rows(rows)
            sources = []
            for part in (slice(0, h), slice(h, rows)):
                sources.append(ref.at[part] if len(ref.shape) == 2 else ref.at[:, part])
        else:
            sources = [ref.at[pick]]
        for source in sources:
            copies.append(pltpu.make_async_copy(source, outs[at], sems.at[at]))
            at += 1
    run_copies(copies)


def hop(order, name, *arrays):
    outs, picks, ins = [], [], []
    for a in arrays:
        if isinstance(a, tuple):
            ins.append(a[0])
            picks.append(a[1])
            outs.append(sds(a[0].shape[1:], a[0].dtype))
        else:
            ins.append(a)
            picks.append(None)
            h = half_rows(a.shape[-2])
            for rows in (h, a.shape[-2] - h):
                outs.append(sds(a.shape[:-2] + (rows, a.shape[-1]), a.dtype))
    got = list(kernel_call(
        order, functools.partial(hop_body, len(ins), picks), name, tuple(outs),
        tuple(ins), [ANY] * len(ins), (ANY,) * len(outs),
        scratch=[pltpu.SemaphoreType.DMA((len(outs),))],
    ))
    return [got.pop(0) if pick is not None else (got.pop(0), got.pop(0)) for pick in picks]


def sds(shape, dtype):
    return jax.ShapeDtypeStruct(shape, dtype)


def nn(a, b):
    return jnp.dot(a, b, preferred_element_type=F32)


def nt(a, b):
    return lax.dot_general(a, b, (((1,), (1,)), ((), ())), preferred_element_type=F32)


def tn(a, b):
    return lax.dot_general(a, b, (((0,), (0,)), ((), ())), preferred_element_type=F32)


def eye():
    return (
        lax.broadcasted_iota(jnp.int32, (LANE, LANE), 0)
        == lax.broadcasted_iota(jnp.int32, (LANE, LANE), 1)
    ).astype(F32)


def col_to_tile(col):
    size = col.shape[0]
    diag = eye()
    row = lax.broadcasted_iota(jnp.int32, (8, LANE), 0)
    tile = jnp.zeros((8, LANE), F32)
    for t in range(pl.cdiv(size, LANE)):
        n = min(LANE, size - t * LANE)
        line = jnp.sum(col[t * LANE : t * LANE + n] * diag[:n], axis=0, keepdims=True)
        tile = jnp.where(row == t, line, tile)
    return tile


def tile_to_col(tile, size):
    diag = eye()
    cols = []
    for t in range(pl.cdiv(size, LANE)):
        n = min(LANE, size - t * LANE)
        cols.append(jnp.sum(tile[t : t + 1] * diag[:n], axis=1, keepdims=True))
    return jnp.concatenate(cols, axis=0)


def split_stats(both):
    high = both.astype(BF)
    rest = both - high.astype(F32)
    mid = rest.astype(BF)
    low = (rest - mid.astype(F32)).astype(BF)
    return jnp.concatenate([high, mid, low], axis=1)


def join_stats(tile):
    wide = tile.astype(F32)
    return wide[:, :LANE] + wide[:, LANE : 2 * LANE] + wide[:, 2 * LANE : 3 * LANE]


def stats_tile(first, second):
    return split_stats(jnp.concatenate([col_to_tile(first), col_to_tile(second)], axis=0))


def block_copies(me, refs, dst, sems, width, base=0, first_sem=0):
    rows = refs[0].shape[0]
    h = half_rows(rows)
    plan = ((0, 0, rows), (1, 0, rows), (2, 0, rows), (3, 0, h), (3, h, rows - h))
    copies = []
    for i, (ref, (k, start, size)) in enumerate(zip(refs, plan)):
        place = pl.multiple_of((me ^ k) * width, LANE)
        target = dst.at[pl.ds(base + start, size), pl.ds(place, width)]
        copies.append(pltpu.make_async_copy(ref, target, sems.at[first_sem + i]))
    return copies


def scatter_copies(me, part, outs, sems, width):
    send, send_a, send_b, keep = outs
    rows = part.shape[0]
    h = half_rows(rows)
    plan = ((0, 0, rows, keep.at[0]), (2, 0, rows, keep.at[1]), (1, 0, rows, send), (3, 0, h, send_a), (3, h, rows - h, send_b))
    copies = []
    for i, (k, start, size, dst) in enumerate(plan):
        place = pl.multiple_of((me ^ k) * width, LANE)
        source = part.at[pl.ds(start, size), pl.ds(place, width)]
        copies.append(pltpu.make_async_copy(source, dst, sems.at[i]))
    return copies


def scatter_shapes(rows, width):
    h = half_rows(rows)
    return (
        sds((rows, width), BF), sds((h, width), BF), sds((rows - h, width), BF), sds((2, rows, width), BF)
    )


def run_copies(copies):
    for c in copies:
        c.start()
    for c in copies:
        c.wait()


def norm_rows(raw, out, stat, size, width, blocks):
    total = width * blocks
    means = []
    for b in range(blocks):
        means.append(tile_to_col(raw[size : size + 8, b * width : b * width + LANE].astype(F32), size))
    mean_sum = jnp.zeros((size, 1), F32)
    for b in range(blocks):
        part = raw[:size, b * width : (b + 1) * width].astype(F32)
        mean_sum = mean_sum + jnp.sum(part, axis=1, keepdims=True) + width * means[b]
    mean = mean_sum * (1.0 / total)
    square = jnp.zeros((size, 1), F32)
    for b in range(blocks):
        part = raw[:size, b * width : (b + 1) * width].astype(F32) + (means[b] - mean)
        square = square + jnp.sum(part * part, axis=1, keepdims=True)
    inverse = lax.rsqrt(square * (1.0 / total) + EPS)
    for b in range(blocks):
        part = raw[:size, b * width : (b + 1) * width].astype(F32) + (means[b] - mean)
        out[:size, b * width : (b + 1) * width] = (part * inverse).astype(BF)
    stat[0] = jnp.broadcast_to(mean, (size, LANE))
    stat[1] = jnp.broadcast_to(inverse, (size, LANE))


def send_rows(values, pay, size, width):
    mean = jnp.mean(values, axis=1, keepdims=True).astype(BF).astype(F32)
    pay[:size] = (values - mean).astype(BF)
    tile = col_to_tile(mean).astype(BF)
    pay[size:] = jnp.zeros((EXTRA, width), BF)
    pay[size : size + EXTRA, :LANE] = jnp.concatenate([tile, jnp.zeros((8, LANE), BF)], axis=0)


def column_masks(size, width):
    slot = lax.broadcasted_iota(jnp.int32, (size, 1), 0).astype(F32)
    col = slot - width * jnp.floor((slot + 0.5) * (1.0 / width))
    return col > 0.5, col < width - 1.5


def conv_forward_body(l, info, x_ref, taps, bias, pay, conv, pad):
    size, width = conv.shape
    slot = lax.broadcasted_iota(jnp.int32, (size, 1), 0)
    x = jnp.where(slot < info[l, 0], x_ref[...].astype(F32), 0.0)
    pad[:MARGIN] = jnp.zeros((MARGIN, width), F32)
    pad[MARGIN + size :] = jnp.zeros((MARGIN, width), F32)
    here = slice(MARGIN, MARGIN + size)
    for bucket, w in enumerate(WIDTHS):

        @pl.when(info[l, 1] == bucket)
        def _():
            not_first, not_last = column_masks(size, w)
            pad[here] = x
            left = jnp.where(not_first, pad[MARGIN - 1 : MARGIN - 1 + size], 0.0)
            right = jnp.where(not_last, pad[MARGIN + 1 : MARGIN + 1 + size], 0.0)
            total = bias[...] + left * taps[3:4] + x * taps[4:5] + right * taps[5:6]
            pad[here] = left * taps[0:1] + x * taps[1:2] + right * taps[2:3]
            total = total + pad[MARGIN - w : MARGIN - w + size]
            pad[here] = left * taps[6:7] + x * taps[7:8] + right * taps[8:9]
            conv[...] = total + pad[MARGIN + w : MARGIN + w + size]

    send_rows(conv[...], pay, size, width)


def conv_backward_body(l, info, keep, got, far, conv, stat, x_ref, first_grad, taps, out, sums, pad, total_width):
    size, width = conv.shape
    slot = lax.broadcasted_iota(jnp.int32, (size, 1), 0)
    mask = slot < info[l, 0]
    grad = keep[:size].astype(F32) + got[:size].astype(F32) + far[:size].astype(F32)
    both = join_stats(keep[size:]) + join_stats(got[size:]) + join_stats(far[size:])
    both = both * (1.0 / total_width)
    mean_grad = tile_to_col(both[:8], size)
    mean_cross = tile_to_col(both[8:], size)
    mean = stat[0][:, :1]
    inverse = stat[1][:, :1]
    normed = (conv[...] - mean) * inverse
    grad = inverse * (grad - mean_grad - normed * mean_cross)
    x = jnp.where(mask, x_ref[...].astype(F32), 0.0)
    pad[:MARGIN] = jnp.zeros((MARGIN, width), F32)
    pad[MARGIN + size :] = jnp.zeros((MARGIN, width), F32)
    here = slice(MARGIN, MARGIN + size)
    sums[...] = jnp.zeros_like(sums)
    sums[9:10] = jnp.sum(grad, axis=0, keepdims=True)
    for bucket, w in enumerate(WIDTHS):

        @pl.when(info[l, 1] == bucket)
        def _():
            not_first, not_last = column_masks(size, w)
            pad[here] = x
            left = jnp.where(not_first, pad[MARGIN - 1 : MARGIN - 1 + size], 0.0)
            right = jnp.where(not_last, pad[MARGIN + 1 : MARGIN + 1 + size], 0.0)
            pad[here] = grad
            rows = (pad[MARGIN + w : MARGIN + w + size], grad, pad[MARGIN - w : MARGIN - w + size])
            for r in range(3):
                for c, side in enumerate((left, x, right)):
                    tap = 3 * r + c
                    sums[tap : tap + 1] = jnp.sum(rows[r] * side, axis=0, keepdims=True)
            back = [sum(rows[r] * taps[3 * r + c : 3 * r + c + 1] for r in range(3)) for c in range(3)]
            pad[here] = jnp.where(not_first, back[0], 0.0)
            total = back[1] + pad[MARGIN + 1 : MARGIN + 1 + size]
            pad[here] = jnp.where(not_last, back[2], 0.0)
            total = total + pad[MARGIN - 1 : MARGIN - 1 + size]
            out[...] = (first_grad[...] + jnp.where(mask, total, 0.0)).astype(BF)


def gelu_both(h):
    t_den = 1.0 + (0.3275911 * 0.7071067811865476) * jnp.abs(h)
    t = pl.reciprocal(t_den, approx=True)
    t = t * (2.0 - t_den * t)
    bell = jnp.exp(-0.5 * h * h)
    poly = t * (
        0.127414796 + t * (-0.142248368 + t * (0.7107068705 + t * (-0.7265760135 + t * 0.5307027145)))
    )
    tail = poly * bell
    phi = jnp.where(h >= 0, 1.0 - tail, tail)
    return h * phi, phi + h * bell * 0.3989422804014327


def ffn_in_body(
    l, lats, info, b0, b1, b2, b3, b4, w, bias, nrm, stat, act, slope, spat, total, raw, sems, width, chunk
):
    j = pl.program_id(0)
    size = nrm.shape[0]

    @pl.when(j == 0)
    def _():
        run_copies(block_copies(info[lats, 0], (b0, b1, b2, b3, b4), raw, sems, width))
        norm_rows(raw, nrm, stat, size, width, 4)
        total[...] = jnp.zeros_like(total)

    valid_from = size - size // 32
    cols = act.shape[1]
    square = jnp.zeros((1, cols), F32)
    for r in range(0, size, chunk):
        h = nn(nrm[r : r + chunk], w[...]) + bias[...]
        a, d = gelu_both(h)
        act[r : r + chunk] = a.astype(BF)
        slope[r : r + chunk] = d.astype(BF)
        sq = a * a
        if r + chunk > valid_from:
            slot = r + lax.broadcasted_iota(jnp.int32, (chunk, 1), 0)
            sq = jnp.where(slot < info[l, 0], sq, 0.0)
        square = square + jnp.sum(sq, axis=0, keepdims=True)
    here = jnp.sqrt(square)
    spat[...] = here
    total[...] = total[...] + jnp.sum(here)


def denominator(t0, t1, t2, t3, hidden_total):
    whole = t0[...] + t1[...] + t2[...] + t3[...]
    return whole[:1, :1] * (1.0 / hidden_total) + EPS


def ffn_out_body(lats, hidden_total, info, act, spat, t0, t1, t2, t3, gamma, beta, w, gated, s0, s1, s2, keep, part, sems, width, chunk):
    j = pl.program_id(0)
    size = act.shape[0]

    @pl.when(j == 0)
    def _():
        gain = 1.0 + gamma[...] * (spat[...] / denominator(t0, t1, t2, t3, hidden_total))
        for r in range(0, size, chunk):
            rows = slice(r, r + chunk)
            gated[rows] = (act[rows].astype(F32) * gain + beta[...]).astype(BF)

    cols = w.shape[1]
    part[:, pl.ds(pl.multiple_of(j * cols, LANE), cols)] = nn(gated[...], w[...]).astype(BF)

    @pl.when(j == pl.num_programs(0) - 1)
    def _():
        run_copies(scatter_copies(info[lats, 0], part, (s0, s1, s2, keep), sems, width))


def add_body(stats, keep, got_a, got_b, out):
    h = got_a.shape[0]
    size = out.shape[0] - (EXTRA if stats else 0)
    out[:h] = (keep[:h].astype(F32) + got_a[...].astype(F32)).astype(BF)
    out[h:size] = (keep[h:size].astype(F32) + got_b[: size - h].astype(F32)).astype(BF)
    if stats:
        out[size:] = split_stats(join_stats(keep[size:]) + join_stats(got_b[size - h :]))


def middle_body(x, keep, got, far, out_bias, scale, shift, first, pay):
    size, width = first.shape
    value = x[...].astype(F32) + (
        keep[...].astype(F32) + got[...].astype(F32) + far[...].astype(F32) + out_bias[...]
    )
    first[...] = value
    send_rows(value * (1.0 + scale[...]) + shift[...], pay, size, width)


def text_body(lats, info, b0, b1, b2, b3, b4, w, bias, full, low, sems, width, text_len):
    lat_count, rows, _ = low.shape
    copies = []
    for l in range(lat_count):
        refs = [b.at[l] for b in (b0, b1, b2, b3, b4)]
        copies += block_copies(info[lats, 0], refs, full.at[l], sems, width, first_sem=5 * l)
    run_copies(copies)
    row = lax.broadcasted_iota(jnp.int32, (rows, 1), 0)
    for l in range(lat_count):
        low[l] = jnp.where(row < text_len, nn(full[l], w[...]) + bias[...], 0.0).astype(BF)


def attention_body(
    l, lats, info, p0, p1, p2, p3, p4, x0, x1, x2, x3, x4, g0, g1, g2, g3, g4, wq, wk, wv, wo, q_bias, v_bias,
    ctx, stat, g_full, att, dqkv, s0, s1, s2, keep, sums,
    raw, w_all, w_out, q_s, k_s, v_s, do_s, kt_s, vt_s, att_t, dq_t, scores, part, sems, width,
):
    me = info[lats, 0]
    size = att.shape[0]
    rows = ctx.shape[0]
    total = ctx.shape[1]
    text = rows - size
    factor = HEAD ** (-0.5)
    copy_in = block_copies(me, (p0, p1, p2, p3, p4), raw, sems, width)
    texts = [x.at[l] for x in (x0, x1, x2, x3, x4)]
    copy_in += block_copies(me, texts, ctx, sems, width, base=size, first_sem=5)
    copy_w = [
        pltpu.make_async_copy(ref, w_all.at[:, k * width : (k + 1) * width], sems.at[10 + k])
        for k, ref in enumerate((wq, wk, wv))
    ]
    copy_g = [pltpu.make_async_copy(wo, w_out, sems.at[13])]
    copy_g += block_copies(me, (g0, g1, g2, g3, g4), g_full, sems, width, first_sem=14)
    for c in copy_in + copy_w + copy_g:
        c.start()
    for c in copy_in:
        c.wait()
    norm_rows(raw, ctx, stat, size, width, 4)
    for c in copy_w:
        c.wait()
    q_s[...] = ((nn(ctx[:size], w_all[:, :width]) + q_bias[...]).astype(BF).astype(F32) * factor).astype(BF)
    keys = nn(ctx[...], w_all[:, width : 2 * width]).astype(BF)
    k_s[...] = keys
    kt_s[...] = keys.T
    values = (nn(ctx[...], w_all[:, 2 * width :]) + v_bias[...]).astype(BF)
    v_s[...] = values
    vt_s[...] = values.T
    for c in copy_g:
        c.wait()
    do_s[...] = nt(g_full[...], w_out[...]).astype(BF)
    tail = (size - size // 32) // 8 * 8
    key_row = tail + lax.broadcasted_iota(jnp.int32, (rows - tail, 1), 0)
    key_ok = (key_row < info[l, 0]) | ((key_row >= size) & (key_row < size + info[l, 2]))

    def pair(p, carry):
        lo = pl.multiple_of(p * LANE, LANE)
        q2 = q_s[:, pl.ds(lo, LANE)]
        k2 = k_s[:, pl.ds(lo, LANE)]
        v2 = v_s[:, pl.ds(lo, LANE)]
        do2 = do_s[:, pl.ds(lo, LANE)]
        dks, dvs = [], []
        for half in range(2):
            lanes = slice(half * HEAD, (half + 1) * HEAD)
            line = pl.ds(pl.multiple_of(p * LANE + half * HEAD, HEAD), HEAD)
            qh, kh, vh, doh = q2[:, lanes], k2[:, lanes], v2[:, lanes], do2[:, lanes]
            scores[...] = nt(kh, qh)
            scores[tail:] = jnp.where(key_ok, scores[tail:], -1e30)
            top = jnp.max(scores[...], axis=0, keepdims=True)
            expo = jnp.exp(scores[...] - top)
            probs = expo * (1.0 / jnp.sum(expo, axis=0, keepdims=True))
            low = probs.astype(BF)
            att_t[line] = nn(vt_s[line], low)
            scores[...] = probs
            grad_p = nt(vh, doh)
            dvs.append(nn(low, doh))
            dot = jnp.sum(scores[...] * grad_p, axis=0, keepdims=True)
            grad_s = (scores[...] * (grad_p - dot)).astype(BF)
            dks.append(nn(grad_s, qh))
            dq_t[line] = nn(kt_s[line], grad_s) * factor
        dqkv[:, pl.ds(pl.multiple_of(width + lo, LANE), LANE)] = jnp.concatenate(dks, axis=1).astype(BF)
        dqkv[:, pl.ds(pl.multiple_of(2 * width + lo, LANE), LANE)] = jnp.concatenate(dvs, axis=1).astype(BF)
        return carry

    lax.fori_loop(0, width // LANE, pair, 0)
    att[...] = att_t[...].astype(BF).T
    dq = dq_t[...].astype(BF).T
    dqkv[:size, :width] = dq
    dqkv[size:, :width] = jnp.zeros((text, width), BF)
    sums[...] = jnp.zeros_like(sums)
    sums[0:1] = jnp.sum(dq.astype(F32), axis=0, keepdims=True)
    sums[1:2] = jnp.sum(dqkv[:, 2 * width :].astype(F32), axis=0, keepdims=True)
    first = jnp.zeros((size, 1), F32)
    second = jnp.zeros((size, 1), F32)
    cols = 256
    for n in range(0, total, cols):
        block = nt(dqkv[...], w_all[n : n + cols]).astype(BF)
        part[:rows, n : n + cols] = block
        wide = block[:size].astype(F32)
        first = first + jnp.sum(wide, axis=1, keepdims=True)
        second = second + jnp.sum(wide * ctx[:size, n : n + cols].astype(F32), axis=1, keepdims=True)
    tile = stats_tile(first, second)
    for b in range(4):
        part[rows:, b * width : (b + 1) * width] = tile
    run_copies(scatter_copies(me, part, (s0, s1, s2, keep), sems, width))


def project_body(lats, info, att, w, s0, s1, s2, keep, part, sems, width):
    cols = 512
    for n in range(0, part.shape[1], cols):
        part[:, n : n + cols] = nn(att[...], w[:, n : n + cols]).astype(BF)
    run_copies(scatter_copies(info[lats, 0], part, (s0, s1, s2, keep), sems, width))


def result_body(first, scale, shift, keep, got, far, bias, out):
    second = first[...] * (1.0 + scale[...]) + shift[...]
    branch = keep[...].astype(F32) + got[...].astype(F32) + far[...].astype(F32) + bias[...]
    out[...] = (second + branch).astype(BF)


def second_grad_body(keep, got, far, g_ref, first_ref, stat, scale, shift, pay, first_grad, text, sums, total_width, text_len):
    size, width = first_grad.shape
    rows = keep.shape[0] - EXTRA
    both = join_stats(keep[rows:]) + join_stats(got[rows:]) + join_stats(far[rows:])
    both = both * (1.0 / total_width)
    mean_grad = tile_to_col(both[:8], size)
    mean_cross = tile_to_col(both[8:], size)
    grad = keep[:size].astype(F32) + got[:size].astype(F32) + far[:size].astype(F32)
    first = first_ref[...]
    gain = 1.0 + scale[...]
    inverse = stat[1][:, :1]
    normed = (first * gain + shift[...] - stat[0][:, :1]) * inverse
    upstream = g_ref[...].astype(F32)
    second_grad = upstream + inverse * (grad - mean_grad - normed * mean_cross)
    scaled = second_grad * gain
    pay[...] = scaled.astype(BF)
    first_grad[...] = scaled
    row = lax.broadcasted_iota(jnp.int32, (rows - size, 1), 0)
    tail = keep[size:rows].astype(F32) + got[size:rows].astype(F32) + far[size:rows].astype(F32)
    low = jnp.where(row < text_len, tail, 0.0).astype(BF)
    text[...] = low
    sums[...] = jnp.zeros_like(sums)
    sums[0:1] = jnp.sum(second_grad * first, axis=0, keepdims=True)
    sums[1:2] = jnp.sum(second_grad, axis=0, keepdims=True)
    sums[2:3] = jnp.sum(scaled, axis=0, keepdims=True)
    sums[3:4] = jnp.sum(low.astype(F32), axis=0, keepdims=True)
    sums[4:5] = jnp.sum(upstream, axis=0, keepdims=True)


def gated_grad_body(lats, info, b0, b1, b2, b3, b4, w, act, gamma, spat, full, out, s1, s2, total, sems, width, chunk):
    j = pl.program_id(0)
    size = full.shape[0]

    @pl.when(j == 0)
    def _():
        run_copies(block_copies(info[lats, 0], (b0, b1, b2, b3, b4), full, sems, width))
        total[...] = jnp.zeros_like(total)

    cols = out.shape[1]
    cross = jnp.zeros((1, cols), F32)
    plain = jnp.zeros((1, cols), F32)
    for r in range(0, size, chunk):
        grad = nt(full[r : r + chunk], w[...])
        out[r : r + chunk] = grad.astype(BF)
        cross = cross + jnp.sum(grad * act[r : r + chunk].astype(F32), axis=0, keepdims=True)
        plain = plain + jnp.sum(grad, axis=0, keepdims=True)
    s1[...] = cross
    s2[...] = plain
    total[...] = total[...] + jnp.sum(cross * gamma[...] * spat[...])


def hidden_grad_body(
    l, lats, hidden_total, info, gg, act, slope, spat, s1, gamma, t0, t1, t2, t3, c0, c1, c2, c3, w, nrm,
    hidden, d0, d1, d2, keep, bias_sum, gamma_sum, part, acc, sems, width, chunk,
):
    j = pl.program_id(0)
    size = hidden.shape[0]

    @pl.when(j == 0)
    def _():
        den = denominator(t0, t1, t2, t3, hidden_total)
        cross = (c0[...] + c1[...] + c2[...] + c3[...])[:1, :1]
        response = spat[...] / den
        gamma_sum[...] = response * s1[...]
        grad_spat = gamma[...] * s1[...] / den - cross / (den * den) * (1.0 / hidden_total)
        gain = gamma[...] * response + 1.0
        pull = grad_spat / spat[...]
        total = jnp.zeros_like(bias_sum[...])
        for r in range(0, size, chunk):
            rows = slice(r, r + chunk)
            slot = r + lax.broadcasted_iota(jnp.int32, (chunk, 1), 0)
            active = jnp.where(slot < info[l, 0], act[rows].astype(F32), 0.0)
            grad = gg[rows].astype(F32) * gain + pull * active
            low = (grad * slope[rows].astype(F32)).astype(BF)
            hidden[rows] = low
            total = total + jnp.sum(low.astype(F32), axis=0, keepdims=True)
        bias_sum[...] = total
        acc[...] = jnp.zeros_like(acc)

    cols = w.shape[0]
    block = nt(hidden[...], w[...]).astype(BF)
    part[:size, pl.ds(pl.multiple_of(j * cols, LANE), cols)] = block
    wide = block.astype(F32)
    acc[0] = acc[0] + jnp.sum(wide, axis=1, keepdims=True)
    acc[1] = acc[1] + jnp.sum(wide * nrm[...].astype(F32), axis=1, keepdims=True)

    @pl.when(j == pl.num_programs(0) - 1)
    def _():
        tile = stats_tile(acc[0][:, :1], acc[1][:, :1])
        for b in range(4):
            part[size:, b * width : (b + 1) * width] = tile
        run_copies(scatter_copies(info[lats, 0], part, (d0, d1, d2, keep), sems, width))


def place_blocks(places, result, send, keep):
    half = keep.shape[0]
    rows = keep.shape[1]
    for s in range(half):
        keep[s] = result[pl.ds(pl.multiple_of(places[s] * rows, 16), rows), :]
        send[s] = result[pl.ds(pl.multiple_of(places[half + s] * rows, 16), rows), :]


def weight_grad_body(pairs, split, plan, places, *refs):
    lefts_rights = refs[:pairs]
    outs = refs[pairs:-1]
    result = refs[-1]
    j = pl.program_id(0)
    for step, terms in enumerate(plan):

        @pl.when(j == step)
        def _():
            total = None
            for left, right in terms:
                term = tn(lefts_rights[left][...], lefts_rights[right][...])
                total = term if total is None else total + term
            result[...] = total.astype(BF)

    if split:
        place_blocks(places, result, *outs)
    else:
        outs[0][...] = result[...]


def weight_grads(order, name, places, lefts, tiles, cols, dp, after=()):
    operands = list(lefts)
    specs = [VM] * len(lefts)
    plan = []
    for terms in tiles:
        entry = []
        for left, right, start in terms:
            entry.append((left, right, start))
        plan.append(entry)
    rights = []
    for terms in plan:
        for _, right, _ in terms:
            if not any(right is r for r in rights):
                rights.append(right)
    body_plan = []
    for step, terms in enumerate(plan):
        entry = []
        for left, right, _ in terms:
            entry.append((left, len(lefts) + [right is r for r in rights].index(True)))
        body_plan.append(entry)
    for right in rights:
        table = []
        last = 0
        for terms in plan:
            for _, r, start in terms:
                if r is right:
                    last = start // cols
            table.append(last)
        first = next(start // cols for terms in plan for _, r, start in terms if r is right)
        for i in range(len(table)):
            if not any(r is right for terms in plan[: i + 1] for _, r, _ in terms):
                table[i] = first

        def index(j, table=tuple(table)):
            place = jnp.int32(table[0])
            for i in range(1, len(table)):
                if table[i] != table[i - 1]:
                    place = jnp.where(j >= i, jnp.int32(table[i]), place)
            return (0, place)

        operands.append(right)
        specs.append(pl.BlockSpec((right.shape[0], cols), index))
    width = lefts[0].shape[1]
    wide = cols * len(tiles)
    split = places is not None
    if split:
        half = dp // 2
        shape = sds((half, width // dp, wide), BF)
        outs = (shape, shape)
        out_specs = (pl.BlockSpec((half, width // dp, cols), lambda j: (0, 0, j)),) * 2
        args = (places, *operands)
        body = functools.partial(weight_grad_body, len(operands), True, body_plan)
        in_specs = [SM] + specs
    else:
        outs = (sds((width, wide), BF),)
        out_specs = (pl.BlockSpec((width, cols), lambda j: (0, j)),)
        args = tuple(operands)
        body = functools.partial(weight_grad_body, len(operands), False, body_plan, None)
        in_specs = specs
    return kernel_call(
        order, body, name, outs, args, in_specs, out_specs, grid=(len(tiles),),
        scratch=[pltpu.VMEM((width, cols), BF)], hbm=(1,) if split else (0,), limit=36, after=after,
    )


def combine_body(small, keep, got, *refs):
    if small:
        mine, near, *outs, whole = refs
        whole[...] = mine[...] + near[...]
    else:
        outs = refs
    count = keep.shape[0]
    for k in range(count):
        total = (keep[k].astype(F32) + got[k].astype(F32)).astype(BF)
        if count == 2:
            outs[1 - k][...] = total
        else:
            outs[1 - k % 2][k // 2] = total


def finish_body(counts, small, layout, *refs):
    chunks = []
    at = 0
    for n in counts:
        chunks.append(refs[at : at + n])
        at += n
    extra = refs[at : at + small]
    outs = refs[at + small :]
    for ins, plan in zip(chunks, layout):
        for start, cols, out, offset, flip in plan:
            lanes = slice(start, start + cols)
            total = 0.0
            for ref in ins:
                total = total + ref[:, lanes].astype(F32)
            if flip:
                outs[out][offset : offset + cols] = total.T
            else:
                outs[out][:, offset : offset + cols] = total
    if small:
        outs[-1][...] = sum(e[...] for e in extra)


def pack_body(lat_count, noise, *refs):
    second, attn, gam, bet, conv, hid = (refs[k * lat_count : (k + 1) * lat_count] for k in range(6))
    out = refs[-1]
    width = out.shape[1]
    r = noise.shape[0]
    out[...] = jnp.zeros_like(out)
    out[:r] = sum(noise[:, l : l + 1] * second[l][0:1] for l in range(lat_count))
    out[r : 2 * r] = sum(noise[:, l : l + 1] * second[l][1:2] for l in range(lat_count))
    base = 2 * r
    out[base : base + 16] = sum(c[...] for c in conv)
    for k, group in enumerate((gam, bet, hid)):
        whole = sum(g[...] for g in group)
        for b in range(whole.shape[1] // width):
            at = base + 16 + 4 * k + b
            out[at : at + 1] = whole[:, b * width : (b + 1) * width]
    for i in range(5):
        out[base + 28 + i : base + 29 + i] = sum(second[l][i : i + 1] for l in range(lat_count))
    for i in range(2):
        out[base + 33 + i : base + 34 + i] = sum(attn[l][i : i + 1] for l in range(lat_count))


def local(
    latents, valid_mask, bucket_ids, text_count, text_tokens, noise_embed, conv_kernel, conv_bias,
    mixer_expand_weight, ffn_in_bias, grn_gamma, grn_beta, mixer_contract_weight, ffn_out_bias,
    scale_weight, scale_bias, shift_weight, shift_bias, text_weight, text_bias, query_weight, query_bias,
    key_weight, value_weight, value_bias, attn_out, attn_out_bias, upstream,
):
    lats, size, width = latents.shape
    groups = lax.axis_size("chan")
    dp = lax.axis_size("dp")
    total = width * groups
    hidden = mixer_expand_weight.shape[1]
    hidden_total = hidden * groups
    text_len = text_tokens.shape[1]
    text_rows = pl.cdiv(text_len, 16) * 16
    rows = size + text_rows
    highest = lax.Precision.HIGHEST
    me = lax.axis_index("chan")
    order = Order()
    order.pinned += [
        mixer_expand_weight, mixer_contract_weight, text_weight, query_weight, key_weight, value_weight, attn_out,
        latents, upstream,
    ]

    def xswap(v):
        return lax.ppermute(v, "chan", [(i, i ^ 2) for i in range(groups)])

    def cswap(v):
        return lax.ppermute(v, "chan", [(i, i ^ 1) for i in range(groups)])

    def gather_start(v):
        return v, cswap(v), xswap(v)

    def gather_end(state, halves):
        return (*state, *(cswap(h) for h in halves))

    def gather_small(v):
        return v, cswap(v), xswap(v), lax.ppermute(v, "chan", [(i, i ^ 3) for i in range(groups)])

    def line(v):
        return v.reshape(1, -1)

    info = jnp.stack(
        [jnp.sum(valid_mask, axis=1), bucket_ids, text_count, jnp.zeros_like(bucket_ids)], axis=1
    )
    info = jnp.concatenate([info, jnp.full((1, 4), me, jnp.int32)], axis=0).astype(jnp.int32)

    def lat_spec(l, *shape):
        return pl.BlockSpec((None,) + shape, lambda *_: (l,) + (0,) * len(shape))

    def part_spec(k, shape):
        return pl.BlockSpec((None,) + tuple(shape[1:]), lambda *_: (k, 0, 0))

    text_act = jax.nn.silu(text_tokens.astype(F32)).astype(BF)
    text_act = jnp.pad(text_act, ((0, 0), (0, text_rows - text_len), (0, 0)))
    text_state = gather_start(text_act)

    def conv_forward(l):
        return kernel_call(
            order, functools.partial(conv_forward_body, l), "conv_forward_%d" % l,
            (sds((size + EXTRA, width), BF), sds((size, width), F32)),
            (info, latents, conv_kernel, line(conv_bias)),
            [SM, lat_spec(l, size, width), VM, VM], (VM, VM),
            scratch=[pltpu.VMEM((size + 2 * MARGIN, width), F32)], hbm=(1,),
        )

    tile_cols = 256

    def ffn_in(l, blocks):
        n = hidden // tile_cols
        col = pl.BlockSpec((1, tile_cols), lambda j: (0, j))
        wide = pl.BlockSpec((size, tile_cols), lambda j: (0, j))
        return kernel_call(
            order, functools.partial(ffn_in_body, l, lats, width=width, chunk=size // 3), "ffn_in_%d" % l,
            (sds((size, total), BF), sds((2, size, LANE), F32), sds((size, hidden), BF),
             sds((size, hidden), BF), sds((1, hidden), F32), sds((8, LANE), F32)),
            (info, *blocks, mixer_expand_weight, line(ffn_in_bias)),
            [SM] + [ANY] * 5 + [pl.BlockSpec((total, tile_cols), lambda j: (0, j)), col],
            (VM, VM, wide, wide, col, VM), grid=(n,),
            scratch=[pltpu.VMEM((size + EXTRA, total), BF), pltpu.SemaphoreType.DMA((5,))], hbm=(0, 1, 3),
        )

    def ffn_out(l, act, spat, tots, after=()):
        n = total // tile_cols
        return kernel_call(
            order, functools.partial(ffn_out_body, lats, hidden_total, width=width, chunk=32), "ffn_out_%d" % l,
            (sds((size, hidden), BF),) + scatter_shapes(size, width),
            (info, act, spat, *tots, line(grn_gamma), line(grn_beta), mixer_contract_weight),
            [SM] + [VM] * 8 + [pl.BlockSpec((hidden, tile_cols), lambda j: (0, j))],
            (VM,) + (ANY,) * 4, grid=(n,),
            scratch=[pltpu.VMEM((size, total), BF), pltpu.SemaphoreType.DMA((5,))], hbm=(0, 4), after=after,
        )

    def swap_halves(outs):
        return tuple(cswap(o) for o in outs)

    def scatter_end(name, keep, gots, stats, after=()):
        got, got_a, got_b = gots
        half = kernel_call(
            order, functools.partial(add_body, stats), name, (sds(keep.shape[1:], BF),), (keep, got_a, got_b),
            [part_spec(1, keep.shape), VM, VM], (VM,), after=after,
        )[0]
        return keep, got, xswap(half)

    scale_rows = (jnp.dot(noise_embed, scale_weight, precision=highest) + scale_bias)[:, None]
    shift_rows = (jnp.dot(noise_embed, shift_weight, precision=highest) + shift_bias)[:, None]

    def middle(l, pieces):
        keep, got, far = pieces
        spec = part_spec(0, keep.shape)
        row = lat_spec(l, 1, width)
        return kernel_call(
            order, middle_body, "middle_%d" % l,
            (sds((size, width), F32), sds((size + EXTRA, width), BF)),
            (latents, keep, got, far, line(ffn_out_bias), scale_rows, shift_rows),
            [lat_spec(l, size, width), spec, VM, VM, VM, row, row], (VM, VM), hbm=(0,),
        )

    def text_low_rows(blocks, after):
        return kernel_call(
            order, functools.partial(text_body, lats, width=width, text_len=text_len), "text_rows",
            (sds((lats, text_rows, total), BF), sds((lats, text_rows, width), BF)),
            (info, *blocks, text_weight, line(text_bias)),
            [SM] + [ANY] * 5 + [VM, VM], (VM, VM), scratch=[pltpu.SemaphoreType.DMA((5 * lats,))], hbm=(0,), after=after,
        )

    def attention(l, blocks, texts, grads):
        return kernel_call(
            order, functools.partial(attention_body, l, lats, width=width), "attention_%d" % l,
            (sds((rows, total), BF), sds((2, size, LANE), F32), sds((size, total), BF),
             sds((size, width), BF), sds((rows, 3 * width), BF))
            + scatter_shapes(rows + EXTRA, width) + (sds((8, width), F32),),
            (info, *blocks, *texts, *grads, query_weight, key_weight, value_weight, attn_out,
             line(query_bias), line(value_bias)),
            [SM] + [ANY] * 19 + [VM, VM],
            (VM, VM, VM, VM, VM, ANY, ANY, ANY, ANY, VM),
            scratch=[
                pltpu.VMEM((size + EXTRA, total), BF),
                pltpu.VMEM((total, 3 * width), BF),
                pltpu.VMEM((width, total), BF),
                pltpu.VMEM((size, width), BF),
                pltpu.VMEM((rows, width), BF),
                pltpu.VMEM((rows, width), BF),
                pltpu.VMEM((size, width), BF),
                pltpu.VMEM((width, rows), BF),
                pltpu.VMEM((width, rows), BF),
                pltpu.VMEM((width, size), F32),
                pltpu.VMEM((width, size), F32),
                pltpu.VMEM((rows, size), F32),
                pltpu.VMEM((rows + EXTRA, total), BF),
                pltpu.SemaphoreType.DMA((19,)),
            ],
            hbm=(0, 1, 2, 3, 4, 8), limit=36,
        )

    def project(l, att):
        return kernel_call(
            order, functools.partial(project_body, lats, width=width), "project_%d" % l,
            scatter_shapes(size, width), (info, att, attn_out), [SM, VM, VM], (ANY,) * 4,
            scratch=[pltpu.VMEM((size, total), BF), pltpu.SemaphoreType.DMA((5,))], hbm=(0, 1, 2, 3),
        )

    def result_rows(l, first, pieces):
        keep, got, far = pieces
        spec = part_spec(0, keep.shape)
        row = lat_spec(l, 1, width)
        return kernel_call(
            order, result_body, "result_%d" % l, (sds((size, width), BF),),
            (first, scale_rows, shift_rows, keep, got, far, line(attn_out_bias)),
            [VM, row, row, spec, VM, VM, VM], (VM,),
        )[0]

    def second_grad(l, pieces, first, stat):
        keep, got, far = pieces
        spec = part_spec(0, keep.shape)
        row = lat_spec(l, 1, width)
        return kernel_call(
            order, functools.partial(second_grad_body, total_width=total, text_len=text_len), "second_grad_%d" % l,
            (sds((size, width), BF), sds((size, width), F32), sds((text_rows, width), BF), sds((8, width), F32)),
            (keep, got, far, upstream, first, stat, scale_rows, shift_rows),
            [spec, VM, VM, lat_spec(l, size, width), VM, VM, row, row], (VM, VM, VM, VM), hbm=(1,),
        )

    def gated_grad(l, blocks, act, spat):
        n = hidden // tile_cols
        col = pl.BlockSpec((1, tile_cols), lambda j: (0, j))
        wide = pl.BlockSpec((size, tile_cols), lambda j: (0, j))
        return kernel_call(
            order, functools.partial(gated_grad_body, lats, width=width, chunk=size // 3), "gated_grad_%d" % l,
            (sds((size, total), BF), sds((size, hidden), BF), sds((1, hidden), F32), sds((1, hidden), F32),
             sds((8, LANE), F32)),
            (info, *blocks, mixer_contract_weight, act, line(grn_gamma), spat),
            [SM] + [ANY] * 5 + [pl.BlockSpec((tile_cols, total), lambda j: (j, 0)), wide, col, col],
            (VM, wide, col, col, VM), grid=(n,), scratch=[pltpu.SemaphoreType.DMA((5,))],
        )

    def hidden_grad(l, gg, act, slope, spat, s1, tots, crosses, nrm):
        n = total // tile_cols
        return kernel_call(
            order, functools.partial(hidden_grad_body, l, lats, hidden_total, width=width, chunk=32),
            "hidden_grad_%d" % l,
            (sds((size, hidden), BF),) + scatter_shapes(size + EXTRA, width)
            + (sds((1, hidden), F32), sds((1, hidden), F32)),
            (info, gg, act, slope, spat, s1, line(grn_gamma), *tots, *crosses, mixer_expand_weight, nrm),
            [SM] + [VM] * 14
            + [pl.BlockSpec((tile_cols, hidden), lambda j: (j, 0)), pl.BlockSpec((size, tile_cols), lambda j: (0, j))],
            (VM, ANY, ANY, ANY, ANY, VM, VM), grid=(n,),
            scratch=[
                pltpu.VMEM((size + EXTRA, total), BF),
                pltpu.VMEM((2, size, LANE), F32),
                pltpu.SemaphoreType.DMA((5,)),
            ],
            hbm=(4,),
        )

    def conv_backward(l, pieces, conv, stat, first_grad):
        keep, got, far = pieces
        spec = part_spec(0, keep.shape)
        return kernel_call(
            order, functools.partial(conv_backward_body, l, total_width=total), "conv_backward_%d" % l,
            (sds((size, width), BF), sds((16, width), F32)),
            (info, keep, got, far, conv, stat, latents, first_grad, conv_kernel),
            [SM, spec, VM, VM, VM, VM, lat_spec(l, size, width), VM, VM], (VM, VM),
            scratch=[pltpu.VMEM((size + 2 * MARGIN, width), F32)],
        )

    half = dp // 2
    split = dp == 8
    if split:
        table = np.zeros((dp, dp), np.int32)
        for d in range(dp):
            for k in range(half):
                table[d, k] = 2 * ((d // 2) ^ k) + d % 2
                table[d, half + k] = 2 * ((d // 2) ^ k) + 1 - d % 2
        places = lax.dynamic_index_in_dim(jnp.asarray(table), lax.axis_index("dp"), 0, keepdims=False)
    else:
        places = None

    def swap_dp(v, bit):
        return lax.ppermute(v, "dp", [(i, i ^ bit) for i in range(dp)])

    def reduce_start(parts):
        if len(parts) == 1:
            return [lax.psum_scatter(parts[0], "dp", scatter_dimension=0, tiled=True)]
        send, keep = parts
        return [keep, swap_dp(send, 1)]

    def reduce_step(name, state, bit, small=None):
        if not split:
            if small is None:
                return state
            return state, (small if bit < 4 else (lax.psum(small[0], "dp"),))
        keep, got = state
        shape = keep.shape[1:] if bit == 4 else (keep.shape[0] // 2,) + keep.shape[1:]
        outs = (sds(shape, BF),) * 2
        args = (keep, got)
        if small is not None:
            args += tuple(small)
            outs += (sds(small[0].shape, F32),)
        res = kernel_call(
            order, functools.partial(combine_body, small is not None), name, outs, args, [VM] * len(args),
            (VM,) * len(outs), hbm=(1,),
        )
        state = [res[1], swap_dp(res[0], bit)]
        if small is not None:
            return state, (res[2], swap_dp(res[2], bit))
        return state

    def reduce_end(name, states, layout, shapes, small=None):
        if not split:
            outs = [jnp.zeros(s, F32) for s in shapes]
            for (part,), plan in zip(states, layout):
                for start, cols, out, offset, flip in plan:
                    block = part[:, start : start + cols].astype(F32)
                    if flip:
                        outs[out] = outs[out].at[offset : offset + cols].set(block.T)
                    else:
                        outs[out] = outs[out].at[:, offset : offset + cols].set(block)
            return outs + ([small[0]] if small is not None else [])
        args, specs = [], []
        for state in states:
            args += state
            specs += [VM] * len(state)
        outs = tuple(sds(s, F32) for s in shapes)
        if small is not None:
            args += small
            specs += [VM] * len(small)
            outs += (sds(small[0].shape, F32),)
        return kernel_call(
            order,
            functools.partial(
                finish_body, [len(state) for state in states], len(small) if small is not None else 0, layout
            ),
            name, outs, tuple(args), specs, (VM,) * len(outs),
        )

    def weights(name, lefts, tiles, cut=True, after=()):
        return weight_grads(order, name, places if cut else None, lefts, tiles, width, dp, after)

    assert lats == 2
    share = total // dp
    conv0 = conv_forward(0)
    pay10 = gather_start(conv0[0])
    conv1 = conv_forward(1)
    pay11 = gather_start(conv1[0])
    conv = (conv0, conv1)
    (far,) = hop(order, "hop_rows_0", pay10[2])
    pay10 = gather_end(pay10, far)
    ffn0 = ffn_in(0, pay10)
    tot0 = gather_small(ffn0[5])
    far, text_far, up0 = hop(order, "hop_rows_1", pay11[2], text_state[2], (upstream, 0))
    up0 = gather_start(up0)
    pay11 = gather_end(pay11, far)
    text_blocks = gather_end(text_state, text_far)
    ffn1 = ffn_in(1, pay11)
    tot1 = gather_small(ffn1[5])
    ffn, tots = (ffn0, ffn1), (tot0, tot1)
    out0 = ffn_out(0, ffn0[2], ffn0[4], tot0, up0[1:])
    gots0 = swap_halves(out0[1:4])
    text_full, text_low = text_low_rows(text_blocks, tot1[1:])
    low = gather_start(text_low)
    part0 = scatter_end("add_ffn_0", out0[4], gots0, False)
    out1 = ffn_out(1, ffn1[2], ffn1[4], tot1)
    gots1 = swap_halves(out1[1:4])
    up_far, low_far = hop(order, "hop_upstream", up0[2], low[2])
    up0 = gather_end(up0, up_far)
    text_low_blocks = gather_end(low, low_far)
    part1 = scatter_end("add_ffn_1", out1[4], gots1, False)
    gated = (out0[0], out1[0])
    mid0 = middle(0, part0)
    pay20 = gather_start(mid0[1])
    mid1 = middle(1, part1)
    pay21 = gather_start(mid1[1])
    far, up1 = hop(order, "hop_context_0", pay20[2], (upstream, 1))
    pay20 = gather_end(pay20, far)
    up1 = gather_start(up1)
    attn0 = attention(0, pay20, text_low_blocks, up0)
    gots0 = swap_halves(attn0[5:8])
    far, up_far = hop(order, "hop_context_1", pay21[2], up1[2])
    pay21 = gather_end(pay21, far)
    up1 = gather_end(up1, up_far)
    proj0 = project(0, attn0[3])
    ctx0 = scatter_end("add_ctx_0", attn0[8], gots0, True)
    attn1 = attention(1, pay21, text_low_blocks, up1)
    gots1 = swap_halves(attn1[5:8])
    attn = (attn0, attn1)
    second0 = second_grad(0, ctx0, mid0[0], attn0[1])
    pay30 = gather_start(second0[0])
    proj1 = project(1, attn1[3])
    ctx1 = scatter_end("add_ctx_1", attn1[8], gots1, True)

    lefts = [attn[l][0] for l in (0, 1)] + [attn[l][2] for l in (0, 1)]
    tiles = [[(l, attn[l][4], k * width) for l in (0, 1)] for k in range(3)]
    tiles.append([(2 + l, attn[l][3], 0) for l in (0, 1)])
    sum_a = reduce_start(weights("attn_weight_grads", lefts, tiles, False))
    (far,) = hop(order, "hop_first_0", pay30[2])
    pay30 = gather_end(pay30, far)
    second1 = second_grad(1, ctx1, mid1[0], attn1[1])
    pay31 = gather_start(second1[0])
    gg0 = gated_grad(0, pay30, ffn0[2], ffn0[4])
    cross0 = gather_small(gg0[4])
    (far,) = hop(order, "hop_first_1", pay31[2])
    pay31 = gather_end(pay31, far)
    gg1 = gated_grad(1, pay31, ffn1[2], ffn1[4])
    cross1 = gather_small(gg1[4])
    gg = (gg0, gg1)

    def hidden_of(l, cross):
        return hidden_grad(l, gg[l][1], ffn[l][2], ffn[l][3], ffn[l][4], gg[l][2], tots[l], cross, ffn[l][0])

    hid0 = hidden_of(0, cross0)
    gots0 = swap_halves(hid0[1:4])
    lefts = [gg[l][0] for l in (0, 1)] + [text_full[l] for l in (0, 1)]
    tiles = [[(l, gated[l], k) for l in (0, 1)] for k in range(0, hidden, width)]
    tiles.append([(2, second0[2], 0), (3, second1[2], 0)])
    near = (hidden // width) // 2
    sum_c0 = reduce_start(weights("contract_weight_grads_0", lefts[:2], tiles[:near], after=cross1[1:]))
    in0 = scatter_end("add_in_0", hid0[4], gots0, True)
    sum_c1 = reduce_start(weights("contract_weight_grads_1", lefts, tiles[near:]))
    hid1 = hidden_of(1, cross1)
    gots1 = swap_halves(hid1[1:4])
    hid = (hid0, hid1)
    lefts = [ffn[l][0] for l in (0, 1)]
    tiles = [[(l, hid[l][0], k) for l in (0, 1)] for k in range(0, hidden, width)]
    sum_e0 = reduce_start(weights("expand_weight_grads_0", lefts, tiles[:near]))
    in1 = scatter_end("add_in_1", hid1[4], gots1, True)
    sum_c0 = reduce_step("contract_sums_0", sum_c0, 2)
    back0 = conv_backward(0, in0, conv[0][1], ffn0[1], second0[1])
    sum_c0 = reduce_step("contract_sums_0b", sum_c0, 4)
    sum_e1 = reduce_start(weights("expand_weight_grads_1", lefts, tiles[near:]))
    back1 = conv_backward(1, in1, conv[1][1], ffn1[1], second1[1])
    sum_c1 = reduce_step("contract_sums_1", sum_c1, 2)
    r = noise_embed.shape[1]
    packed = kernel_call(
        order, functools.partial(pack_body, lats), "pack", (sds((2 * r + 40, width), F32),),
        (noise_embed.T, second0[3], second1[3], attn0[9], attn1[9], hid0[6], hid1[6], gg0[3], gg1[3],
         back0[1], back1[1], hid0[5], hid1[5]),
        [VM] * (1 + 6 * lats), (VM,),
    )[0]
    packed = (packed, swap_dp(packed, 1)) if split else (packed,)
    gots0, gots1 = swap_halves(proj0[:3]), swap_halves(proj1[:3])
    res0 = scatter_end("add_out_0", proj0[3], gots0, False)
    res1 = scatter_end("add_out_1", proj1[3], gots1, False, after=sum_c0[1:])
    sum_e0 = reduce_step("expand_sums_0", sum_e0, 2)
    sum_c1 = reduce_step("contract_sums_1b", sum_c1, 4)
    out_0 = result_rows(0, mid0[0], res0)
    out_1 = result_rows(1, mid1[0], res1)
    sum_e0 = reduce_step("expand_sums_0b", sum_e0, 4)
    sum_e1, packed = reduce_step("expand_sums_1", sum_e1, 2, packed)
    grads_a = reduce_end(
        "attn_grads", [sum_a],
        [[(k * width, width, k, 0, False) for k in range(3)] + [(3 * width, width, 3, 0, True)]],
        [(share, width)] * 3 + [(width, share)],
    )
    sum_e1, packed = reduce_step("expand_sums_1b", sum_e1, 4, packed)
    rest = hidden - near * width
    grads_c = reduce_end(
        "contract_grads", [sum_c0, sum_c1],
        [[(0, near * width, 0, 0, True)], [(0, rest, 0, near * width, True), (rest, width, 1, 0, False)]],
        [(hidden, share), (share, width)],
    )
    grads_e = reduce_end(
        "expand_grads", [sum_e0, sum_e1],
        [[(0, near * width, 0, 0, False)], [(0, rest, 0, near * width, False)]], [(share, hidden)], packed,
    )
    sums = grads_e[-1]
    base = 2 * r
    vec = base + 28
    n = hidden // width
    return (
        jnp.stack([out_0, out_1]),
        jnp.stack([back0[0], back1[0]]),
        sums[base : base + 9],
        sums[base + 9],
        grads_e[0],
        sums[base + 24 : base + 24 + n].reshape(-1),
        sums[base + 16 : base + 16 + n].reshape(-1),
        sums[base + 20 : base + 20 + n].reshape(-1),
        grads_c[0],
        sums[vec + 2],
        sums[:r],
        sums[vec],
        sums[r : 2 * r],
        sums[vec + 1],
        grads_c[1],
        sums[vec + 3],
        grads_a[0],
        sums[vec + 5],
        grads_a[1],
        grads_a[2],
        sums[vec + 6],
        grads_a[3],
        sums[vec + 4],
    )


def solution(mesh):
    rows = P("dp", None, "chan")
    weight_in = P(None, "chan")
    vec = P("chan")
    in_specs = (
        rows, P("dp", None), P("dp"), P("dp"), rows, P("dp", None), weight_in, vec, weight_in, vec, vec, vec,
        P("chan", None), vec, weight_in, vec, weight_in, vec, weight_in, vec, weight_in, vec, weight_in,
        weight_in, vec, P("chan", None), vec, rows,
    )
    out_specs = (
        rows, rows, weight_in, vec, P("dp", "chan"), vec, vec, vec, P("chan", "dp"), vec, weight_in, vec,
        weight_in, vec, P("dp", "chan"), vec, P("dp", "chan"), vec, P("dp", "chan"), P("dp", "chan"), vec,
        P("chan", "dp"), vec,
    )
    return jax.shard_map(local, mesh=mesh, in_specs=in_specs, out_specs=out_specs, check_vma=False)
```

```python
import functools

import jax
import jax.numpy as jnp
import numpy as np
from jax import lax
from jax.experimental import pallas as pl
from jax.experimental.pallas import tpu as pltpu
from jax.sharding import PartitionSpec as P

BF = jnp.bfloat16
F32 = jnp.float32
HEAD = 64
LANE = 128
EXTRA = 16
MARGIN = 40
WIDTHS = (36, 24, 18)
EPS = 1e-6

COSTS = {"gated_grad_1": 10**12}

VM = pl.BlockSpec(memory_space=pltpu.VMEM)
SM = pl.BlockSpec(memory_space=pltpu.SMEM)
ANY = pl.BlockSpec(memory_space=pl.ANY)


class Order:
    def __init__(self, ordered=True):
        self.ordered = ordered
        self.last = None
        self.pinned = []


def kernel_call(
    order, body, name, outs, args, in_specs, out_specs, grid=(1,), scratch=(), hbm=(), limit=20, after=()
):
    count = len(args)
    args = tuple(
        pltpu.with_memory_space_constraint(a, pltpu.HBM) if any(a is p for p in order.pinned) else a for a in args
    )
    outs = tuple(pltpu.HBM(o.shape, o.dtype) if i in hbm else o for i, o in enumerate(outs))
    if order.ordered:
        if order.last is not None:
            after = (order.last, *after)
        args = tuple(args) + tuple(after)
        in_specs = list(in_specs) + [ANY] * len(after)
    extra = len(args) - count

    def ordered(*refs):
        body(*refs[:count], *refs[count + extra :])

    results = pl.pallas_call(
        ordered,
        name=name,
        out_shape=outs,
        grid=grid,
        in_specs=in_specs,
        out_specs=out_specs,
        scratch_shapes=scratch,
        compiler_params=pltpu.CompilerParams(vmem_limit_bytes=limit << 20),
        cost_estimate=pl.CostEstimate(flops=COSTS.get(name, 1000), bytes_accessed=1000, transcendentals=0),
    )(*args)
    order.pinned += [results[i] for i in hbm]
    order.last = min(results, key=lambda r: r.size * r.dtype.itemsize)
    return results


def half_rows(rows):
    return (rows // 16 + 1) // 2 * 16


def hop_body(halves, *refs):
    count = len(halves)
    ins, outs, sems = refs[:count], refs[count:-1], refs[-1]
    copies = []
    for ref, half in zip(ins, halves):
        rows = ref.shape[-2]
        h = half_rows(rows) if half else rows
        for part in ((slice(0, h), slice(h, rows)) if half else (slice(0, rows),)):
            at = len(copies)
            if len(ref.shape) > len(outs[at].shape):
                source = ref.at[0]
            else:
                source = ref.at[part] if len(ref.shape) == 2 else ref.at[:, part]
            copies.append(pltpu.make_async_copy(source, outs[at], sems.at[at]))
    run_copies(copies)


def hop(order, name, *arrays, after=()):
    outs, halves, ins, specs = [], [], [], []
    for a in arrays:
        if isinstance(a, tuple):
            a, pick = a
            shape = a.shape if pick is None else a.shape[1:]
            ins.append(a)
            specs.append(
                VM if pick is None
                else pl.BlockSpec((1,) + shape, lambda *_, pick=pick, n=len(shape): (pick,) + (0,) * n)
            )
            halves.append(False)
            outs.append(sds(shape, a.dtype))
        else:
            ins.append(a)
            specs.append(VM)
            halves.append(True)
            h = half_rows(a.shape[-2])
            for rows in (h, a.shape[-2] - h):
                outs.append(sds(a.shape[:-2] + (rows, a.shape[-1]), a.dtype))
    got = list(kernel_call(
        order, functools.partial(hop_body, halves), name, tuple(outs),
        tuple(ins), specs, (ANY,) * len(outs),
        scratch=[pltpu.SemaphoreType.DMA((len(outs),))], after=after,
    ))
    return [(got.pop(0), got.pop(0)) if half else got.pop(0) for half in halves]


def sds(shape, dtype):
    return jax.ShapeDtypeStruct(shape, dtype)


def nn(a, b):
    return jnp.dot(a, b, preferred_element_type=F32)


def nt(a, b):
    return lax.dot_general(a, b, (((1,), (1,)), ((), ())), preferred_element_type=F32)


def tn(a, b):
    return lax.dot_general(a, b, (((0,), (0,)), ((), ())), preferred_element_type=F32)


def eye():
    return (
        lax.broadcasted_iota(jnp.int32, (LANE, LANE), 0)
        == lax.broadcasted_iota(jnp.int32, (LANE, LANE), 1)
    ).astype(F32)


def col_to_tile(col):
    size = col.shape[0]
    diag = eye()
    row = lax.broadcasted_iota(jnp.int32, (8, LANE), 0)
    tile = jnp.zeros((8, LANE), F32)
    for t in range(pl.cdiv(size, LANE)):
        n = min(LANE, size - t * LANE)
        line = jnp.sum(col[t * LANE : t * LANE + n] * diag[:n], axis=0, keepdims=True)
        tile = jnp.where(row == t, line, tile)
    return tile


def tile_to_col(tile, size):
    diag = eye()
    cols = []
    for t in range(pl.cdiv(size, LANE)):
        n = min(LANE, size - t * LANE)
        cols.append(jnp.sum(tile[t : t + 1] * diag[:n], axis=1, keepdims=True))
    return jnp.concatenate(cols, axis=0)


def split_stats(both):
    high = both.astype(BF)
    rest = both - high.astype(F32)
    mid = rest.astype(BF)
    low = (rest - mid.astype(F32)).astype(BF)
    return jnp.concatenate([high, mid, low], axis=1)


def join_stats(tile):
    wide = tile.astype(F32)
    return wide[:, :LANE] + wide[:, LANE : 2 * LANE] + wide[:, 2 * LANE : 3 * LANE]


def stats_tile(first, second):
    return split_stats(jnp.concatenate([col_to_tile(first), col_to_tile(second)], axis=0))


def block_copies(me, refs, dst, sems, width, base=0, first_sem=0):
    rows = refs[0].shape[0]
    h = half_rows(rows)
    plan = ((0, 0, rows), (1, 0, rows), (2, 0, rows))
    plan += ((3, 0, rows),) if len(refs) == 4 else ((3, 0, h), (3, h, rows - h))
    copies = []
    for i, (ref, (k, start, size)) in enumerate(zip(refs, plan)):
        place = pl.multiple_of((me ^ k) * width, LANE)
        target = dst.at[pl.ds(base + start, size), pl.ds(place, width)]
        copies.append(pltpu.make_async_copy(ref, target, sems.at[first_sem + i]))
    return copies


def scatter_copies(me, part, outs, sems, width):
    send, send_a, send_b, keep = outs
    rows = part.shape[0]
    h = half_rows(rows)
    plan = ((0, 0, rows, keep.at[0]), (2, 0, rows, keep.at[1]), (1, 0, rows, send), (3, 0, h, send_a), (3, h, rows - h, send_b))
    copies = []
    for i, (k, start, size, dst) in enumerate(plan):
        place = pl.multiple_of((me ^ k) * width, LANE)
        source = part.at[pl.ds(start, size), pl.ds(place, width)]
        copies.append(pltpu.make_async_copy(source, dst, sems.at[i]))
    return copies


def scatter_shapes(rows, width):
    h = half_rows(rows)
    return (
        sds((rows, width), BF), sds((h, width), BF), sds((rows - h, width), BF), sds((2, rows, width), BF)
    )


def run_copies(copies):
    for c in copies:
        c.start()
    for c in copies:
        c.wait()


def norm_rows(raw, out, stat, size, width, blocks):
    total = width * blocks
    means = []
    for b in range(blocks):
        means.append(tile_to_col(raw[size : size + 8, b * width : b * width + LANE].astype(F32), size))
    mean_sum = jnp.zeros((size, 1), F32)
    for b in range(blocks):
        part = raw[:size, b * width : (b + 1) * width].astype(F32)
        mean_sum = mean_sum + jnp.sum(part, axis=1, keepdims=True) + width * means[b]
    mean = mean_sum * (1.0 / total)
    square = jnp.zeros((size, 1), F32)
    for b in range(blocks):
        part = raw[:size, b * width : (b + 1) * width].astype(F32) + (means[b] - mean)
        square = square + jnp.sum(part * part, axis=1, keepdims=True)
    inverse = lax.rsqrt(square * (1.0 / total) + EPS)
    for b in range(blocks):
        part = raw[:size, b * width : (b + 1) * width].astype(F32) + (means[b] - mean)
        out[:size, b * width : (b + 1) * width] = (part * inverse).astype(BF)
    stat[0] = jnp.broadcast_to(mean, (size, LANE))
    stat[1] = jnp.broadcast_to(inverse, (size, LANE))


def send_rows(values, pay, size, width):
    mean = jnp.mean(values, axis=1, keepdims=True).astype(BF).astype(F32)
    pay[:size] = (values - mean).astype(BF)
    tile = col_to_tile(mean).astype(BF)
    pay[size:] = jnp.zeros((EXTRA, width), BF)
    pay[size : size + EXTRA, :LANE] = jnp.concatenate([tile, jnp.zeros((8, LANE), BF)], axis=0)


def column_masks(size, width):
    slot = lax.broadcasted_iota(jnp.int32, (size, 1), 0).astype(F32)
    col = slot - width * jnp.floor((slot + 0.5) * (1.0 / width))
    return col > 0.5, col < width - 1.5


def conv_forward_body(l, info, x_ref, taps, bias, pay, conv, pad):
    size, width = conv.shape
    slot = lax.broadcasted_iota(jnp.int32, (size, 1), 0)
    x = jnp.where(slot < info[l, 0], x_ref[...].astype(F32), 0.0)
    pad[:MARGIN] = jnp.zeros((MARGIN, width), F32)
    pad[MARGIN + size :] = jnp.zeros((MARGIN, width), F32)
    here = slice(MARGIN, MARGIN + size)
    for bucket, w in enumerate(WIDTHS):

        @pl.when(info[l, 1] == bucket)
        def _():
            not_first, not_last = column_masks(size, w)
            pad[here] = x
            left = jnp.where(not_first, pad[MARGIN - 1 : MARGIN - 1 + size], 0.0)
            right = jnp.where(not_last, pad[MARGIN + 1 : MARGIN + 1 + size], 0.0)
            total = bias[...] + left * taps[3:4] + x * taps[4:5] + right * taps[5:6]
            pad[here] = left * taps[0:1] + x * taps[1:2] + right * taps[2:3]
            total = total + pad[MARGIN - w : MARGIN - w + size]
            pad[here] = left * taps[6:7] + x * taps[7:8] + right * taps[8:9]
            conv[...] = total + pad[MARGIN + w : MARGIN + w + size]

    send_rows(conv[...], pay, size, width)


def conv_backward_body(l, info, keep, got, far, conv, stat, x_ref, first_grad, taps, out, sums, pad, total_width):
    size, width = conv.shape
    slot = lax.broadcasted_iota(jnp.int32, (size, 1), 0)
    mask = slot < info[l, 0]
    grad = keep[:size].astype(F32) + got[:size].astype(F32) + far[:size].astype(F32)
    both = join_stats(keep[size:]) + join_stats(got[size:]) + join_stats(far[size:])
    both = both * (1.0 / total_width)
    mean_grad = tile_to_col(both[:8], size)
    mean_cross = tile_to_col(both[8:], size)
    mean = stat[0][:, :1]
    inverse = stat[1][:, :1]
    normed = (conv[...] - mean) * inverse
    grad = inverse * (grad - mean_grad - normed * mean_cross)
    x = jnp.where(mask, x_ref[...].astype(F32), 0.0)
    pad[:MARGIN] = jnp.zeros((MARGIN, width), F32)
    pad[MARGIN + size :] = jnp.zeros((MARGIN, width), F32)
    here = slice(MARGIN, MARGIN + size)
    sums[...] = jnp.zeros_like(sums)
    sums[9:10] = jnp.sum(grad, axis=0, keepdims=True)
    for bucket, w in enumerate(WIDTHS):

        @pl.when(info[l, 1] == bucket)
        def _():
            not_first, not_last = column_masks(size, w)
            pad[here] = x
            left = jnp.where(not_first, pad[MARGIN - 1 : MARGIN - 1 + size], 0.0)
            right = jnp.where(not_last, pad[MARGIN + 1 : MARGIN + 1 + size], 0.0)
            pad[here] = grad
            rows = (pad[MARGIN + w : MARGIN + w + size], grad, pad[MARGIN - w : MARGIN - w + size])
            for r in range(3):
                for c, side in enumerate((left, x, right)):
                    tap = 3 * r + c
                    sums[tap : tap + 1] = jnp.sum(rows[r] * side, axis=0, keepdims=True)
            back = [sum(rows[r] * taps[3 * r + c : 3 * r + c + 1] for r in range(3)) for c in range(3)]
            pad[here] = jnp.where(not_first, back[0], 0.0)
            total = back[1] + pad[MARGIN + 1 : MARGIN + 1 + size]
            pad[here] = jnp.where(not_last, back[2], 0.0)
            total = total + pad[MARGIN - 1 : MARGIN - 1 + size]
            out[...] = (first_grad[...] + jnp.where(mask, total, 0.0)).astype(BF)


def gelu_both(h):
    t_den = 1.0 + (0.3275911 * 0.7071067811865476) * jnp.abs(h)
    t = pl.reciprocal(t_den, approx=True)
    t = t * (2.0 - t_den * t)
    bell = jnp.exp(-0.5 * h * h)
    poly = t * (
        0.127414796 + t * (-0.142248368 + t * (0.7107068705 + t * (-0.7265760135 + t * 0.5307027145)))
    )
    tail = poly * bell
    phi = jnp.where(h >= 0, 1.0 - tail, tail)
    return h * phi, phi + h * bell * 0.3989422804014327


def ffn_in_body(
    l, lats, count, info, *refs, width, chunk
):
    blocks, (w, bias, nrm, stat, act, slope, spat, total, raw, sems) = refs[:count], refs[count:]
    j = pl.program_id(0)
    size = nrm.shape[0]

    @pl.when(j == 0)
    def _():
        run_copies(block_copies(info[lats, 0], blocks, raw, sems, width))
        norm_rows(raw, nrm, stat, size, width, 4)
        total[...] = jnp.zeros_like(total)

    valid_from = size - size // 32
    cols = act.shape[1]
    square = jnp.zeros((1, cols), F32)
    for r in range(0, size, chunk):
        h = nn(nrm[r : r + chunk], w[...]) + bias[...]
        a, d = gelu_both(h)
        act[r : r + chunk] = a.astype(BF)
        slope[r : r + chunk] = d.astype(BF)
        sq = a * a
        if r + chunk > valid_from:
            slot = r + lax.broadcasted_iota(jnp.int32, (chunk, 1), 0)
            sq = jnp.where(slot < info[l, 0], sq, 0.0)
        square = square + jnp.sum(sq, axis=0, keepdims=True)
    here = jnp.sqrt(square)
    spat[...] = here
    total[...] = total[...] + jnp.sum(here)


def denominator(t0, t1, t2, t3, hidden_total):
    whole = t0[...] + t1[...] + t2[...] + t3[...]
    return whole[:1, :1] * (1.0 / hidden_total) + EPS


def ffn_out_body(lats, hidden_total, info, act, spat, t0, t1, t2, t3, gamma, beta, w, gated, s0, s1, s2, keep, part, sems, width, chunk):
    j = pl.program_id(0)
    size = act.shape[0]

    @pl.when(j == 0)
    def _():
        gain = 1.0 + gamma[...] * (spat[...] / denominator(t0, t1, t2, t3, hidden_total))
        for r in range(0, size, chunk):
            rows = slice(r, r + chunk)
            gated[rows] = (act[rows].astype(F32) * gain + beta[...]).astype(BF)

    cols = w.shape[1]
    part[:, pl.ds(pl.multiple_of(j * cols, LANE), cols)] = nn(gated[...], w[...]).astype(BF)

    @pl.when(j == pl.num_programs(0) - 1)
    def _():
        run_copies(scatter_copies(info[lats, 0], part, (s0, s1, s2, keep), sems, width))


def add_body(stats, keep, got_a, got_b, out):
    h = got_a.shape[0]
    size = out.shape[0] - (EXTRA if stats else 0)
    out[:h] = (keep[:h].astype(F32) + got_a[...].astype(F32)).astype(BF)
    out[h:size] = (keep[h:size].astype(F32) + got_b[: size - h].astype(F32)).astype(BF)
    if stats:
        out[size:] = split_stats(join_stats(keep[size:]) + join_stats(got_b[size - h :]))


def middle_body(x, keep, got, far, out_bias, scale, shift, first, pay):
    size, width = first.shape
    value = x[...].astype(F32) + (
        keep[...].astype(F32) + got[...].astype(F32) + far[...].astype(F32) + out_bias[...]
    )
    first[...] = value
    send_rows(value * (1.0 + scale[...]) + shift[...], pay, size, width)


def text_body(lats, info, b0, b1, b2, b3, w, bias, full, low, sems, width, text_len):
    lat_count, rows, _ = low.shape
    copies = []
    for l in range(lat_count):
        refs = [b.at[l] for b in (b0, b1, b2, b3)]
        copies += block_copies(info[lats, 0], refs, full.at[l], sems, width, first_sem=4 * l)
    run_copies(copies)
    row = lax.broadcasted_iota(jnp.int32, (rows, 1), 0)
    for l in range(lat_count):
        low[l] = jnp.where(row < text_len, nn(full[l], w[...]) + bias[...], 0.0).astype(BF)


def attention_body(
    l, lats, counts, info, *refs, width
):
    pays, refs = refs[: counts[0]], refs[counts[0] :]
    texts, refs = refs[: counts[1]], refs[counts[1] :]
    grads, refs = refs[: counts[2]], refs[counts[2] :]
    (
    wq, wk, wv, wo, q_bias, v_bias, ctx, stat, g_full, att, dqkv, s0, s1, s2, keep, sums,
    raw, w_all, w_out, q_s, k_s, v_s, do_s, kt_s, vt_s, att_t, dq_t, scores, part, sems,
    ) = refs
    me = info[lats, 0]
    size = att.shape[0]
    rows = ctx.shape[0]
    total = ctx.shape[1]
    text = rows - size
    factor = HEAD ** (-0.5)
    copy_in = block_copies(me, pays, raw, sems, width)
    copy_in += block_copies(me, [x.at[l] for x in texts], ctx, sems, width, base=size, first_sem=5)
    copy_w = [
        pltpu.make_async_copy(ref, w_all.at[:, k * width : (k + 1) * width], sems.at[10 + k])
        for k, ref in enumerate((wq, wk, wv))
    ]
    copy_g = [pltpu.make_async_copy(wo, w_out, sems.at[13])]
    copy_g += block_copies(me, grads, g_full, sems, width, first_sem=14)
    for c in copy_in + copy_w + copy_g:
        c.start()
    for c in copy_in:
        c.wait()
    norm_rows(raw, ctx, stat, size, width, 4)
    for c in copy_w:
        c.wait()
    q_s[...] = ((nn(ctx[:size], w_all[:, :width]) + q_bias[...]).astype(BF).astype(F32) * factor).astype(BF)
    keys = nn(ctx[...], w_all[:, width : 2 * width]).astype(BF)
    k_s[...] = keys
    kt_s[...] = keys.T
    values = (nn(ctx[...], w_all[:, 2 * width :]) + v_bias[...]).astype(BF)
    v_s[...] = values
    vt_s[...] = values.T
    for c in copy_g:
        c.wait()
    do_s[...] = nt(g_full[...], w_out[...]).astype(BF)
    tail = (size - size // 32) // 8 * 8
    key_row = tail + lax.broadcasted_iota(jnp.int32, (rows - tail, 1), 0)
    key_ok = (key_row < info[l, 0]) | ((key_row >= size) & (key_row < size + info[l, 2]))

    def pair(p, carry):
        lo = pl.multiple_of(p * LANE, LANE)
        q2 = q_s[:, pl.ds(lo, LANE)]
        k2 = k_s[:, pl.ds(lo, LANE)]
        v2 = v_s[:, pl.ds(lo, LANE)]
        do2 = do_s[:, pl.ds(lo, LANE)]
        dks, dvs = [], []
        for half in range(2):
            lanes = slice(half * HEAD, (half + 1) * HEAD)
            line = pl.ds(pl.multiple_of(p * LANE + half * HEAD, HEAD), HEAD)
            qh, kh, vh, doh = q2[:, lanes], k2[:, lanes], v2[:, lanes], do2[:, lanes]
            scores[...] = nt(kh, qh)
            scores[tail:] = jnp.where(key_ok, scores[tail:], -1e30)
            top = jnp.max(scores[...], axis=0, keepdims=True)
            expo = jnp.exp(scores[...] - top)
            probs = expo * (1.0 / jnp.sum(expo, axis=0, keepdims=True))
            low = probs.astype(BF)
            att_t[line] = nn(vt_s[line], low)
            scores[...] = probs
            grad_p = nt(vh, doh)
            dvs.append(nn(low, doh))
            dot = jnp.sum(scores[...] * grad_p, axis=0, keepdims=True)
            grad_s = (scores[...] * (grad_p - dot)).astype(BF)
            dks.append(nn(grad_s, qh))
            dq_t[line] = nn(kt_s[line], grad_s) * factor
        dqkv[:, pl.ds(pl.multiple_of(width + lo, LANE), LANE)] = jnp.concatenate(dks, axis=1).astype(BF)
        dqkv[:, pl.ds(pl.multiple_of(2 * width + lo, LANE), LANE)] = jnp.concatenate(dvs, axis=1).astype(BF)
        return carry

    lax.fori_loop(0, width // LANE, pair, 0)
    att[...] = att_t[...].astype(BF).T
    dq = dq_t[...].astype(BF).T
    dqkv[:size, :width] = dq
    dqkv[size:, :width] = jnp.zeros((text, width), BF)
    sums[...] = jnp.zeros_like(sums)
    sums[0:1] = jnp.sum(dq.astype(F32), axis=0, keepdims=True)
    sums[1:2] = jnp.sum(dqkv[:, 2 * width :].astype(F32), axis=0, keepdims=True)
    first = jnp.zeros((size, 1), F32)
    second = jnp.zeros((size, 1), F32)
    cols = 256
    for n in range(0, total, cols):
        block = nt(dqkv[...], w_all[n : n + cols]).astype(BF)
        part[:rows, n : n + cols] = block
        wide = block[:size].astype(F32)
        first = first + jnp.sum(wide, axis=1, keepdims=True)
        second = second + jnp.sum(wide * ctx[:size, n : n + cols].astype(F32), axis=1, keepdims=True)
    tile = stats_tile(first, second)
    for b in range(4):
        part[rows:, b * width : (b + 1) * width] = tile
    run_copies(scatter_copies(me, part, (s0, s1, s2, keep), sems, width))


def project_body(lats, info, *refs):
    atts, w, outs, part, sems = refs[:lats], refs[lats], refs[lats + 1 : lats + 5], refs[-2], refs[-1]
    width = atts[0].shape[1]
    cols = 512
    copies = []
    for l in range(lats):
        for n in range(0, part.shape[2], cols):
            part[l, :, n : n + cols] = nn(atts[l][...], w[:, n : n + cols]).astype(BF)
        views = [o.at[l] for o in outs[:3]] + [outs[3].at[:, l]]
        copies += scatter_copies(info[lats, 0], part.at[l], views, sems.at[l], width)
        for c in copies[-5:]:
            c.start()
    for c in copies:
        c.wait()


def add_out_body(keep, got_a, got_b, out):
    h = got_a.shape[1]
    out[:, :h] = (keep[:, :h].astype(F32) + got_a[...].astype(F32)).astype(BF)
    out[:, h:] = (keep[:, h:].astype(F32) + got_b[...].astype(F32)).astype(BF)


def result_body(lats, *refs):
    firsts, (scale, shift, keep, got, far, bias, out) = refs[:lats], refs[lats:]
    for l in range(lats):
        second = firsts[l][...] * (1.0 + scale[l]) + shift[l]
        branch = keep[l].astype(F32) + got[l].astype(F32) + far[l].astype(F32) + bias[...]
        out[l] = (second + branch).astype(BF)


def second_grad_body(keep, got, far, g_ref, first_ref, stat, scale, shift, pay, first_grad, text, sums, total_width, text_len):
    size, width = first_grad.shape
    rows = keep.shape[0] - EXTRA
    both = join_stats(keep[rows:]) + join_stats(got[rows:]) + join_stats(far[rows:])
    both = both * (1.0 / total_width)
    mean_grad = tile_to_col(both[:8], size)
    mean_cross = tile_to_col(both[8:], size)
    grad = keep[:size].astype(F32) + got[:size].astype(F32) + far[:size].astype(F32)
    first = first_ref[...]
    gain = 1.0 + scale[...]
    inverse = stat[1][:, :1]
    normed = (first * gain + shift[...] - stat[0][:, :1]) * inverse
    upstream = g_ref[...].astype(F32)
    second_grad = upstream + inverse * (grad - mean_grad - normed * mean_cross)
    scaled = second_grad * gain
    pay[...] = scaled.astype(BF)
    first_grad[...] = scaled
    row = lax.broadcasted_iota(jnp.int32, (rows - size, 1), 0)
    tail = keep[size:rows].astype(F32) + got[size:rows].astype(F32) + far[size:rows].astype(F32)
    low = jnp.where(row < text_len, tail, 0.0).astype(BF)
    text[...] = low
    sums[...] = jnp.zeros_like(sums)
    sums[0:1] = jnp.sum(second_grad * first, axis=0, keepdims=True)
    sums[1:2] = jnp.sum(second_grad, axis=0, keepdims=True)
    sums[2:3] = jnp.sum(scaled, axis=0, keepdims=True)
    sums[3:4] = jnp.sum(low.astype(F32), axis=0, keepdims=True)
    sums[4:5] = jnp.sum(upstream, axis=0, keepdims=True)


def gated_grad_body(lats, info, b0, b1, b2, b3, b4, w, act, gamma, spat, full, out, s1, s2, total, sems, width, chunk):
    j = pl.program_id(0)
    size = full.shape[0]

    @pl.when(j == 0)
    def _():
        run_copies(block_copies(info[lats, 0], (b0, b1, b2, b3, b4), full, sems, width))
        total[...] = jnp.zeros_like(total)

    cols = out.shape[1]
    cross = jnp.zeros((1, cols), F32)
    plain = jnp.zeros((1, cols), F32)
    for r in range(0, size, chunk):
        grad = nt(full[r : r + chunk], w[...])
        out[r : r + chunk] = grad.astype(BF)
        cross = cross + jnp.sum(grad * act[r : r + chunk].astype(F32), axis=0, keepdims=True)
        plain = plain + jnp.sum(grad, axis=0, keepdims=True)
    s1[...] = cross
    s2[...] = plain
    total[...] = total[...] + jnp.sum(cross * gamma[...] * spat[...])


def hidden_grad_body(
    l, lats, hidden_total, info, gg, act, slope, spat, s1, gamma, t0, t1, t2, t3, c0, c1, c2, c3, w, nrm,
    hidden, d0, d1, d2, keep, bias_sum, gamma_sum, part, acc, sems, width, chunk,
):
    j = pl.program_id(0)
    size = hidden.shape[0]

    @pl.when(j == 0)
    def _():
        den = denominator(t0, t1, t2, t3, hidden_total)
        cross = (c0[...] + c1[...] + c2[...] + c3[...])[:1, :1]
        response = spat[...] / den
        gamma_sum[...] = response * s1[...]
        grad_spat = gamma[...] * s1[...] / den - cross / (den * den) * (1.0 / hidden_total)
        gain = gamma[...] * response + 1.0
        pull = grad_spat / spat[...]
        total = jnp.zeros_like(bias_sum[...])
        for r in range(0, size, chunk):
            rows = slice(r, r + chunk)
            slot = r + lax.broadcasted_iota(jnp.int32, (chunk, 1), 0)
            active = jnp.where(slot < info[l, 0], act[rows].astype(F32), 0.0)
            grad = gg[rows].astype(F32) * gain + pull * active
            low = (grad * slope[rows].astype(F32)).astype(BF)
            hidden[rows] = low
            total = total + jnp.sum(low.astype(F32), axis=0, keepdims=True)
        bias_sum[...] = total
        acc[...] = jnp.zeros_like(acc)

    cols = w.shape[0]
    block = nt(hidden[...], w[...]).astype(BF)
    part[:size, pl.ds(pl.multiple_of(j * cols, LANE), cols)] = block
    wide = block.astype(F32)
    acc[0] = acc[0] + jnp.sum(wide, axis=1, keepdims=True)
    acc[1] = acc[1] + jnp.sum(wide * nrm[...].astype(F32), axis=1, keepdims=True)

    @pl.when(j == pl.num_programs(0) - 1)
    def _():
        tile = stats_tile(acc[0][:, :1], acc[1][:, :1])
        for b in range(4):
            part[size:, b * width : (b + 1) * width] = tile
        run_copies(scatter_copies(info[lats, 0], part, (d0, d1, d2, keep), sems, width))


def weight_grad_body(sets, split, width, dp, *refs):
    if split:
        places, refs = refs[0], refs[1:]
    count = sum(n for n, _, _ in sets)
    lefts, rights, refs = refs[:count], refs[count : 2 * count], refs[2 * count :]
    outs, refs = refs[: 2 if split else 1], refs[2 if split else 1 :]
    bufs, (stage, sems) = refs[:-2], refs[-2:]
    parts = width // (2 * (width // dp)) if split else 4
    chunk = width // parts
    share = width // dp
    used = 0
    coming = []
    at = 0
    for i, (n, start, cols) in enumerate(sets):
        lbuf, rbuf = bufs[2 * i], bufs[2 * i + 1]
        row = 0
        firsts, chunks = [], [[] for _ in range(parts)]
        for k in range(at, at + n):
            rows = lefts[k].shape[0]
            here = pl.ds(row, rows)
            firsts.append(
                pltpu.make_async_copy(rights[k].at[:, pl.ds(start, cols)], rbuf.at[here], sems.at[used])
            )
            used += 1
            for c in range(parts):
                lanes = pl.ds(c * chunk, chunk)
                chunks[c].append(
                    pltpu.make_async_copy(lefts[k].at[:, lanes], lbuf.at[here, lanes], sems.at[used])
                )
                used += 1
            row += rows
        coming.append((firsts, chunks))
        at += n
    for firsts, _ in coming:
        for c in firsts:
            c.start()
    for c in range(parts):
        for _, chunks in coming:
            for copy in chunks[c]:
                copy.start()
    leaving = []
    for c in range(parts):
        off = 0
        for i, (n, start, cols) in enumerate(sets):
            firsts, chunks = coming[i]
            for copy in (firsts if c == 0 else []) + chunks[c]:
                copy.wait()
            block = tn(bufs[2 * i][:, c * chunk : (c + 1) * chunk], bufs[2 * i + 1][...]).astype(BF)
            if split:
                near, far = block[:share], block[share:]
                flip = places[1] == 1
                stage[0, c, :, off : off + cols] = jnp.where(flip, near, far)
                stage[1, c, :, off : off + cols] = jnp.where(flip, far, near)
            else:
                stage[c * chunk : (c + 1) * chunk, off : off + cols] = block
            off += cols
        if split:
            for k in range(2):
                leaving.append(
                    pltpu.make_async_copy(stage.at[k, c], outs[k].at[places[0] ^ c], sems.at[used])
                )
                used += 1
        else:
            rows = pl.ds(c * chunk, chunk)
            leaving.append(pltpu.make_async_copy(stage.at[rows], outs[0].at[rows], sems.at[used]))
            used += 1
        for copy in leaving[-2 if split else -1 :]:
            copy.start()
    for copy in leaving:
        copy.wait()


def weight_grads(order, name, places, sets, dp, after=()):
    split = places is not None
    lefts = [l for pairs, _, _ in sets for l, _ in pairs]
    rights = [r for pairs, _, _ in sets for _, r in pairs]
    width = lefts[0].shape[1]
    wide = sum(cols for _, _, cols in sets)
    scratch = []
    for pairs, _, cols in sets:
        depth = sum(l.shape[0] for l, _ in pairs)
        scratch += [pltpu.VMEM((depth, width), BF), pltpu.VMEM((depth, cols), BF)]
    share = width // dp
    if split:
        outs = (sds((dp // 2, share, wide), BF),) * 2
        scratch.append(pltpu.VMEM((2, dp // 2, share, wide), BF))
    else:
        outs = (sds((width, wide), BF),)
        scratch.append(pltpu.VMEM((width, wide), BF))
    scratch.append(pltpu.SemaphoreType.DMA((5 * len(lefts) + 8,)))
    plan = [(len(pairs), start, cols) for pairs, start, cols in sets]
    args = ((places,) if split else ()) + (*lefts, *rights)
    return kernel_call(
        order, functools.partial(weight_grad_body, plan, split, width, dp), name, outs, args,
        ([SM] if split else []) + [ANY] * (2 * len(lefts)), (ANY,) * len(outs), scratch=scratch,
        hbm=(1,) if split else (0,), limit=40, after=after,
    )


SUMMED = 32


def join_small(mine, near, out):
    out[:SUMMED] = mine[:SUMMED] + near[:SUMMED]
    rest = mine.shape[0] - SUMMED
    out[SUMMED : SUMMED + rest] = mine[SUMMED:]
    out[SUMMED + rest :] = near[SUMMED:]


def combine_body(small, keep, got, *refs):
    if small:
        mine, near, *outs, whole = refs
        join_small(mine, near, whole)
    else:
        outs = refs
    count = keep.shape[0]
    for k in range(count):
        total = (keep[k].astype(F32) + got[k].astype(F32)).astype(BF)
        if count == 2:
            outs[1 - k][...] = total
        else:
            outs[1 - k % 2][k // 2] = total


def finish_body(counts, small, layout, *refs):
    chunks = []
    at = 0
    for n in counts:
        chunks.append(refs[at : at + n])
        at += n
    extra = refs[at : at + small]
    outs = refs[at + small :]
    for ins, plan in zip(chunks, layout):
        for start, cols, out, offset, flip in plan:
            lanes = slice(start, start + cols)
            total = 0.0
            for ref in ins:
                total = total + ref[:, lanes].astype(F32)
            if flip:
                outs[out][offset : offset + cols] = total.T
            else:
                outs[out][:, offset : offset + cols] = total
    if small:
        *outs, whole, scale, shift = outs
        join_small(*extra, whole)
        rows = whole.shape[0] - SUMMED
        r = scale.shape[0]
        lines = [whole[SUMMED + b : SUMMED + b + 8] for b in range(0, rows, 8)]
        noise = jnp.concatenate([x[4:6, :r] for x in lines], axis=0)
        for k, out in enumerate((scale, shift)):
            values = jnp.concatenate([x[2 * k : 2 * k + 2] for x in lines], axis=0)
            out[...] = lax.dot_general(
                noise, values, (((0,), (0,)), ((), ())), precision=lax.Precision.HIGHEST, preferred_element_type=F32
            )


def pack_body(lat_count, noise, *refs):
    second, attn, gam, bet, conv, hid = (refs[k * lat_count : (k + 1) * lat_count] for k in range(6))
    out = refs[-1]
    width = out.shape[1]
    out[:16] = sum(c[...] for c in conv)
    out[24:] = jnp.zeros((out.shape[0] - 24, width), F32)
    for k, group in enumerate((gam, bet, hid)):
        whole = sum(g[...] for g in group)
        for b in range(whole.shape[1] // width):
            at = 12 + 4 * k + b
            out[at : at + 1] = whole[:, b * width : (b + 1) * width]
    for i in range(5):
        out[24 + i : 25 + i] = sum(second[l][i : i + 1] for l in range(lat_count))
    for i in range(2):
        out[29 + i : 30 + i] = sum(attn[l][i : i + 1] for l in range(lat_count))
    for l in range(lat_count):
        out[SUMMED + l : SUMMED + l + 1] = second[l][0:1]
        out[SUMMED + 2 + l : SUMMED + 3 + l] = second[l][1:2]
        out[SUMMED + 4 + l : SUMMED + 5 + l, : noise.shape[1]] = noise[l : l + 1]


def local(
    latents, valid_mask, bucket_ids, text_count, text_tokens, noise_embed, conv_kernel, conv_bias,
    mixer_expand_weight, ffn_in_bias, grn_gamma, grn_beta, mixer_contract_weight, ffn_out_bias,
    scale_weight, scale_bias, shift_weight, shift_bias, text_weight, text_bias, query_weight, query_bias,
    key_weight, value_weight, value_bias, attn_out, attn_out_bias, upstream,
):
    lats, size, width = latents.shape
    groups = lax.axis_size("chan")
    dp = lax.axis_size("dp")
    total = width * groups
    hidden = mixer_expand_weight.shape[1]
    hidden_total = hidden * groups
    text_len = text_tokens.shape[1]
    text_rows = pl.cdiv(text_len, 16) * 16
    rows = size + text_rows
    highest = lax.Precision.HIGHEST
    me = lax.axis_index("chan")
    order = Order()
    order.pinned += [
        mixer_expand_weight, mixer_contract_weight, text_weight, query_weight, key_weight, value_weight, attn_out,
        latents, upstream,
    ]

    def xswap(v):
        return lax.ppermute(v, "chan", [(i, i ^ 2) for i in range(groups)])

    def cswap(v):
        return lax.ppermute(v, "chan", [(i, i ^ 1) for i in range(groups)])

    def gather_start(v):
        return v, cswap(v), xswap(v)

    def gather_end(state, halves):
        return (*state, *(cswap(h) for h in halves))

    def gather_small(v):
        return v, cswap(v), xswap(v), lax.ppermute(v, "chan", [(i, i ^ 3) for i in range(groups)])

    def line(v):
        return v.reshape(1, -1)

    info = jnp.stack(
        [jnp.sum(valid_mask, axis=1), bucket_ids, text_count, jnp.zeros_like(bucket_ids)], axis=1
    )
    info = jnp.concatenate([info, jnp.full((1, 4), me, jnp.int32)], axis=0).astype(jnp.int32)

    def lat_spec(l, *shape):
        return pl.BlockSpec((None,) + shape, lambda *_: (l,) + (0,) * len(shape))

    def part_spec(k, shape):
        return pl.BlockSpec((None,) + tuple(shape[1:]), lambda *_: (k, 0, 0))

    text_act = jax.nn.silu(text_tokens.astype(F32)).astype(BF)
    text_act = jnp.pad(text_act, ((0, 0), (0, text_rows - text_len), (0, 0)))

    def conv_forward(l, after=()):
        return kernel_call(
            order, functools.partial(conv_forward_body, l), "conv_forward_%d" % l,
            (sds((size + EXTRA, width), BF), sds((size, width), F32)),
            (info, latents, conv_kernel, line(conv_bias)),
            [SM, lat_spec(l, size, width), VM, VM], (VM, VM),
            scratch=[pltpu.VMEM((size + 2 * MARGIN, width), F32)], hbm=(1,), after=after,
        )

    tile_cols = 256

    def ffn_in(l, blocks):
        n = hidden // tile_cols
        col = pl.BlockSpec((1, tile_cols), lambda j: (0, j))
        wide = pl.BlockSpec((size, tile_cols), lambda j: (0, j))
        return kernel_call(
            order, functools.partial(ffn_in_body, l, lats, len(blocks), width=width, chunk=size // 3), "ffn_in_%d" % l,
            (sds((size, total), BF), sds((2, size, LANE), F32), sds((size, hidden), BF),
             sds((size, hidden), BF), sds((1, hidden), F32), sds((8, LANE), F32)),
            (info, *blocks, mixer_expand_weight, line(ffn_in_bias)),
            [SM] + [ANY] * len(blocks) + [pl.BlockSpec((total, tile_cols), lambda j: (0, j)), col],
            (VM, VM, wide, wide, col, VM), grid=(n,),
            scratch=[pltpu.VMEM((size + EXTRA, total), BF), pltpu.SemaphoreType.DMA((5,))], hbm=(0, 1, 3),
        )

    def ffn_out(l, act, spat, tots, after=()):
        n = total // tile_cols
        return kernel_call(
            order, functools.partial(ffn_out_body, lats, hidden_total, width=width, chunk=32), "ffn_out_%d" % l,
            (sds((size, hidden), BF),) + scatter_shapes(size, width),
            (info, act, spat, *tots, line(grn_gamma), line(grn_beta), mixer_contract_weight),
            [SM] + [VM] * 8 + [pl.BlockSpec((hidden, tile_cols), lambda j: (0, j))],
            (VM,) + (ANY,) * 4, grid=(n,),
            scratch=[pltpu.VMEM((size, total), BF), pltpu.SemaphoreType.DMA((5,))], hbm=(0, 4), after=after,
        )

    def swap_halves(outs):
        return tuple(cswap(o) for o in outs)

    def scatter_end(name, keep, gots, stats, after=()):
        got, got_a, got_b = gots
        half = kernel_call(
            order, functools.partial(add_body, stats), name, (sds(keep.shape[1:], BF),), (keep, got_a, got_b),
            [part_spec(1, keep.shape), VM, VM], (VM,), after=after,
        )[0]
        return keep, got, xswap(half)

    scale_rows = (jnp.dot(noise_embed, scale_weight, precision=highest) + scale_bias)[:, None]
    shift_rows = (jnp.dot(noise_embed, shift_weight, precision=highest) + shift_bias)[:, None]

    def middle(l, pieces, after=()):
        keep, got, far = pieces
        spec = part_spec(0, keep.shape)
        row = lat_spec(l, 1, width)
        return kernel_call(
            order, middle_body, "middle_%d" % l,
            (sds((size, width), F32), sds((size + EXTRA, width), BF)),
            (latents, keep, got, far, line(ffn_out_bias), scale_rows, shift_rows),
            [lat_spec(l, size, width), spec, VM, VM, VM, row, row], (VM, VM), hbm=(0,), after=after,
        )

    def text_low_rows(blocks, after):
        return kernel_call(
            order, functools.partial(text_body, lats, width=width, text_len=text_len), "text_rows",
            (sds((lats, text_rows, total), BF), sds((lats, text_rows, width), BF)),
            (info, *blocks, text_weight, line(text_bias)),
            [SM] + [ANY] * 4 + [VM, VM], (VM, VM), scratch=[pltpu.SemaphoreType.DMA((4 * lats,))], hbm=(0,), after=after,
        )

    def attention(l, blocks, texts, grads):
        return kernel_call(
            order,
            functools.partial(attention_body, l, lats, (len(blocks), len(texts), len(grads)), width=width),
            "attention_%d" % l,
            (sds((rows, total), BF), sds((2, size, LANE), F32), sds((size, total), BF),
             sds((size, width), BF), sds((rows, 3 * width), BF))
            + scatter_shapes(rows + EXTRA, width) + (sds((8, width), F32),),
            (info, *blocks, *texts, *grads, query_weight, key_weight, value_weight, attn_out,
             line(query_bias), line(value_bias)),
            [SM] + [ANY] * (len(blocks) + len(texts) + len(grads) + 4) + [VM, VM],
            (VM, VM, VM, VM, VM, ANY, ANY, ANY, ANY, VM),
            scratch=[
                pltpu.VMEM((size + EXTRA, total), BF),
                pltpu.VMEM((total, 3 * width), BF),
                pltpu.VMEM((width, total), BF),
                pltpu.VMEM((size, width), BF),
                pltpu.VMEM((rows, width), BF),
                pltpu.VMEM((rows, width), BF),
                pltpu.VMEM((size, width), BF),
                pltpu.VMEM((width, rows), BF),
                pltpu.VMEM((width, rows), BF),
                pltpu.VMEM((width, size), F32),
                pltpu.VMEM((width, size), F32),
                pltpu.VMEM((rows, size), F32),
                pltpu.VMEM((rows + EXTRA, total), BF),
                pltpu.SemaphoreType.DMA((19,)),
            ],
            hbm=(0, 1, 2, 3, 4, 8, 9), limit=36,
        )

    def project(atts):
        h = half_rows(size)
        return kernel_call(
            order, functools.partial(project_body, lats), "project",
            tuple(sds((lats, r, width), BF) for r in (size, h, size - h)) + (sds((2, lats, size, width), BF),),
            (info, *atts, attn_out), [SM] + [VM] * (lats + 1), (ANY,) * 4,
            scratch=[pltpu.VMEM((lats, size, total), BF), pltpu.SemaphoreType.DMA((lats, 5))], hbm=(3,),
        )

    def project_end(keep, gots):
        got, got_a, got_b = gots
        half = kernel_call(
            order, add_out_body, "add_out", (sds(keep.shape[1:], BF),), (keep, got_a, got_b),
            [pl.BlockSpec((None,) + keep.shape[1:], lambda *_: (1, 0, 0, 0)), VM, VM], (VM,), after=(got,),
        )[0]
        return keep, got, xswap(half)

    def result_rows(firsts, pieces):
        keep, got, far = pieces
        return kernel_call(
            order, functools.partial(result_body, lats), "result", (sds((lats, size, width), BF),),
            (*firsts, scale_rows, shift_rows, keep, got, far, line(attn_out_bias)),
            [VM] * (lats + 2) + [pl.BlockSpec((None,) + keep.shape[1:], lambda *_: (0, 0, 0, 0)), VM, VM, VM], (VM,),
        )[0]

    def second_grad(l, pieces, first, stat):
        keep, got, far = pieces
        spec = part_spec(0, keep.shape)
        row = lat_spec(l, 1, width)
        return kernel_call(
            order, functools.partial(second_grad_body, total_width=total, text_len=text_len), "second_grad_%d" % l,
            (sds((size, width), BF), sds((size, width), F32), sds((text_rows, width), BF), sds((8, width), F32)),
            (keep, got, far, upstream, first, stat, scale_rows, shift_rows),
            [spec, VM, VM, lat_spec(l, size, width), VM, VM, row, row], (VM, VM, VM, VM), hbm=(1, 3),
        )

    def gated_grad(l, blocks, act, spat):
        n = hidden // tile_cols
        col = pl.BlockSpec((1, tile_cols), lambda j: (0, j))
        wide = pl.BlockSpec((size, tile_cols), lambda j: (0, j))
        return kernel_call(
            order, functools.partial(gated_grad_body, lats, width=width, chunk=size // 3), "gated_grad_%d" % l,
            (sds((size, total), BF), sds((size, hidden), BF), sds((1, hidden), F32), sds((1, hidden), F32),
             sds((8, LANE), F32)),
            (info, *blocks, mixer_contract_weight, act, line(grn_gamma), spat),
            [SM] + [ANY] * 5 + [pl.BlockSpec((tile_cols, total), lambda j: (j, 0)), wide, col, col],
            (VM, wide, col, col, VM), grid=(n,), scratch=[pltpu.SemaphoreType.DMA((5,))], hbm=(0, 3),
        )

    def hidden_grad(l, gg, act, slope, spat, s1, tots, crosses, nrm):
        n = total // tile_cols
        return kernel_call(
            order, functools.partial(hidden_grad_body, l, lats, hidden_total, width=width, chunk=32),
            "hidden_grad_%d" % l,
            (sds((size, hidden), BF),) + scatter_shapes(size + EXTRA, width)
            + (sds((1, hidden), F32), sds((1, hidden), F32)),
            (info, gg, act, slope, spat, s1, line(grn_gamma), *tots, *crosses, mixer_expand_weight, nrm),
            [SM] + [VM] * 14
            + [pl.BlockSpec((tile_cols, hidden), lambda j: (j, 0)), pl.BlockSpec((size, tile_cols), lambda j: (0, j))],
            (VM, ANY, ANY, ANY, ANY, VM, VM), grid=(n,),
            scratch=[
                pltpu.VMEM((size + EXTRA, total), BF),
                pltpu.VMEM((2, size, LANE), F32),
                pltpu.SemaphoreType.DMA((5,)),
            ],
            hbm=(0, 4, 5, 6),
        )

    def conv_backward(l, pieces, conv, stat, first_grad):
        keep, got, far = pieces
        spec = part_spec(0, keep.shape)
        return kernel_call(
            order, functools.partial(conv_backward_body, l, total_width=total), "conv_backward_%d" % l,
            (sds((size, width), BF), sds((16, width), F32)),
            (info, keep, got, far, conv, stat, latents, first_grad, conv_kernel),
            [SM, spec, VM, VM, VM, VM, lat_spec(l, size, width), VM, VM], (VM, VM),
            scratch=[pltpu.VMEM((size + 2 * MARGIN, width), F32)], hbm=(1,),
        )

    half = dp // 2
    split = dp == 8
    if split:
        here = lax.axis_index("dp")
        places = jnp.stack([here // 2, here % 2]).astype(jnp.int32)
    else:
        places = None

    def swap_dp(v, bit):
        return lax.ppermute(v, "dp", [(i, i ^ bit) for i in range(dp)])

    def reduce_start(parts):
        if len(parts) == 1:
            return [lax.psum_scatter(parts[0], "dp", scatter_dimension=0, tiled=True)]
        send, keep = parts
        return [keep, swap_dp(send, 1)]

    def reduce_step(name, state, bit, small=None, after=()):
        if not split:
            return state if small is None else (state, small)
        keep, got = state
        shape = keep.shape[1:] if bit == 4 else (keep.shape[0] // 2,) + keep.shape[1:]
        outs = (sds(shape, BF),) * 2
        args = (keep, got)
        if small is not None:
            args += tuple(small)
            outs += (sds((2 * small[0].shape[0] - SUMMED, width), F32),)
        res = kernel_call(
            order, functools.partial(combine_body, small is not None), name, outs, args, [VM] * len(args),
            (VM,) * len(outs), hbm=(1,), after=after,
        )
        state = [res[1], swap_dp(res[0], bit)]
        if small is not None:
            return state, (res[2], swap_dp(res[2], bit))
        return state

    def reduce_end(name, states, layout, shapes, small=None):
        if not split:
            outs = [jnp.zeros(s, F32) for s in shapes]
            for (part,), plan in zip(states, layout):
                for start, cols, out, offset, flip in plan:
                    block = part[:, start : start + cols].astype(F32)
                    if flip:
                        outs[out] = outs[out].at[offset : offset + cols].set(block.T)
                    else:
                        outs[out] = outs[out].at[:, offset : offset + cols].set(block)
            if small is not None:
                rows = small[0]
                outs.append(lax.psum(rows[:SUMMED], "dp"))
                noise = rows[SUMMED + 4 : SUMMED + 6, : noise_embed.shape[1]].T
                for k in range(2):
                    values = rows[SUMMED + 2 * k : SUMMED + 2 * k + 2]
                    outs.append(lax.psum(jnp.dot(noise, values, precision=highest), "dp"))
            return outs
        args, specs = [], []
        for state in states:
            args += state
            specs += [VM] * len(state)
        outs = tuple(sds(s, F32) for s in shapes)
        if small is not None:
            args += small
            specs += [VM] * len(small)
            outs += (sds((2 * small[0].shape[0] - SUMMED, width), F32),)
            outs += (sds((noise_embed.shape[1], width), F32),) * 2
        return kernel_call(
            order,
            functools.partial(
                finish_body, [len(state) for state in states], len(small) if small is not None else 0, layout
            ),
            name, outs, tuple(args), specs, (VM,) * len(outs),
        )

    def weights(name, sets, cut=True, after=()):
        return weight_grads(order, name, places if cut else None, sets, dp, after)

    assert lats == 2
    share = total // dp
    text_blocks = gather_small(text_act)
    conv0 = conv_forward(0, text_blocks[1:])
    pay10 = gather_start(conv0[0])
    conv1 = conv_forward(1)
    pay11 = gather_start(conv1[0])
    conv = (conv0, conv1)
    text_full, text_low = text_low_rows(text_blocks, ())
    text_low_blocks = gather_small(text_low)
    (far,) = hop(order, "hop_rows_0", pay10[2])
    pay10 = gather_end(pay10, far)
    ffn0 = ffn_in(0, pay10)
    tot0 = gather_small(ffn0[5])
    far, up0 = hop(order, "hop_rows_1", pay11[2], (upstream, 0), after=text_low_blocks[1:])
    pay11 = gather_end(pay11, far)
    up0 = gather_start(up0)
    ffn1 = ffn_in(1, pay11)
    tot1 = gather_small(ffn1[5])
    ffn, tots = (ffn0, ffn1), (tot0, tot1)
    out0 = ffn_out(0, ffn0[2], ffn0[4], tot0, up0[1:])
    gots0 = swap_halves(out0[1:4])
    part0 = scatter_end("add_ffn_0", out0[4], gots0, False, tot1[1:])
    out1 = ffn_out(1, ffn1[2], ffn1[4], tot1)
    gots1 = swap_halves(out1[1:4])
    (up_far,) = hop(order, "hop_upstream", up0[2])
    up0 = gather_end(up0, up_far)
    part1 = scatter_end("add_ffn_1", out1[4], gots1, False)
    gated = (out0[0], out1[0])
    mid0 = middle(0, part0)
    pay20 = gather_start(mid0[1])
    mid1 = middle(1, part1, up0[3:])
    pay21 = gather_start(mid1[1])
    far, up1 = hop(order, "hop_context_0", pay20[2], (upstream, 1))
    pay20 = gather_end(pay20, far)
    up1 = gather_start(up1)
    attn0 = attention(0, pay20, text_low_blocks, up0)
    gots0 = swap_halves(attn0[5:8])
    far, up_far = hop(order, "hop_context_1", pay21[2], up1[2])
    pay21 = gather_end(pay21, far)
    up1 = gather_end(up1, up_far)
    ctx0 = scatter_end("add_ctx_0", attn0[8], gots0, True)
    attn1 = attention(1, pay21, text_low_blocks, up1)
    gots1 = swap_halves(attn1[5:8])
    attn = (attn0, attn1)
    second0 = second_grad(0, ctx0, mid0[0], attn0[1])
    pay30 = gather_start(second0[0])
    proj = project([attn0[3], attn1[3]])
    outs = swap_halves(proj[:3])
    ctx1 = scatter_end("add_ctx_1", attn1[8], gots1, True)
    sets = [
        ([(attn[l][0], attn[l][4]) for l in (0, 1)], 0, 3 * width),
        ([(attn[l][2], attn[l][3]) for l in (0, 1)], 0, width),
    ]
    sum_a = reduce_start(weights("attn_weight_grads", sets, False))
    second1 = second_grad(1, ctx1, mid1[0], attn1[1])
    pay31 = gather_start(second1[0])
    (far,) = hop(order, "hop_first_0", pay30[2], after=pay30[1:2])
    pay30 = gather_end(pay30, far)
    gg0 = gated_grad(0, pay30, ffn0[2], ffn0[4])
    cross0 = gather_small(gg0[4])
    (far,) = hop(order, "hop_first_1", pay31[2], after=pay31[1:2])
    pay31 = gather_end(pay31, far)
    out_parts = project_end(proj[3], outs)
    gg1 = gated_grad(1, pay31, ffn1[2], ffn1[4])
    cross1 = gather_small(gg1[4])
    gg = (gg0, gg1)

    def hidden_of(l, cross):
        return hidden_grad(l, gg[l][1], ffn[l][2], ffn[l][3], ffn[l][4], gg[l][2], tots[l], cross, ffn[l][0])

    hid0 = hidden_of(0, cross0)
    gots0 = swap_halves(hid0[1:4])
    near = hidden // 2
    pairs = [(gg[l][0], gated[l]) for l in (0, 1)]
    sum_c0 = reduce_start(weights("contract_weight_grads_0", [(pairs, 0, near)], after=cross1[1:]))
    in0 = scatter_end("add_in_0", hid0[4], gots0, True)
    texts = [(text_full[0], second0[2]), (text_full[1], second1[2])]
    sum_c1 = reduce_start(weights("contract_weight_grads_1", [(pairs, near, hidden - near), (texts, 0, width)]))
    hid1 = hidden_of(1, cross1)
    gots1 = swap_halves(hid1[1:4])
    hid = (hid0, hid1)
    pairs = [(ffn[l][0], hid[l][0]) for l in (0, 1)]
    sum_e0 = reduce_start(weights("expand_weight_grads_0", [(pairs, 0, near)]))
    in1 = scatter_end("add_in_1", hid1[4], gots1, True)
    back0 = conv_backward(0, in0, conv[0][1], ffn0[1], second0[1])
    sum_c0 = reduce_step("contract_sums_0", sum_c0, 2)
    sum_e1 = reduce_start(weights("expand_weight_grads_1", [(pairs, near, hidden - near)]))
    back1 = conv_backward(1, in1, conv[1][1], ffn1[1], second1[1])
    sum_c0 = reduce_step("contract_sums_0b", sum_c0, 4)
    sum_c1 = reduce_step("contract_sums_1", sum_c1, 2)
    packed = kernel_call(
        order, functools.partial(pack_body, lats), "pack", (sds((SUMMED + 8, width), F32),),
        (noise_embed, second0[3], second1[3], attn0[9], attn1[9], hid0[6], hid1[6], gg0[3], gg1[3],
         back0[1], back1[1], hid0[5], hid1[5]),
        [VM] * (1 + 6 * lats), (VM,),
    )[0]
    packed = (packed, swap_dp(packed, 1)) if split else (packed,)
    sum_e0 = reduce_step("expand_sums_0", sum_e0, 2)
    sum_c1 = reduce_step("contract_sums_1b", sum_c1, 4, after=sum_c0[1:])
    grads_a = reduce_end(
        "attn_grads", [sum_a],
        [[(k * width, width, k, 0, False) for k in range(3)] + [(3 * width, width, 3, 0, True)]],
        [(share, width)] * 3 + [(width, share)],
    )
    sum_e1, packed = reduce_step("expand_sums_1", sum_e1, 2, packed)
    sum_e0 = reduce_step("expand_sums_0b", sum_e0, 4)
    result = result_rows([mid0[0], mid1[0]], out_parts)
    sum_e1, packed = reduce_step("expand_sums_1b", sum_e1, 4, packed, after=sum_c1[1:])
    rest = hidden - near
    grads_c = reduce_end(
        "contract_grads", [sum_c0, sum_c1],
        [[(0, near, 0, 0, True)], [(0, rest, 0, near, True), (rest, width, 1, 0, False)]],
        [(hidden, share), (share, width)],
    )
    grads_e = reduce_end(
        "expand_grads", [sum_e0, sum_e1],
        [[(0, near, 0, 0, False)], [(0, rest, 0, near, False)]], [(share, hidden)], packed,
    )
    sums = grads_e[1]
    n = hidden // width
    return (
        result,
        jnp.stack([back0[0], back1[0]]),
        sums[:9],
        sums[9],
        grads_e[0],
        sums[20 : 20 + n].reshape(-1),
        sums[12 : 12 + n].reshape(-1),
        sums[16 : 16 + n].reshape(-1),
        grads_c[0],
        sums[26],
        grads_e[2],
        sums[24],
        grads_e[3],
        sums[25],
        grads_c[1],
        sums[27],
        grads_a[0],
        sums[29],
        grads_a[1],
        grads_a[2],
        sums[30],
        grads_a[3],
        sums[28],
    )


def solution(mesh):
    rows = P("dp", None, "chan")
    weight_in = P(None, "chan")
    vec = P("chan")
    in_specs = (
        rows, P("dp", None), P("dp"), P("dp"), rows, P("dp", None), weight_in, vec, weight_in, vec, vec, vec,
        P("chan", None), vec, weight_in, vec, weight_in, vec, weight_in, vec, weight_in, vec, weight_in,
        weight_in, vec, P("chan", None), vec, rows,
    )
    out_specs = (
        rows, rows, weight_in, vec, P("dp", "chan"), vec, vec, vec, P("chan", "dp"), vec, weight_in, vec,
        weight_in, vec, P("dp", "chan"), vec, P("dp", "chan"), vec, P("dp", "chan"), P("dp", "chan"), vec,
        P("chan", "dp"), vec,
    )
    return jax.shard_map(local, mesh=mesh, in_specs=in_specs, out_specs=out_specs, check_vma=False)
```

```python
import functools

import jax
import jax.numpy as jnp
import numpy as np
from jax import lax
from jax.experimental import pallas as pl
from jax.experimental.pallas import tpu as pltpu
from jax.sharding import PartitionSpec as P

BF = jnp.bfloat16
F32 = jnp.float32
HEAD = 64
LANE = 128
EXTRA = 16
MARGIN = 40
WIDTHS = (36, 24, 18)
EPS = 1e-6

COSTS = {}

VM = pl.BlockSpec(memory_space=pltpu.VMEM)
SM = pl.BlockSpec(memory_space=pltpu.SMEM)
ANY = pl.BlockSpec(memory_space=pl.ANY)


class Order:
    def __init__(self, ordered=True):
        self.ordered = ordered
        self.last = None
        self.pinned = []


def kernel_call(
    order, body, name, outs, args, in_specs, out_specs, grid=(1,), scratch=(), hbm=(), limit=28, after=(), aliases=None
):
    count = len(args)
    args = tuple(
        pltpu.with_memory_space_constraint(a, pltpu.HBM) if any(a is p for p in order.pinned) else a for a in args
    )
    outs = tuple(pltpu.HBM(o.shape, o.dtype) if i in hbm else o for i, o in enumerate(outs))
    if order.ordered:
        if order.last is not None:
            after = (order.last, *after)
        args = tuple(args) + tuple(after)
        in_specs = list(in_specs) + [ANY] * len(after)
    extra = len(args) - count

    def ordered(*refs):
        body(*refs[:count], *refs[count + extra :])

    results = pl.pallas_call(
        ordered,
        name=name,
        out_shape=outs,
        grid=grid,
        in_specs=in_specs,
        out_specs=out_specs,
        scratch_shapes=scratch,
        input_output_aliases=aliases or {},
        compiler_params=pltpu.CompilerParams(vmem_limit_bytes=limit << 20),
        cost_estimate=pl.CostEstimate(flops=COSTS.get(name, 1000), bytes_accessed=1000, transcendentals=0),
    )(*args)
    order.pinned += [results[i] for i in hbm]
    order.last = min(results, key=lambda r: r.size * r.dtype.itemsize)
    return results


def half_rows(rows):
    return (rows // 16 + 1) // 2 * 16


def hop_body(halves, *refs):
    count = len(halves)
    ins, outs, sems = refs[:count], refs[count:-1], refs[-1]
    copies = []
    for ref, half in zip(ins, halves):
        rows = ref.shape[-2]
        h = half_rows(rows) if half else rows
        for part in ((slice(0, h), slice(h, rows)) if half else (slice(0, rows),)):
            at = len(copies)
            if len(ref.shape) > len(outs[at].shape):
                source = ref.at[0]
            else:
                source = ref.at[part] if len(ref.shape) == 2 else ref.at[:, part]
            copies.append(pltpu.make_async_copy(source, outs[at], sems.at[at]))
    run_copies(copies)


def hop(order, name, *arrays, after=()):
    outs, halves, ins, specs = [], [], [], []
    for a in arrays:
        if isinstance(a, tuple):
            a, pick = a
            shape = a.shape if pick is None else a.shape[1:]
            ins.append(a)
            specs.append(
                VM if pick is None
                else pl.BlockSpec((1,) + shape, lambda *_, pick=pick, n=len(shape): (pick,) + (0,) * n)
            )
            halves.append(False)
            outs.append(sds(shape, a.dtype))
        else:
            ins.append(a)
            specs.append(VM)
            halves.append(True)
            h = half_rows(a.shape[-2])
            for rows in (h, a.shape[-2] - h):
                outs.append(sds(a.shape[:-2] + (rows, a.shape[-1]), a.dtype))
    got = list(kernel_call(
        order, functools.partial(hop_body, halves), name, tuple(outs),
        tuple(ins), specs, (ANY,) * len(outs),
        scratch=[pltpu.SemaphoreType.DMA((len(outs),))], after=after,
    ))
    return [(got.pop(0), got.pop(0)) if half else got.pop(0) for half in halves]


def gate(order, name, array):
    def nothing(source, out):
        pass

    return kernel_call(
        order, nothing, name, (sds(array.shape, array.dtype),), (array,), [ANY], (ANY,), aliases={0: 0}
    )[0]


def sds(shape, dtype):
    return jax.ShapeDtypeStruct(shape, dtype)


def nn(a, b):
    return jnp.dot(a, b, preferred_element_type=F32)


def nt(a, b):
    return lax.dot_general(a, b, (((1,), (1,)), ((), ())), preferred_element_type=F32)


def tn(a, b):
    return lax.dot_general(a, b, (((0,), (0,)), ((), ())), preferred_element_type=F32)


def eye():
    return (
        lax.broadcasted_iota(jnp.int32, (LANE, LANE), 0)
        == lax.broadcasted_iota(jnp.int32, (LANE, LANE), 1)
    ).astype(F32)


def col_to_tile(col):
    size = col.shape[0]
    diag = eye()
    row = lax.broadcasted_iota(jnp.int32, (8, LANE), 0)
    tile = jnp.zeros((8, LANE), F32)
    for t in range(pl.cdiv(size, LANE)):
        n = min(LANE, size - t * LANE)
        line = jnp.sum(col[t * LANE : t * LANE + n] * diag[:n], axis=0, keepdims=True)
        tile = jnp.where(row == t, line, tile)
    return tile


def tile_to_col(tile, size):
    diag = eye()
    cols = []
    for t in range(pl.cdiv(size, LANE)):
        n = min(LANE, size - t * LANE)
        cols.append(jnp.sum(tile[t : t + 1] * diag[:n], axis=1, keepdims=True))
    return jnp.concatenate(cols, axis=0)


def split_stats(both):
    high = both.astype(BF)
    rest = both - high.astype(F32)
    mid = rest.astype(BF)
    low = (rest - mid.astype(F32)).astype(BF)
    return jnp.concatenate([high, mid, low], axis=1)


def join_stats(tile):
    wide = tile.astype(F32)
    return wide[:, :LANE] + wide[:, LANE : 2 * LANE] + wide[:, 2 * LANE : 3 * LANE]


def stats_tile(first, second):
    return split_stats(jnp.concatenate([col_to_tile(first), col_to_tile(second)], axis=0))


def block_copies(me, refs, dst, sems, width, base=0, first_sem=0):
    rows = refs[0].shape[0]
    h = half_rows(rows)
    if len(refs) == 6:
        plan = ((0, 0, rows), (2, 0, rows), (3, 0, h), (3, h, rows - h), (1, 0, h), (1, h, rows - h))
    else:
        plan = ((0, 0, rows), (1, 0, rows), (2, 0, rows))
        plan += ((3, 0, rows),) if len(refs) == 4 else ((3, 0, h), (3, h, rows - h))
    copies = []
    for i, (ref, (k, start, size)) in enumerate(zip(refs, plan)):
        place = pl.multiple_of((me ^ k) * width, LANE)
        target = dst.at[pl.ds(base + start, size), pl.ds(place, width)]
        copies.append(pltpu.make_async_copy(ref, target, sems.at[first_sem + i]))
    return copies


def scatter_copies(me, part, outs, sems, width):
    send, send_a, send_b, keep = outs
    rows = part.shape[0]
    h = half_rows(rows)
    plan = ((0, 0, rows, keep.at[0]), (2, 0, rows, keep.at[1]), (1, 0, rows, send), (3, 0, h, send_a), (3, h, rows - h, send_b))
    copies = []
    for i, (k, start, size, dst) in enumerate(plan):
        place = pl.multiple_of((me ^ k) * width, LANE)
        source = part.at[pl.ds(start, size), pl.ds(place, width)]
        copies.append(pltpu.make_async_copy(source, dst, sems.at[i]))
    return copies


def scatter_shapes(rows, width):
    h = half_rows(rows)
    return (
        sds((rows, width), BF), sds((h, width), BF), sds((rows - h, width), BF), sds((2, rows, width), BF)
    )


def run_copies(copies):
    for c in copies:
        c.start()
    for c in copies:
        c.wait()


def norm_rows(raw, out, stat, size, width, blocks):
    total = width * blocks
    means = []
    for b in range(blocks):
        means.append(tile_to_col(raw[size : size + 8, b * width : b * width + LANE].astype(F32), size))
    mean_sum = jnp.zeros((size, 1), F32)
    for b in range(blocks):
        part = raw[:size, b * width : (b + 1) * width].astype(F32)
        mean_sum = mean_sum + jnp.sum(part, axis=1, keepdims=True) + width * means[b]
    mean = mean_sum * (1.0 / total)
    square = jnp.zeros((size, 1), F32)
    for b in range(blocks):
        part = raw[:size, b * width : (b + 1) * width].astype(F32) + (means[b] - mean)
        square = square + jnp.sum(part * part, axis=1, keepdims=True)
    inverse = lax.rsqrt(square * (1.0 / total) + EPS)
    for b in range(blocks):
        part = raw[:size, b * width : (b + 1) * width].astype(F32) + (means[b] - mean)
        out[:size, b * width : (b + 1) * width] = (part * inverse).astype(BF)
    stat[0] = jnp.broadcast_to(mean, (size, LANE))
    stat[1] = jnp.broadcast_to(inverse, (size, LANE))


def send_rows(values, pay, size, width):
    mean = jnp.mean(values, axis=1, keepdims=True).astype(BF).astype(F32)
    pay[:size] = (values - mean).astype(BF)
    tile = col_to_tile(mean).astype(BF)
    pay[size:] = jnp.zeros((EXTRA, width), BF)
    pay[size : size + EXTRA, :LANE] = jnp.concatenate([tile, jnp.zeros((8, LANE), BF)], axis=0)


def column_masks(size, width):
    slot = lax.broadcasted_iota(jnp.int32, (size, 1), 0).astype(F32)
    col = slot - width * jnp.floor((slot + 0.5) * (1.0 / width))
    return col > 0.5, col < width - 1.5


def conv_forward_body(l, info, x_ref, taps, bias, pay, conv, pad):
    size, width = conv.shape
    slot = lax.broadcasted_iota(jnp.int32, (size, 1), 0)
    x = jnp.where(slot < info[l, 0], x_ref[...].astype(F32), 0.0)
    pad[:MARGIN] = jnp.zeros((MARGIN, width), F32)
    pad[MARGIN + size :] = jnp.zeros((MARGIN, width), F32)
    here = slice(MARGIN, MARGIN + size)
    for bucket, w in enumerate(WIDTHS):

        @pl.when(info[l, 1] == bucket)
        def _():
            not_first, not_last = column_masks(size, w)
            pad[here] = x
            left = jnp.where(not_first, pad[MARGIN - 1 : MARGIN - 1 + size], 0.0)
            right = jnp.where(not_last, pad[MARGIN + 1 : MARGIN + 1 + size], 0.0)
            total = bias[...] + left * taps[3:4] + x * taps[4:5] + right * taps[5:6]
            pad[here] = left * taps[0:1] + x * taps[1:2] + right * taps[2:3]
            total = total + pad[MARGIN - w : MARGIN - w + size]
            pad[here] = left * taps[6:7] + x * taps[7:8] + right * taps[8:9]
            conv[...] = total + pad[MARGIN + w : MARGIN + w + size]

    send_rows(conv[...], pay, size, width)


def conv_backward_body(l, info, keep, got, far, conv, stat, x_ref, first_grad, taps, out, sums, pad, total_width):
    size, width = conv.shape
    slot = lax.broadcasted_iota(jnp.int32, (size, 1), 0)
    mask = slot < info[l, 0]
    grad = keep[:size].astype(F32) + got[:size].astype(F32) + far[:size].astype(F32)
    both = join_stats(keep[size:]) + join_stats(got[size:]) + join_stats(far[size:])
    both = both * (1.0 / total_width)
    mean_grad = tile_to_col(both[:8], size)
    mean_cross = tile_to_col(both[8:], size)
    mean = stat[0][:, :1]
    inverse = stat[1][:, :1]
    normed = (conv[...] - mean) * inverse
    grad = inverse * (grad - mean_grad - normed * mean_cross)
    x = jnp.where(mask, x_ref[...].astype(F32), 0.0)
    pad[:MARGIN] = jnp.zeros((MARGIN, width), F32)
    pad[MARGIN + size :] = jnp.zeros((MARGIN, width), F32)
    here = slice(MARGIN, MARGIN + size)
    sums[...] = jnp.zeros_like(sums)
    sums[9:10] = jnp.sum(grad, axis=0, keepdims=True)
    for bucket, w in enumerate(WIDTHS):

        @pl.when(info[l, 1] == bucket)
        def _():
            not_first, not_last = column_masks(size, w)
            pad[here] = x
            left = jnp.where(not_first, pad[MARGIN - 1 : MARGIN - 1 + size], 0.0)
            right = jnp.where(not_last, pad[MARGIN + 1 : MARGIN + 1 + size], 0.0)
            pad[here] = grad
            rows = (pad[MARGIN + w : MARGIN + w + size], grad, pad[MARGIN - w : MARGIN - w + size])
            for r in range(3):
                for c, side in enumerate((left, x, right)):
                    tap = 3 * r + c
                    sums[tap : tap + 1] = jnp.sum(rows[r] * side, axis=0, keepdims=True)
            back = [sum(rows[r] * taps[3 * r + c : 3 * r + c + 1] for r in range(3)) for c in range(3)]
            pad[here] = jnp.where(not_first, back[0], 0.0)
            total = back[1] + pad[MARGIN + 1 : MARGIN + 1 + size]
            pad[here] = jnp.where(not_last, back[2], 0.0)
            total = total + pad[MARGIN - 1 : MARGIN - 1 + size]
            out[...] = (first_grad[...] + jnp.where(mask, total, 0.0)).astype(BF)


def gelu_both(h):
    t_den = 1.0 + (0.3275911 * 0.7071067811865476) * jnp.abs(h)
    t = pl.reciprocal(t_den, approx=True)
    t = t * (2.0 - t_den * t)
    bell = jnp.exp(-0.5 * h * h)
    poly = t * (
        0.127414796 + t * (-0.142248368 + t * (0.7107068705 + t * (-0.7265760135 + t * 0.5307027145)))
    )
    tail = poly * bell
    phi = jnp.where(h >= 0, 1.0 - tail, tail)
    return h * phi, phi + h * bell * 0.3989422804014327


def ffn_in_body(
    l, lats, count, info, *refs, width, chunk
):
    blocks, (w, bias, nrm, stat, act, slope, spat, total, raw, sems) = refs[:count], refs[count:]
    j = pl.program_id(0)
    size = nrm.shape[0]

    @pl.when(j == 0)
    def _():
        run_copies(block_copies(info[lats, 0], blocks, raw, sems, width))
        norm_rows(raw, nrm, stat, size, width, 4)
        total[...] = jnp.zeros_like(total)

    valid_from = size - size // 32
    cols = act.shape[1]
    square = jnp.zeros((1, cols), F32)
    for r in range(0, size, chunk):
        h = nn(nrm[r : r + chunk], w[...]) + bias[...]
        a, d = gelu_both(h)
        act[r : r + chunk] = a.astype(BF)
        slope[r : r + chunk] = d.astype(BF)
        sq = a * a
        if r + chunk > valid_from:
            slot = r + lax.broadcasted_iota(jnp.int32, (chunk, 1), 0)
            sq = jnp.where(slot < info[l, 0], sq, 0.0)
        square = square + jnp.sum(sq, axis=0, keepdims=True)
    here = jnp.sqrt(square)
    spat[...] = here
    total[...] = total[...] + jnp.sum(here)


def denominator(t0, t1, t2, t3, hidden_total):
    whole = t0[...] + t1[...] + t2[...] + t3[...]
    return whole[:1, :1] * (1.0 / hidden_total) + EPS


def ffn_out_body(lats, hidden_total, info, act, spat, t0, t1, t2, t3, gamma, beta, w, gated, s0, s1, s2, keep, part, sems, width, chunk):
    j = pl.program_id(0)
    size = act.shape[0]

    @pl.when(j == 0)
    def _():
        gain = 1.0 + gamma[...] * (spat[...] / denominator(t0, t1, t2, t3, hidden_total))
        for r in range(0, size, chunk):
            rows = slice(r, r + chunk)
            gated[rows] = (act[rows].astype(F32) * gain + beta[...]).astype(BF)

    cols = w.shape[1]
    part[:, pl.ds(pl.multiple_of(j * cols, LANE), cols)] = nn(gated[...], w[...]).astype(BF)

    @pl.when(j == pl.num_programs(0) - 1)
    def _():
        run_copies(scatter_copies(info[lats, 0], part, (s0, s1, s2, keep), sems, width))


def add_body(stats, keep, got_a, got_b, out):
    h = got_a.shape[0]
    size = out.shape[0] - (EXTRA if stats else 0)
    out[:h] = (keep[:h].astype(F32) + got_a[...].astype(F32)).astype(BF)
    out[h:size] = (keep[h:size].astype(F32) + got_b[: size - h].astype(F32)).astype(BF)
    if stats:
        out[size:] = split_stats(join_stats(keep[size:]) + join_stats(got_b[size - h :]))


def middle_body(x, keep, got, far, out_bias, scale, shift, first, pay):
    size, width = first.shape
    value = x[...].astype(F32) + (
        keep[...].astype(F32) + got[...].astype(F32) + far[...].astype(F32) + out_bias[...]
    )
    first[...] = value
    send_rows(value * (1.0 + scale[...]) + shift[...], pay, size, width)


def text_body(lats, info, b0, b1, b2, b3, w, bias, full, low, sems, width, text_len):
    lat_count, rows, _ = low.shape
    copies = []
    for l in range(lat_count):
        refs = [b.at[l] for b in (b0, b1, b2, b3)]
        copies += block_copies(info[lats, 0], refs, full.at[l], sems, width, first_sem=4 * l)
    run_copies(copies)
    row = lax.broadcasted_iota(jnp.int32, (rows, 1), 0)
    for l in range(lat_count):
        low[l] = jnp.where(row < text_len, nn(full[l], w[...]) + bias[...], 0.0).astype(BF)


def attention_body(
    l, lats, counts, info, *refs, width
):
    pays, refs = refs[: counts[0]], refs[counts[0] :]
    texts, refs = refs[: counts[1]], refs[counts[1] :]
    grads, refs = refs[: counts[2]], refs[counts[2] :]
    (
    wq, wk, wv, wo, q_bias, v_bias, ctx_out, stat_out, g_out, att_out, dqkv_out, s0, s1, s2, keep, sums,
    raw, w_all, w_out, q_s, k_s, v_s, do_s, kt_s, vt_s, att_t, dq_t, scores, part, ctx, stat, g_full, att, dqkv, sems,
    ) = refs
    leaving = [
        pltpu.make_async_copy(source, dst, sems.at[19 + i])
        for i, (source, dst) in enumerate(
            ((ctx, ctx_out), (stat, stat_out), (g_full, g_out), (att, att_out), (dqkv, dqkv_out))
        )
    ]
    me = info[lats, 0]
    size = att.shape[0]
    rows = ctx.shape[0]
    total = ctx.shape[1]
    text = rows - size
    factor = HEAD ** (-0.5)
    copy_in = block_copies(me, pays, raw, sems, width)
    copy_in += block_copies(me, [x.at[l] for x in texts], ctx, sems, width, base=size, first_sem=5)
    copy_w = [
        pltpu.make_async_copy(ref, w_all.at[:, k * width : (k + 1) * width], sems.at[10 + k])
        for k, ref in enumerate((wq, wk, wv))
    ]
    copy_g = [pltpu.make_async_copy(wo, w_out, sems.at[13])]
    copy_g += block_copies(me, grads, g_full, sems, width, first_sem=14)
    for c in copy_in + copy_w + copy_g:
        c.start()
    for c in copy_in:
        c.wait()
    norm_rows(raw, ctx, stat, size, width, 4)
    leaving[0].start()
    leaving[1].start()
    for c in copy_w:
        c.wait()
    q_s[...] = ((nn(ctx[:size], w_all[:, :width]) + q_bias[...]).astype(BF).astype(F32) * factor).astype(BF)
    keys = nn(ctx[...], w_all[:, width : 2 * width]).astype(BF)
    k_s[...] = keys
    kt_s[...] = keys.T
    values = (nn(ctx[...], w_all[:, 2 * width :]) + v_bias[...]).astype(BF)
    v_s[...] = values
    vt_s[...] = values.T
    for c in copy_g:
        c.wait()
    leaving[2].start()
    do_s[...] = nt(g_full[...], w_out[...]).astype(BF)
    tail = (size - size // 32) // 8 * 8
    key_row = tail + lax.broadcasted_iota(jnp.int32, (rows - tail, 1), 0)
    key_ok = (key_row < info[l, 0]) | ((key_row >= size) & (key_row < size + info[l, 2]))

    def pair(p, carry):
        lo = pl.multiple_of(p * LANE, LANE)
        q2 = q_s[:, pl.ds(lo, LANE)]
        k2 = k_s[:, pl.ds(lo, LANE)]
        v2 = v_s[:, pl.ds(lo, LANE)]
        do2 = do_s[:, pl.ds(lo, LANE)]
        dks, dvs = [], []
        heads = []
        for half in range(2):
            lanes = slice(half * HEAD, (half + 1) * HEAD)
            line = pl.ds(pl.multiple_of(p * LANE + half * HEAD, HEAD), HEAD)
            heads.append((line, q2[:, lanes], k2[:, lanes], v2[:, lanes], do2[:, lanes]))
        for half, (line, qh, kh, vh, doh) in enumerate(heads):
            scores[half] = nt(kh, qh)
            scores[half, tail:] = jnp.where(key_ok, scores[half, tail:], -1e30)
        lows = []
        for half in range(2):
            top = jnp.max(scores[half], axis=0, keepdims=True)
            expo = jnp.exp(scores[half] - top)
            probs = expo * (1.0 / jnp.sum(expo, axis=0, keepdims=True))
            scores[half] = probs
            lows.append(probs.astype(BF))
        for half, (line, qh, kh, vh, doh) in enumerate(heads):
            att_t[line] = nn(vt_s[line], lows[half])
            dvs.append(nn(lows[half], doh))
            grad_p = nt(vh, doh)
            dot = jnp.sum(scores[half] * grad_p, axis=0, keepdims=True)
            grad_s = (scores[half] * (grad_p - dot)).astype(BF)
            dks.append(nn(grad_s, qh))
            dq_t[line] = nn(kt_s[line], grad_s) * factor
        dqkv[:, pl.ds(pl.multiple_of(width + lo, LANE), LANE)] = jnp.concatenate(dks, axis=1).astype(BF)
        dqkv[:, pl.ds(pl.multiple_of(2 * width + lo, LANE), LANE)] = jnp.concatenate(dvs, axis=1).astype(BF)
        return carry

    lax.fori_loop(0, width // LANE, pair, 0)
    att[...] = att_t[...].astype(BF).T
    leaving[3].start()
    dq = dq_t[...].astype(BF).T
    dqkv[:size, :width] = dq
    dqkv[size:, :width] = jnp.zeros((text, width), BF)
    leaving[4].start()
    sums[...] = jnp.zeros_like(sums)
    sums[0:1] = jnp.sum(dq.astype(F32), axis=0, keepdims=True)
    sums[1:2] = jnp.sum(dqkv[:, 2 * width :].astype(F32), axis=0, keepdims=True)
    first = jnp.zeros((size, 1), F32)
    second = jnp.zeros((size, 1), F32)
    cols = 256
    for n in range(0, total, cols):
        block = nt(dqkv[...], w_all[n : n + cols]).astype(BF)
        part[:rows, n : n + cols] = block
        wide = block[:size].astype(F32)
        first = first + jnp.sum(wide, axis=1, keepdims=True)
        second = second + jnp.sum(wide * ctx[:size, n : n + cols].astype(F32), axis=1, keepdims=True)
    tile = stats_tile(first, second)
    for b in range(4):
        part[rows:, b * width : (b + 1) * width] = tile
    run_copies(scatter_copies(me, part, (s0, s1, s2, keep), sems, width))
    for c in leaving:
        c.wait()


def project_body(lats, info, *refs):
    atts, w, outs, part, sems = refs[:lats], refs[lats], refs[lats + 1 : lats + 5], refs[-2], refs[-1]
    width = atts[0].shape[1]
    cols = 512
    copies = []
    for l in range(lats):
        for n in range(0, part.shape[2], cols):
            part[l, :, n : n + cols] = nn(atts[l][...], w[:, n : n + cols]).astype(BF)
        views = [o.at[l] for o in outs[:3]] + [outs[3].at[:, l]]
        copies += scatter_copies(info[lats, 0], part.at[l], views, sems.at[l], width)
        for c in copies[-5:]:
            c.start()
    for c in copies:
        c.wait()


def add_out_body(keep, got_a, got_b, out):
    h = got_a.shape[1]
    out[:, :h] = (keep[:, :h].astype(F32) + got_a[...].astype(F32)).astype(BF)
    out[:, h:] = (keep[:, h:].astype(F32) + got_b[...].astype(F32)).astype(BF)


def result_body(lats, *refs):
    firsts, (scale, shift, keep, got, far, bias, out) = refs[:lats], refs[lats:]
    for l in range(lats):
        second = firsts[l][...] * (1.0 + scale[l]) + shift[l]
        branch = keep[l].astype(F32) + got[l].astype(F32) + far[l].astype(F32) + bias[...]
        out[l] = (second + branch).astype(BF)


def second_grad_body(keep, got, far, g_ref, first_ref, stat, scale, shift, pay, first_grad, text, sums, total_width, text_len):
    size, width = first_grad.shape
    rows = keep.shape[0] - EXTRA
    both = join_stats(keep[rows:]) + join_stats(got[rows:]) + join_stats(far[rows:])
    both = both * (1.0 / total_width)
    mean_grad = tile_to_col(both[:8], size)
    mean_cross = tile_to_col(both[8:], size)
    grad = keep[:size].astype(F32) + got[:size].astype(F32) + far[:size].astype(F32)
    first = first_ref[...]
    gain = 1.0 + scale[...]
    inverse = stat[1][:, :1]
    normed = (first * gain + shift[...] - stat[0][:, :1]) * inverse
    upstream = g_ref[...].astype(F32)
    second_grad = upstream + inverse * (grad - mean_grad - normed * mean_cross)
    scaled = second_grad * gain
    pay[...] = scaled.astype(BF)
    first_grad[...] = scaled
    row = lax.broadcasted_iota(jnp.int32, (rows - size, 1), 0)
    tail = keep[size:rows].astype(F32) + got[size:rows].astype(F32) + far[size:rows].astype(F32)
    low = jnp.where(row < text_len, tail, 0.0).astype(BF)
    text[...] = low
    sums[...] = jnp.zeros_like(sums)
    sums[0:1] = jnp.sum(second_grad * first, axis=0, keepdims=True)
    sums[1:2] = jnp.sum(second_grad, axis=0, keepdims=True)
    sums[2:3] = jnp.sum(scaled, axis=0, keepdims=True)
    sums[3:4] = jnp.sum(low.astype(F32), axis=0, keepdims=True)
    sums[4:5] = jnp.sum(upstream, axis=0, keepdims=True)


def gated_grad_body(lats, count, joined, info, *refs, width, chunk):
    blocks, (w, act, gamma, spat, *refs) = refs[:count], refs[count:]
    if joined:
        before, *refs = refs
    full, out, s1, s2, both, sems = refs
    total = both.at[1] if joined else both
    j = pl.program_id(0)
    size = full.shape[0]

    @pl.when(j == 0)
    def _():
        run_copies(block_copies(info[lats, 0], blocks, full, sems, width))
        total[...] = jnp.zeros((8, LANE), F32)
        if joined:
            both[0] = before[...]

    cols = out.shape[1]
    cross = jnp.zeros((1, cols), F32)
    plain = jnp.zeros((1, cols), F32)
    for r in range(0, size, chunk):
        grad = nt(full[r : r + chunk], w[...])
        out[r : r + chunk] = grad.astype(BF)
        cross = cross + jnp.sum(grad * act[r : r + chunk].astype(F32), axis=0, keepdims=True)
        plain = plain + jnp.sum(grad, axis=0, keepdims=True)
    s1[...] = cross
    s2[...] = plain
    total[...] = total[...] + jnp.sum(cross * gamma[...] * spat[...])


def hidden_grad_body(
    l, lats, hidden_total, info, gg, act, slope, spat, s1, gamma, t0, t1, t2, t3, c0, c1, c2, c3, w, nrm,
    hidden, d0, d1, d2, keep, bias_sum, gamma_sum, part, acc, sems, width, chunk,
):
    j = pl.program_id(0)
    size = hidden.shape[0]

    @pl.when(j == 0)
    def _():
        den = denominator(t0, t1, t2, t3, hidden_total)
        cross = (c0[...] + c1[...] + c2[...] + c3[...])[:1, :1]
        response = spat[...] / den
        gamma_sum[...] = response * s1[...]
        grad_spat = gamma[...] * s1[...] / den - cross / (den * den) * (1.0 / hidden_total)
        gain = gamma[...] * response + 1.0
        pull = grad_spat / spat[...]
        total = jnp.zeros_like(bias_sum[...])
        for r in range(0, size, chunk):
            rows = slice(r, r + chunk)
            slot = r + lax.broadcasted_iota(jnp.int32, (chunk, 1), 0)
            active = jnp.where(slot < info[l, 0], act[rows].astype(F32), 0.0)
            grad = gg[rows].astype(F32) * gain + pull * active
            low = (grad * slope[rows].astype(F32)).astype(BF)
            hidden[rows] = low
            total = total + jnp.sum(low.astype(F32), axis=0, keepdims=True)
        bias_sum[...] = total
        acc[...] = jnp.zeros_like(acc)

    cols = w.shape[0]
    block = nt(hidden[...], w[...]).astype(BF)
    part[:size, pl.ds(pl.multiple_of(j * cols, LANE), cols)] = block
    wide = block.astype(F32)
    acc[0] = acc[0] + jnp.sum(wide, axis=1, keepdims=True)
    acc[1] = acc[1] + jnp.sum(wide * nrm[...].astype(F32), axis=1, keepdims=True)

    @pl.when(j == pl.num_programs(0) - 1)
    def _():
        tile = stats_tile(acc[0][:, :1], acc[1][:, :1])
        for b in range(4):
            part[size:, b * width : (b + 1) * width] = tile
        run_copies(scatter_copies(info[lats, 0], part, (d0, d1, d2, keep), sems, width))


def weight_grad_body(sets, split, width, dp, *refs):
    if split:
        places, refs = refs[0], refs[1:]
    count = sum(n for n, _, _ in sets)
    lefts, rights, refs = refs[:count], refs[count : 2 * count], refs[2 * count :]
    outs, refs = refs[: 2 if split else 1], refs[2 if split else 1 :]
    bufs, (stage, sems) = refs[:-2], refs[-2:]
    parts = width // (2 * (width // dp)) if split else 4
    chunk = width // parts
    share = width // dp
    used = 0
    coming = []
    at = 0
    for i, (n, start, cols) in enumerate(sets):
        lbuf, rbuf = bufs[2 * i], bufs[2 * i + 1]
        row = 0
        firsts, chunks = [], [[] for _ in range(parts)]
        for k in range(at, at + n):
            rows = lefts[k].shape[0]
            here = pl.ds(row, rows)
            firsts.append(
                pltpu.make_async_copy(rights[k].at[:, pl.ds(start, cols)], rbuf.at[here], sems.at[used])
            )
            used += 1
            for c in range(parts):
                lanes = pl.ds(c * chunk, chunk)
                chunks[c].append(
                    pltpu.make_async_copy(lefts[k].at[:, lanes], lbuf.at[here, lanes], sems.at[used])
                )
                used += 1
            row += rows
        coming.append((firsts, chunks))
        at += n
    for firsts, _ in coming:
        for c in firsts:
            c.start()
    for c in range(parts):
        for _, chunks in coming:
            for copy in chunks[c]:
                copy.start()
    leaving = []
    for c in range(parts):
        off = 0
        for i, (n, start, cols) in enumerate(sets):
            firsts, chunks = coming[i]
            for copy in (firsts if c == 0 else []) + chunks[c]:
                copy.wait()
            block = tn(bufs[2 * i][:, c * chunk : (c + 1) * chunk], bufs[2 * i + 1][...]).astype(BF)
            if split:
                near, far = block[:share], block[share:]
                flip = places[1] == 1
                stage[0, c, :, off : off + cols] = jnp.where(flip, near, far)
                stage[1, c, :, off : off + cols] = jnp.where(flip, far, near)
            else:
                stage[c * chunk : (c + 1) * chunk, off : off + cols] = block
            off += cols
        if split:
            for k in range(2):
                leaving.append(
                    pltpu.make_async_copy(stage.at[k, c], outs[k].at[places[0] ^ c], sems.at[used])
                )
                used += 1
        else:
            rows = pl.ds(c * chunk, chunk)
            leaving.append(pltpu.make_async_copy(stage.at[rows], outs[0].at[rows], sems.at[used]))
            used += 1
        for copy in leaving[-2 if split else -1 :]:
            copy.start()
    for copy in leaving:
        copy.wait()


def weight_grads(order, name, places, sets, dp, after=()):
    split = places is not None
    lefts = [l for pairs, _, _ in sets for l, _ in pairs]
    rights = [r for pairs, _, _ in sets for _, r in pairs]
    width = lefts[0].shape[1]
    wide = sum(cols for _, _, cols in sets)
    scratch = []
    for pairs, _, cols in sets:
        depth = sum(l.shape[0] for l, _ in pairs)
        scratch += [pltpu.VMEM((depth, width), BF), pltpu.VMEM((depth, cols), BF)]
    share = width // dp
    if split:
        outs = (sds((dp // 2, share, wide), BF),) * 2
        scratch.append(pltpu.VMEM((2, dp // 2, share, wide), BF))
    else:
        outs = (sds((width, wide), BF),)
        scratch.append(pltpu.VMEM((width, wide), BF))
    scratch.append(pltpu.SemaphoreType.DMA((5 * len(lefts) + 8,)))
    plan = [(len(pairs), start, cols) for pairs, start, cols in sets]
    args = ((places,) if split else ()) + (*lefts, *rights)
    return kernel_call(
        order, functools.partial(weight_grad_body, plan, split, width, dp), name, outs, args,
        ([SM] if split else []) + [ANY] * (2 * len(lefts)), (ANY,) * len(outs), scratch=scratch,
        hbm=(1,) if split else (0,), limit=40, after=after,
    )


SUMMED = 32


def join_small(mine, near, out):
    out[:SUMMED] = mine[:SUMMED] + near[:SUMMED]
    rest = mine.shape[0] - SUMMED
    out[SUMMED : SUMMED + rest] = mine[SUMMED:]
    out[SUMMED + rest :] = near[SUMMED:]


def combine_body(small, keep, got, *refs):
    if small:
        mine, near, *outs, whole = refs
        join_small(mine, near, whole)
    else:
        outs = refs
    count = keep.shape[0]
    for k in range(count):
        total = (keep[k].astype(F32) + got[k].astype(F32)).astype(BF)
        if count == 2:
            outs[1 - k][...] = total
        else:
            outs[1 - k % 2][k // 2] = total


def finish_body(counts, small, layout, *refs):
    chunks = []
    at = 0
    for n in counts:
        chunks.append(refs[at : at + n])
        at += n
    extra = refs[at : at + small]
    outs = refs[at + small :]
    for ins, plan in zip(chunks, layout):
        for start, cols, out, offset, flip in plan:
            lanes = slice(start, start + cols)
            total = 0.0
            for ref in ins:
                total = total + ref[:, lanes].astype(F32)
            if flip:
                outs[out][offset : offset + cols] = total.T
            else:
                outs[out][:, offset : offset + cols] = total
    if small:
        *outs, whole, scale, shift = outs
        join_small(*extra, whole)
        rows = whole.shape[0] - SUMMED
        r = scale.shape[0]
        lines = [whole[SUMMED + b : SUMMED + b + 8] for b in range(0, rows, 8)]
        noise = jnp.concatenate([x[4:6, :r] for x in lines], axis=0)
        for k, out in enumerate((scale, shift)):
            values = jnp.concatenate([x[2 * k : 2 * k + 2] for x in lines], axis=0)
            out[...] = lax.dot_general(
                noise, values, (((0,), (0,)), ((), ())), precision=lax.Precision.HIGHEST, preferred_element_type=F32
            )


def pack_body(lat_count, noise, *refs):
    second, attn, gam, bet, conv, hid = (refs[k * lat_count : (k + 1) * lat_count] for k in range(6))
    out = refs[-1]
    width = out.shape[1]
    out[:16] = sum(c[...] for c in conv)
    out[24:] = jnp.zeros((out.shape[0] - 24, width), F32)
    for k, group in enumerate((gam, bet, hid)):
        whole = sum(g[...] for g in group)
        for b in range(whole.shape[1] // width):
            at = 12 + 4 * k + b
            out[at : at + 1] = whole[:, b * width : (b + 1) * width]
    for i in range(5):
        out[24 + i : 25 + i] = sum(second[l][i : i + 1] for l in range(lat_count))
    for i in range(2):
        out[29 + i : 30 + i] = sum(attn[l][i : i + 1] for l in range(lat_count))
    for l in range(lat_count):
        out[SUMMED + l : SUMMED + l + 1] = second[l][0:1]
        out[SUMMED + 2 + l : SUMMED + 3 + l] = second[l][1:2]
        out[SUMMED + 4 + l : SUMMED + 5 + l, : noise.shape[1]] = noise[l : l + 1]


def local(
    latents, valid_mask, bucket_ids, text_count, text_tokens, noise_embed, conv_kernel, conv_bias,
    mixer_expand_weight, ffn_in_bias, grn_gamma, grn_beta, mixer_contract_weight, ffn_out_bias,
    scale_weight, scale_bias, shift_weight, shift_bias, text_weight, text_bias, query_weight, query_bias,
    key_weight, value_weight, value_bias, attn_out, attn_out_bias, upstream,
):
    lats, size, width = latents.shape
    groups = lax.axis_size("chan")
    dp = lax.axis_size("dp")
    total = width * groups
    hidden = mixer_expand_weight.shape[1]
    hidden_total = hidden * groups
    text_len = text_tokens.shape[1]
    text_rows = pl.cdiv(text_len, 16) * 16
    rows = size + text_rows
    highest = lax.Precision.HIGHEST
    me = lax.axis_index("chan")
    order = Order()
    order.pinned += [
        mixer_expand_weight, mixer_contract_weight, text_weight, query_weight, key_weight, value_weight, attn_out,
        latents, upstream,
    ]

    def xswap(v):
        return lax.ppermute(v, "chan", [(i, i ^ 2) for i in range(groups)])

    def cswap(v):
        return lax.ppermute(v, "chan", [(i, i ^ 1) for i in range(groups)])

    def gather_start(v):
        return v, cswap(v), xswap(v)

    def gather_end(state, halves):
        return (*state, *(cswap(h) for h in halves))

    def gather_late(name, v, far):
        far_parts, own_parts = hop(order, name, far, v)
        return (v, far, *(cswap(h) for h in far_parts), *(cswap(h) for h in own_parts))

    def gather_small(v):
        return v, cswap(v), xswap(v), lax.ppermute(v, "chan", [(i, i ^ 3) for i in range(groups)])

    def line(v):
        return v.reshape(1, -1)

    info = jnp.stack(
        [jnp.sum(valid_mask, axis=1), bucket_ids, text_count, jnp.zeros_like(bucket_ids)], axis=1
    )
    info = jnp.concatenate([info, jnp.full((1, 4), me, jnp.int32)], axis=0).astype(jnp.int32)

    def lat_spec(l, *shape):
        return pl.BlockSpec((None,) + shape, lambda *_: (l,) + (0,) * len(shape))

    def part_spec(k, shape):
        return pl.BlockSpec((None,) + tuple(shape[1:]), lambda *_: (k, 0, 0))

    text_act = jax.nn.silu(text_tokens.astype(F32)).astype(BF)
    text_act = jnp.pad(text_act, ((0, 0), (0, text_rows - text_len), (0, 0)))

    def conv_forward(l, after=()):
        return kernel_call(
            order, functools.partial(conv_forward_body, l), "conv_forward_%d" % l,
            (sds((size + EXTRA, width), BF), sds((size, width), F32)),
            (info, latents, conv_kernel, line(conv_bias)),
            [SM, lat_spec(l, size, width), VM, VM], (VM, VM),
            scratch=[pltpu.VMEM((size + 2 * MARGIN, width), F32)], hbm=(1,), after=after,
        )

    tile_cols = 512

    def ffn_in(l, blocks):
        n = hidden // tile_cols
        col = pl.BlockSpec((1, tile_cols), lambda j: (0, j))
        wide = pl.BlockSpec((size, tile_cols), lambda j: (0, j))
        return kernel_call(
            order, functools.partial(ffn_in_body, l, lats, len(blocks), width=width, chunk=size // 3), "ffn_in_%d" % l,
            (sds((size, total), BF), sds((2, size, LANE), F32), sds((size, hidden), BF),
             sds((size, hidden), BF), sds((1, hidden), F32), sds((8, LANE), F32)),
            (info, *blocks, mixer_expand_weight, line(ffn_in_bias)),
            [SM] + [ANY] * len(blocks) + [pl.BlockSpec((total, tile_cols), lambda j: (0, j)), col],
            (VM, VM, wide, wide, col, VM), grid=(n,),
            scratch=[pltpu.VMEM((size + EXTRA, total), BF), pltpu.SemaphoreType.DMA((5,))], hbm=(0, 1, 3),
        )

    def ffn_out(l, act, spat, tots, after=()):
        n = total // tile_cols
        return kernel_call(
            order, functools.partial(ffn_out_body, lats, hidden_total, width=width, chunk=32), "ffn_out_%d" % l,
            (sds((size, hidden), BF),) + scatter_shapes(size, width),
            (info, act, spat, *tots, line(grn_gamma), line(grn_beta), mixer_contract_weight),
            [SM] + [VM] * 8 + [pl.BlockSpec((hidden, tile_cols), lambda j: (0, j))],
            (VM,) + (ANY,) * 4, grid=(n,),
            scratch=[pltpu.VMEM((size, total), BF), pltpu.SemaphoreType.DMA((5,))], hbm=(0, 4), after=after,
        )

    def swap_halves(outs):
        return tuple(cswap(o) for o in outs)

    def scatter_end(name, keep, gots, stats, after=()):
        got, got_a, got_b = gots
        half = kernel_call(
            order, functools.partial(add_body, stats), name, (sds(keep.shape[1:], BF),), (keep, got_a, got_b),
            [part_spec(1, keep.shape), VM, VM], (VM,), after=after,
        )[0]
        return keep, got, xswap(half)

    scale_rows = (jnp.dot(noise_embed, scale_weight, precision=highest) + scale_bias)[:, None]
    shift_rows = (jnp.dot(noise_embed, shift_weight, precision=highest) + shift_bias)[:, None]

    def middle(l, pieces, after=()):
        keep, got, far = pieces
        spec = part_spec(0, keep.shape)
        row = lat_spec(l, 1, width)
        return kernel_call(
            order, middle_body, "middle_%d" % l,
            (sds((size, width), F32), sds((size + EXTRA, width), BF)),
            (latents, keep, got, far, line(ffn_out_bias), scale_rows, shift_rows),
            [lat_spec(l, size, width), spec, VM, VM, VM, row, row], (VM, VM), hbm=(0,), after=after,
        )

    def text_low_rows(blocks, after):
        return kernel_call(
            order, functools.partial(text_body, lats, width=width, text_len=text_len), "text_rows",
            (sds((lats, text_rows, total), BF), sds((lats, text_rows, width), BF)),
            (info, *blocks, text_weight, line(text_bias)),
            [SM] + [ANY] * 4 + [VM, VM], (VM, VM), scratch=[pltpu.SemaphoreType.DMA((4 * lats,))], hbm=(0,), after=after,
        )

    def attention(l, blocks, texts, grads):
        return kernel_call(
            order,
            functools.partial(attention_body, l, lats, (len(blocks), len(texts), len(grads)), width=width),
            "attention_%d" % l,
            (sds((rows, total), BF), sds((2, size, LANE), F32), sds((size, total), BF),
             sds((size, width), BF), sds((rows, 3 * width), BF))
            + scatter_shapes(rows + EXTRA, width) + (sds((8, width), F32),),
            (info, *blocks, *texts, *grads, query_weight, key_weight, value_weight, attn_out,
             line(query_bias), line(value_bias)),
            [SM] + [ANY] * (len(blocks) + len(texts) + len(grads) + 4) + [VM, VM],
            (ANY,) * 9 + (VM,),
            scratch=[
                pltpu.VMEM((size + EXTRA, total), BF),
                pltpu.VMEM((total, 3 * width), BF),
                pltpu.VMEM((width, total), BF),
                pltpu.VMEM((size, width), BF),
                pltpu.VMEM((rows, width), BF),
                pltpu.VMEM((rows, width), BF),
                pltpu.VMEM((size, width), BF),
                pltpu.VMEM((width, rows), BF),
                pltpu.VMEM((width, rows), BF),
                pltpu.VMEM((width, size), F32),
                pltpu.VMEM((width, size), F32),
                pltpu.VMEM((2, rows, size), F32),
                pltpu.VMEM((rows + EXTRA, total), BF),
                pltpu.VMEM((rows, total), BF),
                pltpu.VMEM((2, size, LANE), F32),
                pltpu.VMEM((size, total), BF),
                pltpu.VMEM((size, width), BF),
                pltpu.VMEM((rows, 3 * width), BF),
                pltpu.SemaphoreType.DMA((24,)),
            ],
            hbm=(0, 1, 2, 3, 4, 8, 9), limit=36,
        )

    def project(atts):
        h = half_rows(size)
        return kernel_call(
            order, functools.partial(project_body, lats), "project",
            tuple(sds((lats, r, width), BF) for r in (size, h, size - h)) + (sds((2, lats, size, width), BF),),
            (info, *atts, attn_out), [SM] + [VM] * (lats + 1), (ANY,) * 4,
            scratch=[pltpu.VMEM((lats, size, total), BF), pltpu.SemaphoreType.DMA((lats, 5))], hbm=(3,),
        )

    def project_end(keep, gots):
        got, got_a, got_b = gots
        half = kernel_call(
            order, add_out_body, "add_out", (sds(keep.shape[1:], BF),), (keep, got_a, got_b),
            [pl.BlockSpec((None,) + keep.shape[1:], lambda *_: (1, 0, 0, 0)), VM, VM], (VM,), after=(got,),
        )[0]
        return keep, got, xswap(half)

    def result_rows(firsts, pieces):
        keep, got, far = pieces
        return kernel_call(
            order, functools.partial(result_body, lats), "result", (sds((lats, size, width), BF),),
            (*firsts, scale_rows, shift_rows, keep, got, far, line(attn_out_bias)),
            [VM] * (lats + 2) + [pl.BlockSpec((None,) + keep.shape[1:], lambda *_: (0, 0, 0, 0)), VM, VM, VM], (VM,),
        )[0]

    def second_grad(l, pieces, first, stat):
        keep, got, far = pieces
        spec = part_spec(0, keep.shape)
        row = lat_spec(l, 1, width)
        return kernel_call(
            order, functools.partial(second_grad_body, total_width=total, text_len=text_len), "second_grad_%d" % l,
            (sds((size, width), BF), sds((size, width), F32), sds((text_rows, width), BF), sds((8, width), F32)),
            (keep, got, far, upstream, first, stat, scale_rows, shift_rows),
            [spec, VM, VM, lat_spec(l, size, width), VM, VM, row, row], (VM, VM, VM, VM), hbm=(1, 3),
        )

    def gated_grad(l, blocks, act, spat, before=()):
        n = hidden // tile_cols
        col = pl.BlockSpec((1, tile_cols), lambda j: (0, j))
        wide = pl.BlockSpec((size, tile_cols), lambda j: (0, j))
        joined = len(before)
        return kernel_call(
            order,
            functools.partial(gated_grad_body, lats, len(blocks), joined, width=width, chunk=size // 3),
            "gated_grad_%d" % l,
            (sds((size, total), BF), sds((size, hidden), BF), sds((1, hidden), F32), sds((1, hidden), F32),
             sds((2, 8, LANE) if joined else (8, LANE), F32)),
            (info, *blocks, mixer_contract_weight, act, line(grn_gamma), spat, *before),
            [SM] + [ANY] * len(blocks)
            + [pl.BlockSpec((tile_cols, total), lambda j: (j, 0)), wide, col, col] + [VM] * joined,
            (VM, wide, col, col, VM), grid=(n,), scratch=[pltpu.SemaphoreType.DMA((6,))], hbm=(0, 3),
        )

    def hidden_grad(l, gg, act, slope, spat, s1, tots, crosses, nrm):
        n = total // tile_cols
        return kernel_call(
            order, functools.partial(hidden_grad_body, l, lats, hidden_total, width=width, chunk=32),
            "hidden_grad_%d" % l,
            (sds((size, hidden), BF),) + scatter_shapes(size + EXTRA, width)
            + (sds((1, hidden), F32), sds((1, hidden), F32)),
            (info, gg, act, slope, spat, s1, line(grn_gamma), *tots, *crosses, mixer_expand_weight, nrm),
            [SM] + [VM] * 10 + [lat_spec(l, 8, LANE)] * 4
            + [pl.BlockSpec((tile_cols, hidden), lambda j: (j, 0)), pl.BlockSpec((size, tile_cols), lambda j: (0, j))],
            (VM, ANY, ANY, ANY, ANY, VM, VM), grid=(n,),
            scratch=[
                pltpu.VMEM((size + EXTRA, total), BF),
                pltpu.VMEM((2, size, LANE), F32),
                pltpu.SemaphoreType.DMA((5,)),
            ],
            hbm=(0, 4, 5, 6),
        )

    def conv_backward(l, pieces, conv, stat, first_grad):
        keep, got, far = pieces
        spec = part_spec(0, keep.shape)
        return kernel_call(
            order, functools.partial(conv_backward_body, l, total_width=total), "conv_backward_%d" % l,
            (sds((size, width), BF), sds((16, width), F32)),
            (info, keep, got, far, conv, stat, latents, first_grad, conv_kernel),
            [SM, spec, VM, VM, VM, VM, lat_spec(l, size, width), VM, VM], (VM, VM),
            scratch=[pltpu.VMEM((size + 2 * MARGIN, width), F32)], hbm=(1,),
        )

    half = dp // 2
    split = dp == 8
    if split:
        here = lax.axis_index("dp")
        places = jnp.stack([here // 2, here % 2]).astype(jnp.int32)
    else:
        places = None

    def swap_dp(v, bit):
        return lax.ppermute(v, "dp", [(i, i ^ bit) for i in range(dp)])

    def reduce_start(parts):
        if len(parts) == 1:
            return [lax.psum_scatter(parts[0], "dp", scatter_dimension=0, tiled=True)]
        send, keep = parts
        return [keep, swap_dp(send, 1)]

    def reduce_step(name, state, bit, small=None, after=()):
        if not split:
            return state if small is None else (state, small)
        keep, got = state
        shape = keep.shape[1:] if bit == 4 else (keep.shape[0] // 2,) + keep.shape[1:]
        outs = (sds(shape, BF),) * 2
        args = (keep, got)
        if small is not None:
            args += tuple(small)
            outs += (sds((2 * small[0].shape[0] - SUMMED, width), F32),)
        res = kernel_call(
            order, functools.partial(combine_body, small is not None), name, outs, args, [VM] * len(args),
            (VM,) * len(outs), hbm=(1,), after=after,
        )
        state = [res[1], swap_dp(res[0], bit)]
        if small is not None:
            return state, (res[2], swap_dp(res[2], bit))
        return state

    def reduce_end(name, states, layout, shapes, small=None):
        if not split:
            outs = [jnp.zeros(s, F32) for s in shapes]
            for (part,), plan in zip(states, layout):
                for start, cols, out, offset, flip in plan:
                    block = part[:, start : start + cols].astype(F32)
                    if flip:
                        outs[out] = outs[out].at[offset : offset + cols].set(block.T)
                    else:
                        outs[out] = outs[out].at[:, offset : offset + cols].set(block)
            if small is not None:
                rows = small[0]
                outs.append(lax.psum(rows[:SUMMED], "dp"))
                noise = rows[SUMMED + 4 : SUMMED + 6, : noise_embed.shape[1]].T
                for k in range(2):
                    values = rows[SUMMED + 2 * k : SUMMED + 2 * k + 2]
                    outs.append(lax.psum(jnp.dot(noise, values, precision=highest), "dp"))
            return outs
        args, specs = [], []
        for state in states:
            args += state
            specs += [VM] * len(state)
        outs = tuple(sds(s, F32) for s in shapes)
        if small is not None:
            args += small
            specs += [VM] * len(small)
            outs += (sds((2 * small[0].shape[0] - SUMMED, width), F32),)
            outs += (sds((noise_embed.shape[1], width), F32),) * 2
        return kernel_call(
            order,
            functools.partial(
                finish_body, [len(state) for state in states], len(small) if small is not None else 0, layout
            ),
            name, outs, tuple(args), specs, (VM,) * len(outs),
        )

    def weights(name, sets, cut=True, after=()):
        return weight_grads(order, name, places if cut else None, sets, dp, after)

    assert lats == 2
    share = total // dp
    text_blocks = gather_small(text_act)
    conv0 = conv_forward(0, text_blocks[1:])
    pay10 = gather_start(conv0[0])
    conv1 = conv_forward(1)
    pay11 = gather_start(conv1[0])
    conv = (conv0, conv1)
    text_full, text_low = text_low_rows(text_blocks, ())
    text_low_blocks = gather_small(text_low)
    (far,) = hop(order, "hop_rows_0", pay10[2])
    pay10 = gather_end(pay10, far)
    ffn0 = ffn_in(0, pay10)
    tot0 = gather_small(ffn0[5])
    far, up0 = hop(order, "hop_rows_1", pay11[2], (upstream, 0), after=text_low_blocks[1:])
    pay11 = gather_end(pay11, far)
    up0 = gather_start(up0)
    ffn1 = ffn_in(1, pay11)
    tot1 = gather_small(ffn1[5])
    ffn, tots = (ffn0, ffn1), (tot0, tot1)
    out0 = ffn_out(0, ffn0[2], ffn0[4], tot0, up0[1:])
    gots0 = swap_halves(out0[1:4])
    part0 = scatter_end("add_ffn_0", out0[4], gots0, False, tot1[1:])
    out1 = ffn_out(1, ffn1[2], ffn1[4], tot1)
    gots1 = swap_halves(out1[1:4])
    (up_far,) = hop(order, "hop_upstream", up0[2])
    up0 = gather_end(up0, up_far)
    part1 = scatter_end("add_ffn_1", out1[4], gots1, False)
    gated = (out0[0], out1[0])
    mid0 = middle(0, part0)
    pay20 = gather_start(mid0[1])
    mid1 = middle(1, part1, up0[3:])
    pay21 = gather_start(mid1[1])
    far, up1 = hop(order, "hop_context_0", pay20[2], (upstream, 1))
    pay20 = gather_end(pay20, far)
    up1 = gather_start(up1)
    attn0 = attention(0, pay20, text_low_blocks, up0)
    gots0 = swap_halves(attn0[5:8])
    far, up_far = hop(order, "hop_context_1", pay21[2], up1[2])
    pay21 = gather_end(pay21, far)
    up1 = gather_end(up1, up_far)
    ctx0 = scatter_end("add_ctx_0", attn0[8], gots0, True)
    attn1 = attention(1, pay21, text_low_blocks, up1)
    gots1 = swap_halves(attn1[5:8])
    attn = (attn0, attn1)
    proj = project([attn0[3], attn1[3]])
    outs = swap_halves(proj[:3])
    second0 = second_grad(0, ctx0, mid0[0], attn0[1])
    far30 = xswap(second0[0])
    ctx1 = scatter_end("add_ctx_1", attn1[8], gots1, True)
    out_parts = project_end(proj[3], outs)
    sets = [
        ([(attn[l][0], attn[l][4]) for l in (0, 1)], 0, 3 * width),
        ([(attn[l][2], attn[l][3]) for l in (0, 1)], 0, width),
    ]
    parts_a = weights("attn_weight_grads", sets)
    second1 = second_grad(1, ctx1, mid1[0], attn1[1])
    far31 = xswap(second1[0])
    pay30 = gather_late("hop_first_0", second0[0], far30)
    if split:
        parts_a = (gate(order, "gate_attn", parts_a[0]), parts_a[1])
    sum_a = reduce_start(parts_a)
    gg0 = gated_grad(0, pay30, ffn0[2], ffn0[4])
    pay31 = gather_late("hop_first_1", second1[0], far31)
    gg1 = gated_grad(1, pay31, ffn1[2], ffn1[4], gg0[4:])
    cross = gather_small(gg1[4])
    gg = (gg0, gg1)

    def hidden_of(l, cross):
        return hidden_grad(l, gg[l][1], ffn[l][2], ffn[l][3], ffn[l][4], gg[l][2], tots[l], cross, ffn[l][0])

    near = hidden // 2
    pairs = [(gg[l][0], gated[l]) for l in (0, 1)]
    sum_c0 = reduce_start(weights("contract_weight_grads_0", [(pairs, 0, near)], after=out_parts[2:]))
    hid0 = hidden_of(0, cross)
    gots0 = swap_halves(hid0[1:4])
    sum_a = reduce_step("attn_sums", sum_a, 2)
    in0 = scatter_end("add_in_0", hid0[4], gots0, True)
    texts = [(text_full[0], second0[2]), (text_full[1], second1[2])]
    sum_c1 = reduce_start(weights("contract_weight_grads_1", [(pairs, near, hidden - near), (texts, 0, width)]))
    hid1 = hidden_of(1, cross)
    gots1 = swap_halves(hid1[1:4])
    hid = (hid0, hid1)
    sum_a = reduce_step("attn_sums_b", sum_a, 4)
    pairs = [(ffn[l][0], hid[l][0]) for l in (0, 1)]
    sum_e0 = reduce_start(weights("expand_weight_grads_0", [(pairs, 0, near)]))
    in1 = scatter_end("add_in_1", hid1[4], gots1, True)
    back0 = conv_backward(0, in0, conv[0][1], ffn0[1], second0[1])
    sum_c0 = reduce_step("contract_sums_0", sum_c0, 2)
    sum_e1 = reduce_start(weights("expand_weight_grads_1", [(pairs, near, hidden - near)], after=sum_a[1:]))
    back1 = conv_backward(1, in1, conv[1][1], ffn1[1], second1[1])
    sum_c0 = reduce_step("contract_sums_0b", sum_c0, 4)
    sum_c1 = reduce_step("contract_sums_1", sum_c1, 2)
    packed = kernel_call(
        order, functools.partial(pack_body, lats), "pack", (sds((SUMMED + 8, width), F32),),
        (noise_embed, second0[3], second1[3], attn0[9], attn1[9], hid0[6], hid1[6], gg0[3], gg1[3],
         back0[1], back1[1], hid0[5], hid1[5]),
        [VM] * (1 + 6 * lats), (VM,),
    )[0]
    packed = (packed, swap_dp(packed, 1)) if split else (packed,)
    sum_e0 = reduce_step("expand_sums_0", sum_e0, 2)
    sum_c1 = reduce_step("contract_sums_1b", sum_c1, 4, after=sum_c0[1:])
    grads_a = reduce_end(
        "attn_grads", [sum_a],
        [[(k * width, width, k, 0, False) for k in range(3)] + [(3 * width, width, 3, 0, True)]],
        [(share, width)] * 3 + [(width, share)],
    )
    sum_e1, packed = reduce_step("expand_sums_1", sum_e1, 2, packed)
    sum_e0 = reduce_step("expand_sums_0b", sum_e0, 4)
    result = result_rows([mid0[0], mid1[0]], out_parts)
    sum_e1, packed = reduce_step("expand_sums_1b", sum_e1, 4, packed, after=sum_c1[1:])
    rest = hidden - near
    grads_c = reduce_end(
        "contract_grads", [sum_c0, sum_c1],
        [[(0, near, 0, 0, True)], [(0, rest, 0, near, True), (rest, width, 1, 0, False)]],
        [(hidden, share), (share, width)],
    )
    grads_e = reduce_end(
        "expand_grads", [sum_e0, sum_e1],
        [[(0, near, 0, 0, False)], [(0, rest, 0, near, False)]], [(share, hidden)], packed,
    )
    sums = grads_e[1]
    n = hidden // width
    return (
        result,
        jnp.stack([back0[0], back1[0]]),
        sums[:9],
        sums[9],
        grads_e[0],
        sums[20 : 20 + n].reshape(-1),
        sums[12 : 12 + n].reshape(-1),
        sums[16 : 16 + n].reshape(-1),
        grads_c[0],
        sums[26],
        grads_e[2],
        sums[24],
        grads_e[3],
        sums[25],
        grads_c[1],
        sums[27],
        grads_a[0],
        sums[29],
        grads_a[1],
        grads_a[2],
        sums[30],
        grads_a[3],
        sums[28],
    )


def solution(mesh):
    rows = P("dp", None, "chan")
    weight_in = P(None, "chan")
    vec = P("chan")
    in_specs = (
        rows, P("dp", None), P("dp"), P("dp"), rows, P("dp", None), weight_in, vec, weight_in, vec, vec, vec,
        P("chan", None), vec, weight_in, vec, weight_in, vec, weight_in, vec, weight_in, vec, weight_in,
        weight_in, vec, P("chan", None), vec, rows,
    )
    out_specs = (
        rows, rows, weight_in, vec, P("dp", "chan"), vec, vec, vec, P("chan", "dp"), vec, weight_in, vec,
        weight_in, vec, P("dp", "chan"), vec, P("dp", "chan"), vec, P("dp", "chan"), P("dp", "chan"), vec,
        P("chan", "dp"), vec,
    )
    return jax.shard_map(local, mesh=mesh, in_specs=in_specs, out_specs=out_specs, check_vma=False)
```

```python
import functools

import jax
import jax.numpy as jnp
import numpy as np
from jax import lax
from jax.experimental import pallas as pl
from jax.experimental.pallas import tpu as pltpu
from jax.sharding import PartitionSpec as P

BF = jnp.bfloat16
F32 = jnp.float32
HEAD = 64
LANE = 128
EXTRA = 16
MARGIN = 40
WIDTHS = (36, 24, 18)
EPS = 1e-6

COSTS = {}

VM = pl.BlockSpec(memory_space=pltpu.VMEM)
SM = pl.BlockSpec(memory_space=pltpu.SMEM)
ANY = pl.BlockSpec(memory_space=pl.ANY)


class Order:
    def __init__(self, ordered=True):
        self.ordered = ordered
        self.last = None
        self.pinned = []


def kernel_call(
    order, body, name, outs, args, in_specs, out_specs, grid=(1,), scratch=(), hbm=(), limit=28, after=(), aliases=None
):
    count = len(args)
    args = tuple(
        pltpu.with_memory_space_constraint(a, pltpu.HBM) if any(a is p for p in order.pinned) else a for a in args
    )
    outs = tuple(pltpu.HBM(o.shape, o.dtype) if i in hbm else o for i, o in enumerate(outs))
    if order.ordered:
        if order.last is not None:
            after = (order.last, *after)
        args = tuple(args) + tuple(after)
        in_specs = list(in_specs) + [ANY] * len(after)
    extra = len(args) - count

    def ordered(*refs):
        body(*refs[:count], *refs[count + extra :])

    results = pl.pallas_call(
        ordered,
        name=name,
        out_shape=outs,
        grid=grid,
        in_specs=in_specs,
        out_specs=out_specs,
        scratch_shapes=scratch,
        input_output_aliases=aliases or {},
        compiler_params=pltpu.CompilerParams(vmem_limit_bytes=limit << 20),
        cost_estimate=pl.CostEstimate(flops=COSTS.get(name, 1000), bytes_accessed=1000, transcendentals=0),
    )(*args)
    order.pinned += [results[i] for i in hbm]
    order.last = min(results, key=lambda r: r.size * r.dtype.itemsize)
    return results


def half_rows(rows):
    return (rows // 16 + 1) // 2 * 16


def hop_body(halves, *refs):
    count = len(halves)
    ins, outs, sems = refs[:count], refs[count:-1], refs[-1]
    copies = []
    for ref, half in zip(ins, halves):
        rows = ref.shape[-2]
        h = half_rows(rows) if half else rows
        for part in ((slice(0, h), slice(h, rows)) if half else (slice(0, rows),)):
            at = len(copies)
            if len(ref.shape) > len(outs[at].shape):
                source = ref.at[0]
            else:
                source = ref.at[part] if len(ref.shape) == 2 else ref.at[:, part]
            copies.append(pltpu.make_async_copy(source, outs[at], sems.at[at]))
    run_copies(copies)


def hop(order, name, *arrays, after=()):
    outs, halves, ins, specs = [], [], [], []
    for a in arrays:
        if isinstance(a, tuple):
            a, pick = a
            shape = a.shape if pick is None else a.shape[1:]
            ins.append(a)
            specs.append(
                VM if pick is None
                else pl.BlockSpec((1,) + shape, lambda *_, pick=pick, n=len(shape): (pick,) + (0,) * n)
            )
            halves.append(False)
            outs.append(sds(shape, a.dtype))
        else:
            ins.append(a)
            specs.append(VM)
            halves.append(True)
            h = half_rows(a.shape[-2])
            for rows in (h, a.shape[-2] - h):
                outs.append(sds(a.shape[:-2] + (rows, a.shape[-1]), a.dtype))
    got = list(kernel_call(
        order, functools.partial(hop_body, halves), name, tuple(outs),
        tuple(ins), specs, (ANY,) * len(outs),
        scratch=[pltpu.SemaphoreType.DMA((len(outs),))], after=after,
    ))
    return [(got.pop(0), got.pop(0)) if half else got.pop(0) for half in halves]


def gate(order, name, array):
    def nothing(source, out):
        pass

    return kernel_call(
        order, nothing, name, (sds(array.shape, array.dtype),), (array,), [ANY], (ANY,), aliases={0: 0}
    )[0]


def sds(shape, dtype):
    return jax.ShapeDtypeStruct(shape, dtype)


def nn(a, b):
    return jnp.dot(a, b, preferred_element_type=F32)


def nt(a, b):
    return lax.dot_general(a, b, (((1,), (1,)), ((), ())), preferred_element_type=F32)


def tn(a, b):
    return lax.dot_general(a, b, (((0,), (0,)), ((), ())), preferred_element_type=F32)


def eye():
    return (
        lax.broadcasted_iota(jnp.int32, (LANE, LANE), 0)
        == lax.broadcasted_iota(jnp.int32, (LANE, LANE), 1)
    ).astype(F32)


def col_to_tile(col):
    size = col.shape[0]
    diag = eye()
    row = lax.broadcasted_iota(jnp.int32, (8, LANE), 0)
    tile = jnp.zeros((8, LANE), F32)
    for t in range(pl.cdiv(size, LANE)):
        n = min(LANE, size - t * LANE)
        line = jnp.sum(col[t * LANE : t * LANE + n] * diag[:n], axis=0, keepdims=True)
        tile = jnp.where(row == t, line, tile)
    return tile


def tile_to_col(tile, size):
    diag = eye()
    cols = []
    for t in range(pl.cdiv(size, LANE)):
        n = min(LANE, size - t * LANE)
        cols.append(jnp.sum(tile[t : t + 1] * diag[:n], axis=1, keepdims=True))
    return jnp.concatenate(cols, axis=0)


def split_stats(both):
    high = both.astype(BF)
    rest = both - high.astype(F32)
    mid = rest.astype(BF)
    low = (rest - mid.astype(F32)).astype(BF)
    return jnp.concatenate([high, mid, low], axis=1)


def join_stats(tile):
    wide = tile.astype(F32)
    return wide[:, :LANE] + wide[:, LANE : 2 * LANE] + wide[:, 2 * LANE : 3 * LANE]


def stats_tile(first, second):
    return split_stats(jnp.concatenate([col_to_tile(first), col_to_tile(second)], axis=0))


def block_copies(me, refs, dst, sems, width, base=0, first_sem=0):
    rows = refs[0].shape[0]
    h = half_rows(rows)
    if len(refs) == 6:
        plan = ((0, 0, rows), (2, 0, rows), (3, 0, h), (3, h, rows - h), (1, 0, h), (1, h, rows - h))
    else:
        plan = ((0, 0, rows), (1, 0, rows), (2, 0, rows))
        plan += ((3, 0, rows),) if len(refs) == 4 else ((3, 0, h), (3, h, rows - h))
    copies = []
    for i, (ref, (k, start, size)) in enumerate(zip(refs, plan)):
        place = pl.multiple_of((me ^ k) * width, LANE)
        target = dst.at[pl.ds(base + start, size), pl.ds(place, width)]
        copies.append(pltpu.make_async_copy(ref, target, sems.at[first_sem + i]))
    return copies


def scatter_copies(me, part, outs, sems, width):
    send, send_a, send_b, keep = outs
    rows = part.shape[0]
    h = half_rows(rows)
    plan = ((0, 0, rows, keep.at[0]), (2, 0, rows, keep.at[1]), (1, 0, rows, send), (3, 0, h, send_a), (3, h, rows - h, send_b))
    copies = []
    for i, (k, start, size, dst) in enumerate(plan):
        place = pl.multiple_of((me ^ k) * width, LANE)
        source = part.at[pl.ds(start, size), pl.ds(place, width)]
        copies.append(pltpu.make_async_copy(source, dst, sems.at[i]))
    return copies


def scatter_shapes(rows, width):
    h = half_rows(rows)
    return (
        sds((rows, width), BF), sds((h, width), BF), sds((rows - h, width), BF), sds((2, rows, width), BF)
    )


def run_copies(copies):
    for c in copies:
        c.start()
    for c in copies:
        c.wait()


def norm_rows(raw, out, stat, size, width, blocks):
    total = width * blocks
    means = []
    for b in range(blocks):
        means.append(tile_to_col(raw[size : size + 8, b * width : b * width + LANE].astype(F32), size))
    mean_sum = jnp.zeros((size, 1), F32)
    for b in range(blocks):
        part = raw[:size, b * width : (b + 1) * width].astype(F32)
        mean_sum = mean_sum + jnp.sum(part, axis=1, keepdims=True) + width * means[b]
    mean = mean_sum * (1.0 / total)
    square = jnp.zeros((size, 1), F32)
    for b in range(blocks):
        part = raw[:size, b * width : (b + 1) * width].astype(F32) + (means[b] - mean)
        square = square + jnp.sum(part * part, axis=1, keepdims=True)
    inverse = lax.rsqrt(square * (1.0 / total) + EPS)
    for b in range(blocks):
        part = raw[:size, b * width : (b + 1) * width].astype(F32) + (means[b] - mean)
        out[:size, b * width : (b + 1) * width] = (part * inverse).astype(BF)
    stat[0] = jnp.broadcast_to(mean, (size, LANE))
    stat[1] = jnp.broadcast_to(inverse, (size, LANE))


def send_rows(values, pay, size, width):
    mean = jnp.mean(values, axis=1, keepdims=True).astype(BF).astype(F32)
    pay[:size] = (values - mean).astype(BF)
    tile = col_to_tile(mean).astype(BF)
    pay[size:] = jnp.zeros((EXTRA, width), BF)
    pay[size : size + EXTRA, :LANE] = jnp.concatenate([tile, jnp.zeros((8, LANE), BF)], axis=0)


def column_masks(size, width):
    slot = lax.broadcasted_iota(jnp.int32, (size, 1), 0).astype(F32)
    col = slot - width * jnp.floor((slot + 0.5) * (1.0 / width))
    return col > 0.5, col < width - 1.5


def conv_forward_body(l, info, x_ref, taps, bias, pay, conv, pad):
    size, width = conv.shape
    slot = lax.broadcasted_iota(jnp.int32, (size, 1), 0)
    x = jnp.where(slot < info[l, 0], x_ref[...].astype(F32), 0.0)
    pad[:MARGIN] = jnp.zeros((MARGIN, width), F32)
    pad[MARGIN + size :] = jnp.zeros((MARGIN, width), F32)
    here = slice(MARGIN, MARGIN + size)
    for bucket, w in enumerate(WIDTHS):

        @pl.when(info[l, 1] == bucket)
        def _():
            not_first, not_last = column_masks(size, w)
            pad[here] = x
            left = jnp.where(not_first, pad[MARGIN - 1 : MARGIN - 1 + size], 0.0)
            right = jnp.where(not_last, pad[MARGIN + 1 : MARGIN + 1 + size], 0.0)
            total = bias[...] + left * taps[3:4] + x * taps[4:5] + right * taps[5:6]
            pad[here] = left * taps[0:1] + x * taps[1:2] + right * taps[2:3]
            total = total + pad[MARGIN - w : MARGIN - w + size]
            pad[here] = left * taps[6:7] + x * taps[7:8] + right * taps[8:9]
            conv[...] = total + pad[MARGIN + w : MARGIN + w + size]

    send_rows(conv[...], pay, size, width)


def conv_backward_body(l, info, keep, got, far, conv, stat, x_ref, first_grad, taps, out, sums, pad, total_width):
    size, width = conv.shape
    slot = lax.broadcasted_iota(jnp.int32, (size, 1), 0)
    mask = slot < info[l, 0]
    grad = keep[:size].astype(F32) + got[:size].astype(F32) + far[:size].astype(F32)
    both = join_stats(keep[size:]) + join_stats(got[size:]) + join_stats(far[size:])
    both = both * (1.0 / total_width)
    mean_grad = tile_to_col(both[:8], size)
    mean_cross = tile_to_col(both[8:], size)
    mean = stat[0][:, :1]
    inverse = stat[1][:, :1]
    normed = (conv[...] - mean) * inverse
    grad = inverse * (grad - mean_grad - normed * mean_cross)
    x = jnp.where(mask, x_ref[...].astype(F32), 0.0)
    pad[:MARGIN] = jnp.zeros((MARGIN, width), F32)
    pad[MARGIN + size :] = jnp.zeros((MARGIN, width), F32)
    here = slice(MARGIN, MARGIN + size)
    sums[...] = jnp.zeros_like(sums)
    sums[9:10] = jnp.sum(grad, axis=0, keepdims=True)
    for bucket, w in enumerate(WIDTHS):

        @pl.when(info[l, 1] == bucket)
        def _():
            not_first, not_last = column_masks(size, w)
            pad[here] = x
            left = jnp.where(not_first, pad[MARGIN - 1 : MARGIN - 1 + size], 0.0)
            right = jnp.where(not_last, pad[MARGIN + 1 : MARGIN + 1 + size], 0.0)
            pad[here] = grad
            rows = (pad[MARGIN + w : MARGIN + w + size], grad, pad[MARGIN - w : MARGIN - w + size])
            for r in range(3):
                for c, side in enumerate((left, x, right)):
                    tap = 3 * r + c
                    sums[tap : tap + 1] = jnp.sum(rows[r] * side, axis=0, keepdims=True)
            back = [sum(rows[r] * taps[3 * r + c : 3 * r + c + 1] for r in range(3)) for c in range(3)]
            pad[here] = jnp.where(not_first, back[0], 0.0)
            total = back[1] + pad[MARGIN + 1 : MARGIN + 1 + size]
            pad[here] = jnp.where(not_last, back[2], 0.0)
            total = total + pad[MARGIN - 1 : MARGIN - 1 + size]
            out[...] = (first_grad[...] + jnp.where(mask, total, 0.0)).astype(BF)


def gelu_both(h):
    t_den = 1.0 + (0.3275911 * 0.7071067811865476) * jnp.abs(h)
    t = pl.reciprocal(t_den, approx=True)
    t = t * (2.0 - t_den * t)
    bell = jnp.exp(-0.5 * h * h)
    poly = t * (
        0.127414796 + t * (-0.142248368 + t * (0.7107068705 + t * (-0.7265760135 + t * 0.5307027145)))
    )
    tail = poly * bell
    phi = jnp.where(h >= 0, 1.0 - tail, tail)
    return h * phi, phi + h * bell * 0.3989422804014327


def ffn_in_body(
    l, lats, count, info, *refs, width, chunk
):
    blocks, (w, bias, nrm, stat, act, slope, spat, total, raw, sems) = refs[:count], refs[count:]
    j = pl.program_id(0)
    size = nrm.shape[0]

    @pl.when(j == 0)
    def _():
        run_copies(block_copies(info[lats, 0], blocks, raw, sems, width))
        norm_rows(raw, nrm, stat, size, width, 4)
        total[...] = jnp.zeros_like(total)

    valid_from = size - size // 32
    cols = act.shape[1]
    square = jnp.zeros((1, cols), F32)
    for r in range(0, size, chunk):
        h = nn(nrm[r : r + chunk], w[...]) + bias[...]
        a, d = gelu_both(h)
        act[r : r + chunk] = a.astype(BF)
        slope[r : r + chunk] = d.astype(BF)
        sq = a * a
        if r + chunk > valid_from:
            slot = r + lax.broadcasted_iota(jnp.int32, (chunk, 1), 0)
            sq = jnp.where(slot < info[l, 0], sq, 0.0)
        square = square + jnp.sum(sq, axis=0, keepdims=True)
    here = jnp.sqrt(square)
    spat[...] = here
    total[...] = total[...] + jnp.sum(here)


def denominator(t0, t1, t2, t3, hidden_total):
    whole = t0[...] + t1[...] + t2[...] + t3[...]
    return whole[:1, :1] * (1.0 / hidden_total) + EPS


def ffn_out_body(lats, hidden_total, info, act, spat, t0, t1, t2, t3, gamma, beta, w, gated, s0, s1, s2, keep, part, sems, width, chunk):
    j = pl.program_id(0)
    size = act.shape[0]

    @pl.when(j == 0)
    def _():
        gain = 1.0 + gamma[...] * (spat[...] / denominator(t0, t1, t2, t3, hidden_total))
        for r in range(0, size, chunk):
            rows = slice(r, r + chunk)
            gated[rows] = (act[rows].astype(F32) * gain + beta[...]).astype(BF)

    cols = w.shape[1]
    part[:, pl.ds(pl.multiple_of(j * cols, LANE), cols)] = nn(gated[...], w[...]).astype(BF)

    @pl.when(j == pl.num_programs(0) - 1)
    def _():
        run_copies(scatter_copies(info[lats, 0], part, (s0, s1, s2, keep), sems, width))


def add_body(stats, keep, got_a, got_b, out):
    h = got_a.shape[0]
    size = out.shape[0] - (EXTRA if stats else 0)
    out[:h] = (keep[:h].astype(F32) + got_a[...].astype(F32)).astype(BF)
    out[h:size] = (keep[h:size].astype(F32) + got_b[: size - h].astype(F32)).astype(BF)
    if stats:
        out[size:] = split_stats(join_stats(keep[size:]) + join_stats(got_b[size - h :]))


def middle_body(x, keep, got, far, out_bias, scale, shift, first, pay):
    size, width = first.shape
    value = x[...].astype(F32) + (
        keep[...].astype(F32) + got[...].astype(F32) + far[...].astype(F32) + out_bias[...]
    )
    first[...] = value
    send_rows(value * (1.0 + scale[...]) + shift[...], pay, size, width)


def text_body(lats, info, b0, b1, b2, b3, w, bias, full, low, sems, width, text_len):
    lat_count, rows, _ = low.shape
    copies = []
    for l in range(lat_count):
        refs = [b.at[l] for b in (b0, b1, b2, b3)]
        copies += block_copies(info[lats, 0], refs, full.at[l], sems, width, first_sem=4 * l)
    run_copies(copies)
    row = lax.broadcasted_iota(jnp.int32, (rows, 1), 0)
    for l in range(lat_count):
        low[l] = jnp.where(row < text_len, nn(full[l], w[...]) + bias[...], 0.0).astype(BF)


def attention_body(
    l, lats, counts, info, *refs, width
):
    pays, refs = refs[: counts[0]], refs[counts[0] :]
    texts, refs = refs[: counts[1]], refs[counts[1] :]
    grads, refs = refs[: counts[2]], refs[counts[2] :]
    (
    wq, wk, wv, wo, q_bias, v_bias, ctx_out, stat_out, g_out, att_out, dqkv_out, s0, s1, s2, keep, sums,
    raw, w_all, w_out, q_s, k_s, v_s, do_s, kt_s, vt_s, att_t, dq_t, scores, part, ctx, stat, g_full, att, dqkv, sems,
    ) = refs
    leaving = [
        pltpu.make_async_copy(source, dst, sems.at[19 + i])
        for i, (source, dst) in enumerate(
            ((ctx, ctx_out), (stat, stat_out), (g_full, g_out), (att, att_out), (dqkv, dqkv_out))
        )
    ]
    me = info[lats, 0]
    size = att.shape[0]
    rows = ctx.shape[0]
    total = ctx.shape[1]
    text = rows - size
    factor = HEAD ** (-0.5)
    copy_in = block_copies(me, pays, raw, sems, width)
    copy_in += block_copies(me, [x.at[l] for x in texts], ctx, sems, width, base=size, first_sem=5)
    copy_w = [
        pltpu.make_async_copy(ref, w_all.at[:, k * width : (k + 1) * width], sems.at[10 + k])
        for k, ref in enumerate((wq, wk, wv))
    ]
    copy_g = [pltpu.make_async_copy(wo, w_out, sems.at[13])]
    copy_g += block_copies(me, grads, g_full, sems, width, first_sem=14)
    for c in copy_in + copy_w + copy_g:
        c.start()
    for c in copy_in:
        c.wait()
    norm_rows(raw, ctx, stat, size, width, 4)
    leaving[0].start()
    leaving[1].start()
    for c in copy_w:
        c.wait()
    q_s[...] = ((nn(ctx[:size], w_all[:, :width]) + q_bias[...]).astype(BF).astype(F32) * factor).astype(BF)
    keys = nn(ctx[...], w_all[:, width : 2 * width]).astype(BF)
    k_s[...] = keys
    kt_s[...] = keys.T
    values = (nn(ctx[...], w_all[:, 2 * width :]) + v_bias[...]).astype(BF)
    v_s[...] = values
    vt_s[...] = values.T
    for c in copy_g:
        c.wait()
    leaving[2].start()
    do_s[...] = nt(g_full[...], w_out[...]).astype(BF)
    tail = (size - size // 32) // 8 * 8
    key_row = tail + lax.broadcasted_iota(jnp.int32, (rows - tail, 1), 0)
    key_ok = (key_row < info[l, 0]) | ((key_row >= size) & (key_row < size + info[l, 2]))

    def pair(p, carry):
        lo = pl.multiple_of(p * LANE, LANE)
        q2 = q_s[:, pl.ds(lo, LANE)]
        k2 = k_s[:, pl.ds(lo, LANE)]
        v2 = v_s[:, pl.ds(lo, LANE)]
        do2 = do_s[:, pl.ds(lo, LANE)]
        dks, dvs = [], []
        heads = []
        for half in range(2):
            lanes = slice(half * HEAD, (half + 1) * HEAD)
            line = pl.ds(pl.multiple_of(p * LANE + half * HEAD, HEAD), HEAD)
            heads.append((line, q2[:, lanes], k2[:, lanes], v2[:, lanes], do2[:, lanes]))
        for half, (line, qh, kh, vh, doh) in enumerate(heads):
            scores[half] = nt(kh, qh)
            scores[half, tail:] = jnp.where(key_ok, scores[half, tail:], -1e30)
        lows = []
        for half in range(2):
            top = jnp.max(scores[half], axis=0, keepdims=True)
            expo = jnp.exp(scores[half] - top)
            probs = expo * (1.0 / jnp.sum(expo, axis=0, keepdims=True))
            scores[half] = probs
            lows.append(probs.astype(BF))
        for half, (line, qh, kh, vh, doh) in enumerate(heads):
            att_t[line] = nn(vt_s[line], lows[half])
            dvs.append(nn(lows[half], doh))
            grad_p = nt(vh, doh)
            dot = jnp.sum(scores[half] * grad_p, axis=0, keepdims=True)
            grad_s = (scores[half] * (grad_p - dot)).astype(BF)
            dks.append(nn(grad_s, qh))
            dq_t[line] = nn(kt_s[line], grad_s) * factor
        dqkv[:, pl.ds(pl.multiple_of(width + lo, LANE), LANE)] = jnp.concatenate(dks, axis=1).astype(BF)
        dqkv[:, pl.ds(pl.multiple_of(2 * width + lo, LANE), LANE)] = jnp.concatenate(dvs, axis=1).astype(BF)
        return carry

    lax.fori_loop(0, width // LANE, pair, 0)
    att[...] = att_t[...].astype(BF).T
    leaving[3].start()
    dq = dq_t[...].astype(BF).T
    dqkv[:size, :width] = dq
    dqkv[size:, :width] = jnp.zeros((text, width), BF)
    leaving[4].start()
    sums[...] = jnp.zeros_like(sums)
    sums[0:1] = jnp.sum(dq.astype(F32), axis=0, keepdims=True)
    sums[1:2] = jnp.sum(dqkv[:, 2 * width :].astype(F32), axis=0, keepdims=True)
    first = jnp.zeros((size, 1), F32)
    second = jnp.zeros((size, 1), F32)
    cols = 256
    for n in range(0, total, cols):
        block = nt(dqkv[...], w_all[n : n + cols]).astype(BF)
        part[:rows, n : n + cols] = block
        wide = block[:size].astype(F32)
        first = first + jnp.sum(wide, axis=1, keepdims=True)
        second = second + jnp.sum(wide * ctx[:size, n : n + cols].astype(F32), axis=1, keepdims=True)
    tile = stats_tile(first, second)
    for b in range(4):
        part[rows:, b * width : (b + 1) * width] = tile
    run_copies(scatter_copies(me, part, (s0, s1, s2, keep), sems, width))
    for c in leaving:
        c.wait()


def project_body(lats, info, *refs):
    atts, w, outs, part, sems = refs[:lats], refs[lats], refs[lats + 1 : lats + 5], refs[-2], refs[-1]
    width = atts[0].shape[1]
    cols = 512
    copies = []
    for l in range(lats):
        for n in range(0, part.shape[2], cols):
            part[l, :, n : n + cols] = nn(atts[l][...], w[:, n : n + cols]).astype(BF)
        views = [o.at[l] for o in outs[:3]] + [outs[3].at[:, l]]
        copies += scatter_copies(info[lats, 0], part.at[l], views, sems.at[l], width)
        for c in copies[-5:]:
            c.start()
    for c in copies:
        c.wait()


def add_out_body(keep, got_a, got_b, out):
    h = got_a.shape[1]
    out[:, :h] = (keep[:, :h].astype(F32) + got_a[...].astype(F32)).astype(BF)
    out[:, h:] = (keep[:, h:].astype(F32) + got_b[...].astype(F32)).astype(BF)


def result_body(lats, *refs):
    firsts, (scale, shift, keep, got, far, bias, out) = refs[:lats], refs[lats:]
    for l in range(lats):
        second = firsts[l][...] * (1.0 + scale[l]) + shift[l]
        branch = keep[l].astype(F32) + got[l].astype(F32) + far[l].astype(F32) + bias[...]
        out[l] = (second + branch).astype(BF)


def second_grad_body(keep, got, far, g_ref, first_ref, stat, scale, shift, pay, first_grad, text, sums, total_width, text_len):
    size, width = first_grad.shape
    rows = keep.shape[0] - EXTRA
    both = join_stats(keep[rows:]) + join_stats(got[rows:]) + join_stats(far[rows:])
    both = both * (1.0 / total_width)
    mean_grad = tile_to_col(both[:8], size)
    mean_cross = tile_to_col(both[8:], size)
    grad = keep[:size].astype(F32) + got[:size].astype(F32) + far[:size].astype(F32)
    first = first_ref[...]
    gain = 1.0 + scale[...]
    inverse = stat[1][:, :1]
    normed = (first * gain + shift[...] - stat[0][:, :1]) * inverse
    upstream = g_ref[...].astype(F32)
    second_grad = upstream + inverse * (grad - mean_grad - normed * mean_cross)
    scaled = second_grad * gain
    pay[...] = scaled.astype(BF)
    first_grad[...] = scaled
    row = lax.broadcasted_iota(jnp.int32, (rows - size, 1), 0)
    tail = keep[size:rows].astype(F32) + got[size:rows].astype(F32) + far[size:rows].astype(F32)
    low = jnp.where(row < text_len, tail, 0.0).astype(BF)
    text[...] = low
    sums[...] = jnp.zeros_like(sums)
    sums[0:1] = jnp.sum(second_grad * first, axis=0, keepdims=True)
    sums[1:2] = jnp.sum(second_grad, axis=0, keepdims=True)
    sums[2:3] = jnp.sum(scaled, axis=0, keepdims=True)
    sums[3:4] = jnp.sum(low.astype(F32), axis=0, keepdims=True)
    sums[4:5] = jnp.sum(upstream, axis=0, keepdims=True)


def gated_grad_body(lats, count, joined, info, *refs, width, chunk):
    blocks, (w, act, gamma, spat, *refs) = refs[:count], refs[count:]
    if joined:
        before, *refs = refs
    full, out, s1, s2, both, sems = refs
    total = both.at[1] if joined else both
    j = pl.program_id(0)
    size = full.shape[0]

    @pl.when(j == 0)
    def _():
        run_copies(block_copies(info[lats, 0], blocks, full, sems, width))
        total[...] = jnp.zeros((8, LANE), F32)
        if joined:
            both[0] = before[...]

    cols = out.shape[1]
    cross = jnp.zeros((1, cols), F32)
    plain = jnp.zeros((1, cols), F32)
    for r in range(0, size, chunk):
        grad = nt(full[r : r + chunk], w[...])
        out[r : r + chunk] = grad.astype(BF)
        cross = cross + jnp.sum(grad * act[r : r + chunk].astype(F32), axis=0, keepdims=True)
        plain = plain + jnp.sum(grad, axis=0, keepdims=True)
    s1[...] = cross
    s2[...] = plain
    total[...] = total[...] + jnp.sum(cross * gamma[...] * spat[...])


def hidden_grad_body(
    l, lats, hidden_total, info, gg, act, slope, spat, s1, gamma, t0, t1, t2, t3, c0, c1, c2, c3, w, nrm,
    hidden, d0, d1, d2, keep, bias_sum, gamma_sum, part, acc, sems, width, chunk,
):
    j = pl.program_id(0)
    size = hidden.shape[0]

    @pl.when(j == 0)
    def _():
        den = denominator(t0, t1, t2, t3, hidden_total)
        cross = (c0[...] + c1[...] + c2[...] + c3[...])[:1, :1]
        response = spat[...] / den
        gamma_sum[...] = response * s1[...]
        grad_spat = gamma[...] * s1[...] / den - cross / (den * den) * (1.0 / hidden_total)
        gain = gamma[...] * response + 1.0
        pull = grad_spat / spat[...]
        total = jnp.zeros_like(bias_sum[...])
        for r in range(0, size, chunk):
            rows = slice(r, r + chunk)
            slot = r + lax.broadcasted_iota(jnp.int32, (chunk, 1), 0)
            active = jnp.where(slot < info[l, 0], act[rows].astype(F32), 0.0)
            grad = gg[rows].astype(F32) * gain + pull * active
            low = (grad * slope[rows].astype(F32)).astype(BF)
            hidden[rows] = low
            total = total + jnp.sum(low.astype(F32), axis=0, keepdims=True)
        bias_sum[...] = total
        acc[...] = jnp.zeros_like(acc)

    cols = w.shape[0]
    block = nt(hidden[...], w[...]).astype(BF)
    part[:size, pl.ds(pl.multiple_of(j * cols, LANE), cols)] = block
    wide = block.astype(F32)
    acc[0] = acc[0] + jnp.sum(wide, axis=1, keepdims=True)
    acc[1] = acc[1] + jnp.sum(wide * nrm[...].astype(F32), axis=1, keepdims=True)

    @pl.when(j == pl.num_programs(0) - 1)
    def _():
        tile = stats_tile(acc[0][:, :1], acc[1][:, :1])
        for b in range(4):
            part[size:, b * width : (b + 1) * width] = tile
        run_copies(scatter_copies(info[lats, 0], part, (d0, d1, d2, keep), sems, width))


def weight_grad_body(sets, split, width, dp, *refs):
    if split:
        places, refs = refs[0], refs[1:]
    count = sum(n for n, _, _ in sets)
    lefts, rights, refs = refs[:count], refs[count : 2 * count], refs[2 * count :]
    outs, refs = refs[: 2 if split else 1], refs[2 if split else 1 :]
    bufs, (stage, sems) = refs[:-2], refs[-2:]
    parts = width // (2 * (width // dp)) if split else 4
    chunk = width // parts
    share = width // dp
    used = 0
    coming = []
    at = 0
    for i, (n, start, cols) in enumerate(sets):
        lbuf, rbuf = bufs[2 * i], bufs[2 * i + 1]
        row = 0
        firsts, chunks = [], [[] for _ in range(parts)]
        for k in range(at, at + n):
            rows = lefts[k].shape[0]
            here = pl.ds(row, rows)
            firsts.append(
                pltpu.make_async_copy(rights[k].at[:, pl.ds(start, cols)], rbuf.at[here], sems.at[used])
            )
            used += 1
            for c in range(parts):
                lanes = pl.ds(c * chunk, chunk)
                chunks[c].append(
                    pltpu.make_async_copy(lefts[k].at[:, lanes], lbuf.at[here, lanes], sems.at[used])
                )
                used += 1
            row += rows
        coming.append((firsts, chunks))
        at += n
    for firsts, _ in coming:
        for c in firsts:
            c.start()
    for c in range(parts):
        for _, chunks in coming:
            for copy in chunks[c]:
                copy.start()
    leaving = []
    for c in range(parts):
        off = 0
        for i, (n, start, cols) in enumerate(sets):
            firsts, chunks = coming[i]
            for copy in (firsts if c == 0 else []) + chunks[c]:
                copy.wait()
            block = tn(bufs[2 * i][:, c * chunk : (c + 1) * chunk], bufs[2 * i + 1][...]).astype(BF)
            if split:
                near, far = block[:share], block[share:]
                flip = places[1] == 1
                stage[0, c, :, off : off + cols] = jnp.where(flip, near, far)
                stage[1, c, :, off : off + cols] = jnp.where(flip, far, near)
            else:
                stage[c * chunk : (c + 1) * chunk, off : off + cols] = block
            off += cols
        if split:
            for k in range(2):
                leaving.append(
                    pltpu.make_async_copy(stage.at[k, c], outs[k].at[places[0] ^ c], sems.at[used])
                )
                used += 1
        else:
            rows = pl.ds(c * chunk, chunk)
            leaving.append(pltpu.make_async_copy(stage.at[rows], outs[0].at[rows], sems.at[used]))
            used += 1
        for copy in leaving[-2 if split else -1 :]:
            copy.start()
    for copy in leaving:
        copy.wait()


def weight_grads(order, name, places, sets, dp, after=()):
    split = places is not None
    lefts = [l for pairs, _, _ in sets for l, _ in pairs]
    rights = [r for pairs, _, _ in sets for _, r in pairs]
    width = lefts[0].shape[1]
    wide = sum(cols for _, _, cols in sets)
    scratch = []
    for pairs, _, cols in sets:
        depth = sum(l.shape[0] for l, _ in pairs)
        scratch += [pltpu.VMEM((depth, width), BF), pltpu.VMEM((depth, cols), BF)]
    share = width // dp
    if split:
        outs = (sds((dp // 2, share, wide), BF),) * 2
        scratch.append(pltpu.VMEM((2, dp // 2, share, wide), BF))
    else:
        outs = (sds((width, wide), BF),)
        scratch.append(pltpu.VMEM((width, wide), BF))
    scratch.append(pltpu.SemaphoreType.DMA((5 * len(lefts) + 8,)))
    plan = [(len(pairs), start, cols) for pairs, start, cols in sets]
    args = ((places,) if split else ()) + (*lefts, *rights)
    return kernel_call(
        order, functools.partial(weight_grad_body, plan, split, width, dp), name, outs, args,
        ([SM] if split else []) + [ANY] * (2 * len(lefts)), (ANY,) * len(outs), scratch=scratch,
        hbm=(1,) if split else (0,), limit=40, after=after,
    )


SUMMED = 32


def join_small(mine, near, out):
    out[:SUMMED] = mine[:SUMMED] + near[:SUMMED]
    rest = mine.shape[0] - SUMMED
    out[SUMMED : SUMMED + rest] = mine[SUMMED:]
    out[SUMMED + rest :] = near[SUMMED:]


def combine_body(small, keep, got, *refs):
    if small:
        mine, near, *outs, whole = refs
        join_small(mine, near, whole)
    else:
        outs = refs
    count = keep.shape[0]
    for k in range(count):
        total = (keep[k].astype(F32) + got[k].astype(F32)).astype(BF)
        if count == 2:
            outs[1 - k][...] = total
        else:
            outs[1 - k % 2][k // 2] = total


def finish_body(counts, small, layout, *refs):
    chunks = []
    at = 0
    for n in counts:
        chunks.append(refs[at : at + n])
        at += n
    extra = refs[at : at + small]
    outs = refs[at + small :]
    for ins, plan in zip(chunks, layout):
        for start, cols, out, offset, flip in plan:
            lanes = slice(start, start + cols)
            total = 0.0
            for ref in ins:
                total = total + ref[:, lanes].astype(F32)
            if flip:
                outs[out][offset : offset + cols] = total.T
            else:
                outs[out][:, offset : offset + cols] = total
    if small:
        *outs, whole, scale, shift = outs
        join_small(*extra, whole)
        rows = whole.shape[0] - SUMMED
        r = scale.shape[0]
        lines = [whole[SUMMED + b : SUMMED + b + 8] for b in range(0, rows, 8)]
        noise = jnp.concatenate([x[4:6, :r] for x in lines], axis=0)
        for k, out in enumerate((scale, shift)):
            values = jnp.concatenate([x[2 * k : 2 * k + 2] for x in lines], axis=0)
            out[...] = lax.dot_general(
                noise, values, (((0,), (0,)), ((), ())), precision=lax.Precision.HIGHEST, preferred_element_type=F32
            )


def pack_body(lat_count, noise, *refs):
    second, attn, gam, bet, conv, hid = (refs[k * lat_count : (k + 1) * lat_count] for k in range(6))
    out = refs[-1]
    width = out.shape[1]
    out[:16] = sum(c[...] for c in conv)
    out[24:] = jnp.zeros((out.shape[0] - 24, width), F32)
    for k, group in enumerate((gam, bet, hid)):
        whole = sum(g[...] for g in group)
        for b in range(whole.shape[1] // width):
            at = 12 + 4 * k + b
            out[at : at + 1] = whole[:, b * width : (b + 1) * width]
    for i in range(5):
        out[24 + i : 25 + i] = sum(second[l][i : i + 1] for l in range(lat_count))
    for i in range(2):
        out[29 + i : 30 + i] = sum(attn[l][i : i + 1] for l in range(lat_count))
    for l in range(lat_count):
        out[SUMMED + l : SUMMED + l + 1] = second[l][0:1]
        out[SUMMED + 2 + l : SUMMED + 3 + l] = second[l][1:2]
        out[SUMMED + 4 + l : SUMMED + 5 + l, : noise.shape[1]] = noise[l : l + 1]


def local(
    latents, valid_mask, bucket_ids, text_count, text_tokens, noise_embed, conv_kernel, conv_bias,
    mixer_expand_weight, ffn_in_bias, grn_gamma, grn_beta, mixer_contract_weight, ffn_out_bias,
    scale_weight, scale_bias, shift_weight, shift_bias, text_weight, text_bias, query_weight, query_bias,
    key_weight, value_weight, value_bias, attn_out, attn_out_bias, upstream,
):
    lats, size, width = latents.shape
    groups = lax.axis_size("chan")
    dp = lax.axis_size("dp")
    total = width * groups
    hidden = mixer_expand_weight.shape[1]
    hidden_total = hidden * groups
    text_len = text_tokens.shape[1]
    text_rows = pl.cdiv(text_len, 16) * 16
    rows = size + text_rows
    highest = lax.Precision.HIGHEST
    me = lax.axis_index("chan")
    order = Order()
    order.pinned += [
        mixer_expand_weight, mixer_contract_weight, text_weight, query_weight, key_weight, value_weight, attn_out,
        latents, upstream,
    ]

    def xswap(v):
        return lax.ppermute(v, "chan", [(i, i ^ 2) for i in range(groups)])

    def cswap(v):
        return lax.ppermute(v, "chan", [(i, i ^ 1) for i in range(groups)])

    def gather_start(v):
        return v, cswap(v), xswap(v)

    def gather_end(state, halves):
        return (*state, *(cswap(h) for h in halves))

    def gather_late(name, v, far):
        far_parts, own_parts = hop(order, name, far, v)
        return (v, far, *(cswap(h) for h in far_parts), *(cswap(h) for h in own_parts))

    def gather_small(v):
        return v, cswap(v), xswap(v), lax.ppermute(v, "chan", [(i, i ^ 3) for i in range(groups)])

    def line(v):
        return v.reshape(1, -1)

    info = jnp.stack(
        [jnp.sum(valid_mask, axis=1), bucket_ids, text_count, jnp.zeros_like(bucket_ids)], axis=1
    )
    info = jnp.concatenate([info, jnp.full((1, 4), me, jnp.int32)], axis=0).astype(jnp.int32)

    def lat_spec(l, *shape):
        return pl.BlockSpec((None,) + shape, lambda *_: (l,) + (0,) * len(shape))

    def part_spec(k, shape):
        return pl.BlockSpec((None,) + tuple(shape[1:]), lambda *_: (k, 0, 0))

    text_act = jax.nn.silu(text_tokens.astype(F32)).astype(BF)
    text_act = jnp.pad(text_act, ((0, 0), (0, text_rows - text_len), (0, 0)))

    def conv_forward(l, after=()):
        return kernel_call(
            order, functools.partial(conv_forward_body, l), "conv_forward_%d" % l,
            (sds((size + EXTRA, width), BF), sds((size, width), F32)),
            (info, latents, conv_kernel, line(conv_bias)),
            [SM, lat_spec(l, size, width), VM, VM], (VM, VM),
            scratch=[pltpu.VMEM((size + 2 * MARGIN, width), F32)], hbm=(1,), after=after,
        )

    tile_cols = 512

    def ffn_in(l, blocks):
        n = hidden // tile_cols
        col = pl.BlockSpec((1, tile_cols), lambda j: (0, j))
        wide = pl.BlockSpec((size, tile_cols), lambda j: (0, j))
        return kernel_call(
            order, functools.partial(ffn_in_body, l, lats, len(blocks), width=width, chunk=size // 3), "ffn_in_%d" % l,
            (sds((size, total), BF), sds((2, size, LANE), F32), sds((size, hidden), BF),
             sds((size, hidden), BF), sds((1, hidden), F32), sds((8, LANE), F32)),
            (info, *blocks, mixer_expand_weight, line(ffn_in_bias)),
            [SM] + [ANY] * len(blocks) + [pl.BlockSpec((total, tile_cols), lambda j: (0, j)), col],
            (VM, VM, wide, wide, col, VM), grid=(n,),
            scratch=[pltpu.VMEM((size + EXTRA, total), BF), pltpu.SemaphoreType.DMA((5,))], hbm=(0, 1, 3),
        )

    def ffn_out(l, act, spat, tots, after=()):
        n = total // tile_cols
        return kernel_call(
            order, functools.partial(ffn_out_body, lats, hidden_total, width=width, chunk=32), "ffn_out_%d" % l,
            (sds((size, hidden), BF),) + scatter_shapes(size, width),
            (info, act, spat, *tots, line(grn_gamma), line(grn_beta), mixer_contract_weight),
            [SM] + [VM] * 8 + [pl.BlockSpec((hidden, tile_cols), lambda j: (0, j))],
            (VM,) + (ANY,) * 4, grid=(n,),
            scratch=[pltpu.VMEM((size, total), BF), pltpu.SemaphoreType.DMA((5,))], hbm=(0, 4), after=after,
        )

    def swap_halves(outs):
        return tuple(cswap(o) for o in outs)

    def scatter_end(name, keep, gots, stats, after=()):
        got, got_a, got_b = gots
        half = kernel_call(
            order, functools.partial(add_body, stats), name, (sds(keep.shape[1:], BF),), (keep, got_a, got_b),
            [part_spec(1, keep.shape), VM, VM], (VM,), after=after,
        )[0]
        return keep, got, xswap(half)

    scale_rows = (jnp.dot(noise_embed, scale_weight, precision=highest) + scale_bias)[:, None]
    shift_rows = (jnp.dot(noise_embed, shift_weight, precision=highest) + shift_bias)[:, None]

    def middle(l, pieces, after=()):
        keep, got, far = pieces
        spec = part_spec(0, keep.shape)
        row = lat_spec(l, 1, width)
        return kernel_call(
            order, middle_body, "middle_%d" % l,
            (sds((size, width), F32), sds((size + EXTRA, width), BF)),
            (latents, keep, got, far, line(ffn_out_bias), scale_rows, shift_rows),
            [lat_spec(l, size, width), spec, VM, VM, VM, row, row], (VM, VM), hbm=(0,), after=after,
        )

    def text_low_rows(blocks, after):
        return kernel_call(
            order, functools.partial(text_body, lats, width=width, text_len=text_len), "text_rows",
            (sds((lats, text_rows, total), BF), sds((lats, text_rows, width), BF)),
            (info, *blocks, text_weight, line(text_bias)),
            [SM] + [ANY] * 4 + [VM, VM], (VM, VM), scratch=[pltpu.SemaphoreType.DMA((4 * lats,))], hbm=(0,), after=after,
        )

    def attention(l, blocks, texts, grads):
        return kernel_call(
            order,
            functools.partial(attention_body, l, lats, (len(blocks), len(texts), len(grads)), width=width),
            "attention_%d" % l,
            (sds((rows, total), BF), sds((2, size, LANE), F32), sds((size, total), BF),
             sds((size, width), BF), sds((rows, 3 * width), BF))
            + scatter_shapes(rows + EXTRA, width) + (sds((8, width), F32),),
            (info, *blocks, *texts, *grads, query_weight, key_weight, value_weight, attn_out,
             line(query_bias), line(value_bias)),
            [SM] + [ANY] * (len(blocks) + len(texts) + len(grads) + 4) + [VM, VM],
            (ANY,) * 9 + (VM,),
            scratch=[
                pltpu.VMEM((size + EXTRA, total), BF),
                pltpu.VMEM((total, 3 * width), BF),
                pltpu.VMEM((width, total), BF),
                pltpu.VMEM((size, width), BF),
                pltpu.VMEM((rows, width), BF),
                pltpu.VMEM((rows, width), BF),
                pltpu.VMEM((size, width), BF),
                pltpu.VMEM((width, rows), BF),
                pltpu.VMEM((width, rows), BF),
                pltpu.VMEM((width, size), F32),
                pltpu.VMEM((width, size), F32),
                pltpu.VMEM((2, rows, size), F32),
                pltpu.VMEM((rows + EXTRA, total), BF),
                pltpu.VMEM((rows, total), BF),
                pltpu.VMEM((2, size, LANE), F32),
                pltpu.VMEM((size, total), BF),
                pltpu.VMEM((size, width), BF),
                pltpu.VMEM((rows, 3 * width), BF),
                pltpu.SemaphoreType.DMA((24,)),
            ],
            hbm=(0, 1, 2, 3, 4, 8, 9), limit=36,
        )

    def project(atts):
        h = half_rows(size)
        return kernel_call(
            order, functools.partial(project_body, lats), "project",
            tuple(sds((lats, r, width), BF) for r in (size, h, size - h)) + (sds((2, lats, size, width), BF),),
            (info, *atts, attn_out), [SM] + [VM] * (lats + 1), (ANY,) * 4,
            scratch=[pltpu.VMEM((lats, size, total), BF), pltpu.SemaphoreType.DMA((lats, 5))], hbm=(3,),
        )

    def project_end(keep, gots):
        got, got_a, got_b = gots
        half = kernel_call(
            order, add_out_body, "add_out", (sds(keep.shape[1:], BF),), (keep, got_a, got_b),
            [pl.BlockSpec((None,) + keep.shape[1:], lambda *_: (1, 0, 0, 0)), VM, VM], (VM,), after=(got,),
        )[0]
        return keep, got, xswap(half)

    def result_rows(firsts, pieces):
        keep, got, far = pieces
        return kernel_call(
            order, functools.partial(result_body, lats), "result", (sds((lats, size, width), BF),),
            (*firsts, scale_rows, shift_rows, keep, got, far, line(attn_out_bias)),
            [VM] * (lats + 2) + [pl.BlockSpec((None,) + keep.shape[1:], lambda *_: (0, 0, 0, 0)), VM, VM, VM], (VM,),
        )[0]

    def second_grad(l, pieces, first, stat):
        keep, got, far = pieces
        spec = part_spec(0, keep.shape)
        row = lat_spec(l, 1, width)
        return kernel_call(
            order, functools.partial(second_grad_body, total_width=total, text_len=text_len), "second_grad_%d" % l,
            (sds((size, width), BF), sds((size, width), F32), sds((text_rows, width), BF), sds((8, width), F32)),
            (keep, got, far, upstream, first, stat, scale_rows, shift_rows),
            [spec, VM, VM, lat_spec(l, size, width), VM, VM, row, row], (VM, VM, VM, VM), hbm=(1, 3),
        )

    def gated_grad(l, blocks, act, spat, before=()):
        n = hidden // tile_cols
        col = pl.BlockSpec((1, tile_cols), lambda j: (0, j))
        wide = pl.BlockSpec((size, tile_cols), lambda j: (0, j))
        joined = len(before)
        return kernel_call(
            order,
            functools.partial(gated_grad_body, lats, len(blocks), joined, width=width, chunk=size // 3),
            "gated_grad_%d" % l,
            (sds((size, total), BF), sds((size, hidden), BF), sds((1, hidden), F32), sds((1, hidden), F32),
             sds((2, 8, LANE) if joined else (8, LANE), F32)),
            (info, *blocks, mixer_contract_weight, act, line(grn_gamma), spat, *before),
            [SM] + [ANY] * len(blocks)
            + [pl.BlockSpec((tile_cols, total), lambda j: (j, 0)), wide, col, col] + [VM] * joined,
            (VM, wide, col, col, VM), grid=(n,), scratch=[pltpu.SemaphoreType.DMA((6,))], hbm=(0, 3),
        )

    def hidden_grad(l, gg, act, slope, spat, s1, tots, crosses, nrm):
        n = total // tile_cols
        return kernel_call(
            order, functools.partial(hidden_grad_body, l, lats, hidden_total, width=width, chunk=32),
            "hidden_grad_%d" % l,
            (sds((size, hidden), BF),) + scatter_shapes(size + EXTRA, width)
            + (sds((1, hidden), F32), sds((1, hidden), F32)),
            (info, gg, act, slope, spat, s1, line(grn_gamma), *tots, *crosses, mixer_expand_weight, nrm),
            [SM] + [VM] * 10 + [lat_spec(l, 8, LANE)] * 4
            + [pl.BlockSpec((tile_cols, hidden), lambda j: (j, 0)), pl.BlockSpec((size, tile_cols), lambda j: (0, j))],
            (VM, ANY, ANY, ANY, ANY, VM, VM), grid=(n,),
            scratch=[
                pltpu.VMEM((size + EXTRA, total), BF),
                pltpu.VMEM((2, size, LANE), F32),
                pltpu.SemaphoreType.DMA((5,)),
            ],
            hbm=(0, 4, 5, 6),
        )

    def conv_backward(l, pieces, conv, stat, first_grad):
        keep, got, far = pieces
        spec = part_spec(0, keep.shape)
        return kernel_call(
            order, functools.partial(conv_backward_body, l, total_width=total), "conv_backward_%d" % l,
            (sds((size, width), BF), sds((16, width), F32)),
            (info, keep, got, far, conv, stat, latents, first_grad, conv_kernel),
            [SM, spec, VM, VM, VM, VM, lat_spec(l, size, width), VM, VM], (VM, VM),
            scratch=[pltpu.VMEM((size + 2 * MARGIN, width), F32)], hbm=(1,),
        )

    half = dp // 2
    split = dp == 8
    if split:
        here = lax.axis_index("dp")
        places = jnp.stack([here // 2, here % 2]).astype(jnp.int32)
    else:
        places = None

    def swap_dp(v, bit):
        return lax.ppermute(v, "dp", [(i, i ^ bit) for i in range(dp)])

    def reduce_start(parts):
        if len(parts) == 1:
            return [lax.psum_scatter(parts[0], "dp", scatter_dimension=0, tiled=True)]
        send, keep = parts
        return [keep, swap_dp(send, 1)]

    def reduce_step(name, state, bit, small=None, after=()):
        if not split:
            return state if small is None else (state, small)
        keep, got = state
        shape = keep.shape[1:] if bit == 4 else (keep.shape[0] // 2,) + keep.shape[1:]
        outs = (sds(shape, BF),) * 2
        args = (keep, got)
        if small is not None:
            args += tuple(small)
            outs += (sds((2 * small[0].shape[0] - SUMMED, width), F32),)
        res = kernel_call(
            order, functools.partial(combine_body, small is not None), name, outs, args, [VM] * len(args),
            (VM,) * len(outs), hbm=(1,), after=after,
        )
        state = [res[1], swap_dp(res[0], bit)]
        if small is not None:
            return state, (res[2], swap_dp(res[2], bit))
        return state

    def reduce_end(name, states, layout, shapes, small=None):
        if not split:
            outs = [jnp.zeros(s, F32) for s in shapes]
            for (part,), plan in zip(states, layout):
                for start, cols, out, offset, flip in plan:
                    block = part[:, start : start + cols].astype(F32)
                    if flip:
                        outs[out] = outs[out].at[offset : offset + cols].set(block.T)
                    else:
                        outs[out] = outs[out].at[:, offset : offset + cols].set(block)
            if small is not None:
                rows = small[0]
                outs.append(lax.psum(rows[:SUMMED], "dp"))
                noise = rows[SUMMED + 4 : SUMMED + 6, : noise_embed.shape[1]].T
                for k in range(2):
                    values = rows[SUMMED + 2 * k : SUMMED + 2 * k + 2]
                    outs.append(lax.psum(jnp.dot(noise, values, precision=highest), "dp"))
            return outs
        args, specs = [], []
        for state in states:
            args += state
            specs += [VM] * len(state)
        outs = tuple(sds(s, F32) for s in shapes)
        if small is not None:
            args += small
            specs += [VM] * len(small)
            outs += (sds((2 * small[0].shape[0] - SUMMED, width), F32),)
            outs += (sds((noise_embed.shape[1], width), F32),) * 2
        return kernel_call(
            order,
            functools.partial(
                finish_body, [len(state) for state in states], len(small) if small is not None else 0, layout
            ),
            name, outs, tuple(args), specs, (VM,) * len(outs),
        )

    def weights(name, sets, cut=True, after=()):
        return weight_grads(order, name, places if cut else None, sets, dp, after)

    assert lats == 2
    share = total // dp
    text_blocks = gather_small(text_act)
    conv0 = conv_forward(0, text_blocks[1:])
    pay10 = gather_start(conv0[0])
    conv1 = conv_forward(1)
    pay11 = gather_start(conv1[0])
    conv = (conv0, conv1)
    text_full, text_low = text_low_rows(text_blocks, ())
    text_low_blocks = gather_small(text_low)
    (far,) = hop(order, "hop_rows_0", pay10[2])
    pay10 = gather_end(pay10, far)
    ffn0 = ffn_in(0, pay10)
    tot0 = gather_small(ffn0[5])
    far, up0 = hop(order, "hop_rows_1", pay11[2], (upstream, 0), after=text_low_blocks[1:])
    pay11 = gather_end(pay11, far)
    up0 = gather_start(up0)
    ffn1 = ffn_in(1, pay11)
    tot1 = gather_small(ffn1[5])
    ffn, tots = (ffn0, ffn1), (tot0, tot1)
    out0 = ffn_out(0, ffn0[2], ffn0[4], tot0, up0[1:])
    gots0 = swap_halves(out0[1:4])
    part0 = scatter_end("add_ffn_0", out0[4], gots0, False, tot1[1:])
    out1 = ffn_out(1, ffn1[2], ffn1[4], tot1)
    gots1 = swap_halves(out1[1:4])
    (up_far,) = hop(order, "hop_upstream", up0[2])
    up0 = gather_end(up0, up_far)
    part1 = scatter_end("add_ffn_1", out1[4], gots1, False)
    gated = (out0[0], out1[0])
    mid0 = middle(0, part0)
    pay20 = gather_start(mid0[1])
    mid1 = middle(1, part1, up0[3:])
    pay21 = gather_start(mid1[1])
    far, up1 = hop(order, "hop_context_0", pay20[2], (upstream, 1))
    pay20 = gather_end(pay20, far)
    up1 = gather_start(up1)
    attn0 = attention(0, pay20, text_low_blocks, up0)
    gots0 = swap_halves(attn0[5:8])
    far, up_far = hop(order, "hop_context_1", pay21[2], up1[2])
    pay21 = gather_end(pay21, far)
    up1 = gather_end(up1, up_far)
    ctx0 = scatter_end("add_ctx_0", attn0[8], gots0, True)
    attn1 = attention(1, pay21, text_low_blocks, up1)
    gots1 = swap_halves(attn1[5:8])
    attn = (attn0, attn1)
    proj = project([attn0[3], attn1[3]])
    outs = swap_halves(proj[:3])
    second0 = second_grad(0, ctx0, mid0[0], attn0[1])
    far30 = xswap(second0[0])
    ctx1 = scatter_end("add_ctx_1", attn1[8], gots1, True)
    out_parts = project_end(proj[3], outs)
    sets = [
        ([(attn[l][0], attn[l][4]) for l in (0, 1)], 0, 3 * width),
        ([(attn[l][2], attn[l][3]) for l in (0, 1)], 0, width),
    ]
    parts_a = weights("attn_weight_grads", sets)
    second1 = second_grad(1, ctx1, mid1[0], attn1[1])
    far31 = xswap(second1[0])
    pay30 = gather_late("hop_first_0", second0[0], far30)
    if split:
        parts_a = (gate(order, "gate_attn", parts_a[0]), parts_a[1])
    sum_a = reduce_start(parts_a)
    gg0 = gated_grad(0, pay30, ffn0[2], ffn0[4])
    pay31 = gather_late("hop_first_1", second1[0], far31)
    gg1 = gated_grad(1, pay31, ffn1[2], ffn1[4], gg0[4:])
    cross = gather_small(gg1[4])
    gg = (gg0, gg1)

    def hidden_of(l, cross):
        return hidden_grad(l, gg[l][1], ffn[l][2], ffn[l][3], ffn[l][4], gg[l][2], tots[l], cross, ffn[l][0])

    near = hidden // 2
    pairs = [(gg[l][0], gated[l]) for l in (0, 1)]
    sum_c0 = reduce_start(weights("contract_weight_grads_0", [(pairs, 0, near)], after=out_parts[2:]))
    hid0 = hidden_of(0, cross)
    gots0 = swap_halves(hid0[1:4])
    sum_a = reduce_step("attn_sums", sum_a, 2)
    in0 = scatter_end("add_in_0", hid0[4], gots0, True)
    texts = [(text_full[0], second0[2]), (text_full[1], second1[2])]
    sum_c1 = reduce_start(weights("contract_weight_grads_1", [(pairs, near, hidden - near), (texts, 0, width)]))
    hid1 = hidden_of(1, cross)
    gots1 = swap_halves(hid1[1:4])
    hid = (hid0, hid1)
    sum_a = reduce_step("attn_sums_b", sum_a, 4)
    pairs = [(ffn[l][0], hid[l][0]) for l in (0, 1)]
    sum_e0 = reduce_start(weights("expand_weight_grads_0", [(pairs, 0, near)]))
    in1 = scatter_end("add_in_1", hid1[4], gots1, True)
    back0 = conv_backward(0, in0, conv[0][1], ffn0[1], second0[1])
    sum_c0 = reduce_step("contract_sums_0", sum_c0, 2)
    sum_e1 = reduce_start(weights("expand_weight_grads_1", [(pairs, near, hidden - near)], after=(*sum_a[1:], *in1[2:])))
    sum_c0 = reduce_step("contract_sums_0b", sum_c0, 4)
    sum_c1 = reduce_step("contract_sums_1", sum_c1, 2)
    back1 = conv_backward(1, in1, conv[1][1], ffn1[1], second1[1])
    packed = kernel_call(
        order, functools.partial(pack_body, lats), "pack", (sds((SUMMED + 8, width), F32),),
        (noise_embed, second0[3], second1[3], attn0[9], attn1[9], hid0[6], hid1[6], gg0[3], gg1[3],
         back0[1], back1[1], hid0[5], hid1[5]),
        [VM] * (1 + 6 * lats), (VM,),
    )[0]
    packed = (packed, swap_dp(packed, 1)) if split else (packed,)
    sum_e0 = reduce_step("expand_sums_0", sum_e0, 2)
    sum_c1 = reduce_step("contract_sums_1b", sum_c1, 4, after=sum_c0[1:])
    grads_a = reduce_end(
        "attn_grads", [sum_a],
        [[(k * width, width, k, 0, False) for k in range(3)] + [(3 * width, width, 3, 0, True)]],
        [(share, width)] * 3 + [(width, share)],
    )
    sum_e1, packed = reduce_step("expand_sums_1", sum_e1, 2, packed)
    sum_e0 = reduce_step("expand_sums_0b", sum_e0, 4)
    result = result_rows([mid0[0], mid1[0]], out_parts)
    sum_e1, packed = reduce_step("expand_sums_1b", sum_e1, 4, packed, after=sum_c1[1:])
    rest = hidden - near
    grads_c = reduce_end(
        "contract_grads", [sum_c0, sum_c1],
        [[(0, near, 0, 0, True)], [(0, rest, 0, near, True), (rest, width, 1, 0, False)]],
        [(hidden, share), (share, width)],
    )
    grads_e = reduce_end(
        "expand_grads", [sum_e0, sum_e1],
        [[(0, near, 0, 0, False)], [(0, rest, 0, near, False)]], [(share, hidden)], packed,
    )
    sums = grads_e[1]
    n = hidden // width
    return (
        result,
        jnp.stack([back0[0], back1[0]]),
        sums[:9],
        sums[9],
        grads_e[0],
        sums[20 : 20 + n].reshape(-1),
        sums[12 : 12 + n].reshape(-1),
        sums[16 : 16 + n].reshape(-1),
        grads_c[0],
        sums[26],
        grads_e[2],
        sums[24],
        grads_e[3],
        sums[25],
        grads_c[1],
        sums[27],
        grads_a[0],
        sums[29],
        grads_a[1],
        grads_a[2],
        sums[30],
        grads_a[3],
        sums[28],
    )


def solution(mesh):
    rows = P("dp", None, "chan")
    weight_in = P(None, "chan")
    vec = P("chan")
    in_specs = (
        rows, P("dp", None), P("dp"), P("dp"), rows, P("dp", None), weight_in, vec, weight_in, vec, vec, vec,
        P("chan", None), vec, weight_in, vec, weight_in, vec, weight_in, vec, weight_in, vec, weight_in,
        weight_in, vec, P("chan", None), vec, rows,
    )
    out_specs = (
        rows, rows, weight_in, vec, P("dp", "chan"), vec, vec, vec, P("chan", "dp"), vec, weight_in, vec,
        weight_in, vec, P("dp", "chan"), vec, P("dp", "chan"), vec, P("dp", "chan"), P("dp", "chan"), vec,
        P("chan", "dp"), vec,
    )
    return jax.shard_map(local, mesh=mesh, in_specs=in_specs, out_specs=out_specs, check_vma=False)
```
